32 devices in a mesh: pipe: 2 (over core), dp: 16 (over z, y, x).
Axes of the slice: x: 2, y: 2, z: 4, core: 2. Of those that a mesh axis runs over, the one named last changes fastest.
Arguments:
- frames: bfloat16 [32, 8, 49, 2048], P('dp'), may hold values from -6 to 6
- out_grad: bfloat16 [32, 8, 49, 2048], P('dp'), may hold values from -6 to 6
- seg_counts: int32 [32], P('dp'), may hold values from 1 to 8, as said below
- reducer: bfloat16 [2, 2048, 512], P('pipe'), may hold values from -0.125 to 0.125
- spatial: bfloat16 [2, 512, 9, 512], P('pipe'), may hold values from -0.09375 to 0.09375
- expander: bfloat16 [2, 512, 2048], P('pipe'), may hold values from -0.25 to 0.25
- squeezer: bfloat16 [2, 512, 128], P('pipe'), may hold values from -0.25 to 0.25
- motion: bfloat16 [2, 128, 9, 128], P('pipe'), may hold values from -0.1875 to 0.1875
- context: bfloat16 [2, 128, 128], P('pipe'), may hold values from -0.5 to 0.5
- gating: bfloat16 [2, 128, 512], P('pipe'), may hold values from -0.5 to 0.5
- gating_bias: float32 [2, 512], P('pipe'), may hold values from -3 to 3
- norm_params: float32 [2, 2, 3072], P('pipe'), may hold values from -1.5 to 1.5, as said below
Outputs:
- section_out: bfloat16 [2, 32, 8, 49, 2048], P('pipe', 'dp')
- input_grad: bfloat16 [2, 32, 8, 49, 2048], P('pipe', 'dp')
- grad_flat: float32 [2, 4751872], P('pipe', 'dp')
- grad_norms: float32 [2, 2, 3072], P('pipe')
The draws below stay inside these ranges and needn't reach their ends.
Inputs may be any that keep to these rules, and one draw needn't show every extreme that they name: The first seg_counts[c] segments of clip c are valid and the rest are not; some clip has all 8. `norm_params`: row 0 holds gains, row 1 offsets.
All inputs are finite; a program needn't handle non-finite values.
Results may differ from the reference program's by a relative error of at most 0.02.
Values may be sent and summed in bfloat16 or wider, within the bound.
A program may use at most 256 MiB of HBM per device.

```python
import jax
import jax.numpy as jnp
from jax import lax

CH = 2048
MID = 512
RED = 128
SIDE = 7
PIX = 49
SEGS = 8
MICRO = 2
CLIPS_MB = 1
CLIPS = 32
GRAD_LEN = 4751872
N_DP = 16


def draw_seg_counts(key, part):
    key = jax.random.fold_in(key, 3)
    first, second = jax.random.split(key)
    counts = jax.random.randint(first, (CLIPS,), 1, SEGS + 1)
    place = jax.random.randint(second, (), 0, CLIPS)
    return counts.at[place].set(SEGS).astype(jnp.int32)


def draw_norm_params(key, part):
    key = jax.random.fold_in(key, 5)
    first, second = jax.random.split(key)
    width = 2 * MID + CH
    gains = jnp.clip(1.0 + 0.15 * jax.random.normal(first, (2, 1, width), jnp.float32), 0.5, 1.5)
    offsets = jnp.clip(0.5 * jax.random.normal(second, (2, 1, width), jnp.float32), -1.5, 1.5)
    return jnp.concatenate([gains, offsets], axis=1)


def steps_of(stream_key, dims, pieces, low, largest):
    def one(dim, blocks):
        draws = jax.random.uniform(jax.random.fold_in(jax.random.fold_in(stream_key, 6), dim), (blocks,), jnp.float32, low / len(pieces), largest / len(pieces))
        return jnp.repeat(jnp.exp(draws), dims[dim] // blocks).reshape((-1,) + (1,) * (len(dims) - dim - 1))

    loudness = one(*pieces[0])
    for cut in pieces[1:]:
        loudness = loudness * one(*cut)
    return loudness


def noise(own_key, dims, spread, most, cuts=(), kind=jnp.bfloat16):
    drawn = spread * jax.random.normal(own_key, dims, jnp.float32)
    if cuts:
        drawn = drawn * steps_of(own_key, dims, cuts, -0.22, 0.18)
    return jnp.clip(drawn, -most, most).astype(kind)


def setup_inputs(seed: int = 0) -> dict:
    seeds = jax.random.split(jax.random.key(seed), 13)
    return {
        "frames": noise(seeds[0], (CLIPS, SEGS, PIX, CH), 1.0, 6.0, ((0, 16),)),
        "out_grad": noise(seeds[1], (CLIPS, SEGS, PIX, CH), 1.0, 6.0, ((0, 16),)),
        "seg_counts": draw_seg_counts(jax.random.fold_in(seeds[12], 71), 0),
        "reducer": noise(seeds[3], (2, CH, MID), CH ** -0.5, 0.125, ((0, 2),)),
        "spatial": noise(seeds[4], (2, MID, 9, MID), (9 * MID) ** -0.5, 0.09375, ((0, 2),)),
        "expander": noise(seeds[5], (2, MID, CH), MID ** -0.5, 0.25, ((0, 2),)),
        "squeezer": noise(seeds[6], (2, MID, RED), MID ** -0.5, 0.25, ((0, 2),)),
        "motion": noise(seeds[7], (2, RED, 9, RED), (9 * RED) ** -0.5, 0.1875, ((0, 2),)),
        "context": noise(seeds[8], (2, RED, RED), RED ** -0.5, 0.5, ((0, 2),)),
        "gating": noise(seeds[9], (2, RED, MID), RED ** -0.5, 0.5, ((0, 2),)),
        "gating_bias": noise(seeds[10], (2, MID), 0.5, 3.0, ((0, 2),), jnp.float32),
        "norm_params": draw_norm_params(jax.random.fold_in(seeds[12], 71), 0),
    }


EPSILON = 1e-05
HIGH = lax.Precision.HIGHEST

@jax.custom_vjp
def low(v):
    return lax.optimization_barrier(v.astype(jnp.bfloat16)).astype(jnp.float32)

@jax.custom_vjp
def low_back(v):
    return v

def low_keep(v):
    return (low(v), None)

def low_pass(kept, grad):
    return (grad,)

def back_keep(v):
    return (v, None)

def back_low(kept, grad):
    return (low(grad),)
low.defvjp(low_keep, low_pass)
low_back.defvjp(back_keep, back_low)

def project(values, weight):
    return jnp.einsum('...c,co->...o', values, weight, precision=HIGH)

def conv_three(values, kernel):
    leading = values.shape[:2]
    maps = values.reshape((-1, SIDE, SIDE, values.shape[-1]))
    padded = jnp.pad(maps, ((0, 0), (1, 1), (1, 1), (0, 0)))
    patches = jnp.stack([padded[:, down:down + SIDE, right:right + SIDE, :] for down in range(3) for right in range(3)], axis=3)
    result = jnp.einsum('nhwkc,cko->nhwo', patches, kernel, precision=HIGH)
    return result.reshape(leading + (SIDE * SIDE, kernel.shape[-1]))

def batch_norm(values, mask_pix, count, gain, offset):
    mean_value = lax.optimization_barrier(jnp.sum(values * mask_pix, axis=(0, 1, 2))) / count
    centred = values - mean_value
    variance = lax.optimization_barrier(jnp.sum(mask_pix * centred * centred, axis=(0, 1, 2))) / count
    return centred * lax.rsqrt(variance + EPSILON) * gain + offset

def section_block(inputs, params, valid, pairs):
    reducer, spatial, expander, squeezer, motion, context, gating, gating_bias, norm_params = params
    gains = norm_params[0]
    offsets = norm_params[1]
    mask_pix = valid[:, :, None, None]
    count = PIX * jnp.sum(valid)
    inputs = low_back(inputs)
    reduced = low_back(project(inputs, reducer))
    first_act = low(jax.nn.silu(batch_norm(reduced, mask_pix, count, gains[:MID], offsets[:MID])))
    spatial_out = low_back(conv_three(first_act, spatial))
    middle = low(jax.nn.silu(batch_norm(spatial_out, mask_pix, count, gains[MID:2 * MID], offsets[MID:2 * MID])))
    squeezed = low_back(project(middle, squeezer))
    later = jnp.concatenate([squeezed[:, 1:], jnp.zeros_like(squeezed[:, :1])], axis=1)
    motion_field = low(pairs[:, :, None, None] * (later - squeezed))
    context_mean = lax.optimization_barrier(jnp.mean(motion_field, axis=2, keepdims=True))
    scores = low(low_back(conv_three(motion_field, motion) + project(context_mean, context)))
    logits = low_back(project(scores, gating) + gating_bias)
    gated = low(middle * (0.5 + jax.nn.sigmoid(logits)))
    expanded = low_back(project(gated, expander))
    normed = batch_norm(expanded, mask_pix, count, gains[2 * MID:], offsets[2 * MID:])
    return low(mask_pix * jax.nn.silu(inputs + normed))

def section_all(values, params, valid, pairs):
    outputs = []
    for micro in range(MICRO):

        def pick(array):
            shaped = array.reshape((N_DP, MICRO, CLIPS_MB) + array.shape[1:])
            return shaped[:, micro].reshape((N_DP * CLIPS_MB,) + array.shape[1:])
        result = section_block(pick(values), params, pick(valid), pick(pairs))
        outputs.append(result.reshape((N_DP, CLIPS_MB) + result.shape[1:]))
    stacked = jnp.stack(outputs, axis=1)
    return stacked.reshape(values.shape)

def reference(frames, out_grad, seg_counts, reducer, spatial, expander, squeezer, motion, context, gating, gating_bias, norm_params):
    segment = jnp.arange(SEGS, dtype=jnp.int32)
    valid = (segment[None, :] < seg_counts[:, None]).astype(jnp.float32)
    pairs = (segment[None, :] + 1 < seg_counts[:, None]).astype(jnp.float32)
    everything = (reducer, spatial, expander, squeezer, motion, context, gating, gating_bias, norm_params)

    def params_of(section):
        return tuple((item[section].astype(jnp.float32) for item in everything))

    def run(values, params):
        return section_all(values, params, valid, pairs)
    first_out, first_back = jax.vjp(run, frames.astype(jnp.float32), params_of(0))
    second_out, second_back = jax.vjp(run, first_out, params_of(1))
    second_in, second_grads = second_back(out_grad.astype(jnp.float32))
    first_in, first_grads = first_back(second_in)
    merged = [jnp.stack([first_grads[which], second_grads[which]]) for which in range(9)]
    flat = jnp.concatenate([merged[which].reshape(2, -1) for which in range(8)], axis=1)
    grad_flat = jnp.pad(flat, ((0, 0), (0, GRAD_LEN - flat.shape[1])))
    section_out = jnp.stack([first_out, second_out]).astype(jnp.bfloat16)
    input_grad = jnp.stack([first_in, second_in]).astype(jnp.bfloat16)
    return (section_out, input_grad, grad_flat, merged[8])
```

```python
import functools
from types import SimpleNamespace

import jax
import jax.numpy as jnp
from jax import lax
from jax.experimental import pallas as pl
from jax.experimental.pallas import tpu as pltpu
from jax.sharding import PartitionSpec as P

SIDE = 7
PIX = 49
MICRO = 2
PIECES = 16
EPSILON = 1e-05
HIGH = lax.Precision.HIGHEST
BF = jnp.bfloat16
F32 = jnp.float32
MESH = pl.DeviceIdType.MESH
LANES = 128
HALF = 256
ROW = 512
GRID = SIDE + 2
WEIGHTS = ("red", "spa", "exp", "squ", "mot", "con", "gat")
SMALL = ("squ", "mot", "con", "gat")
CHUNKS = ("a", "b", "c")
COMPS = ("red", "spa", "exp", "small")
HOLDS = dict(a=("exp", "small"), b=("spa",), c=("red",))


def sigmoid(values):
    return 0.5 * jnp.tanh(0.5 * values) + 0.5


def silu_slope(values):
    sigma = sigmoid(values)
    return sigma * (1.0 + values * (1.0 - sigma))


def dot(a, b):
    return jnp.dot(a, b, preferred_element_type=F32)


def dot_nt(a, b):
    return lax.dot_general(a, b, (((1,), (1,)), ((), ())), preferred_element_type=F32)


def dot_tn(a, b):
    return lax.dot_general(a, b, (((0,), (0,)), ((), ())), preferred_element_type=F32)


def up(value, step):
    return -(-value // step) * step


def plan(n, ch, mid, red, segs, share):
    side = 4 if n % 64 == 0 else 2 if n % 4 == 0 else 1
    depth = n // (side * side)
    slots = PIECES // (side * side)
    levels = [(n, 1)] if n <= 16 else [(side * side, 1), (depth, side * side)]
    rows = dict(red=ch * mid // ROW, spa=9 * mid * mid // ROW, exp=mid * ch // ROW)
    small = mid * red + 9 * red * red + red * red + red * mid + mid
    small_rows = up(small, ROW) // ROW
    parts = dict(
        red=(0, rows["red"] // PIECES),
        spa=(rows["red"], rows["spa"] // PIECES),
        exp=(rows["red"] + rows["spa"], rows["exp"] // PIECES),
        small=(rows["red"] + rows["spa"] + rows["exp"], up(up(small_rows, PIECES) // PIECES, 16)),
    )
    total = (parts["small"][0] + small_rows) * ROW
    margin = max(size for _, size in parts.values())
    reach = 1
    for start, size in parts.values():
        for piece in range(PIECES):
            first = (start + size * piece) * ROW
            if first < total:
                last = min((start + size * (piece + 1)) * ROW, total) - 1
                reach = max(reach, last // share - first // share + 1)
    land = margin + up(share // ROW + 18, 16) + margin
    return SimpleNamespace(
        side=side,
        depth=depth,
        slots=slots,
        levels=levels,
        parts=parts,
        total=total,
        margin=margin,
        reach=reach,
        land=land,
        small_rows=small_rows,
    )


def kernel(n, sizes, names, *refs):
    r = SimpleNamespace(**dict(zip(names, refs)))
    own_w = dict(
        red=r.in_red, spa=r.in_spa, exp=r.in_exp, squ=r.in_squ, mot=r.in_mot, con=r.in_con, gat=r.in_gat
    )
    sib_w = dict(
        red=r.sib_red, spa=r.sib_spa, exp=r.sib_exp, squ=r.sib_squ, mot=r.sib_mot, con=r.sib_con, gat=r.sib_gat
    )
    held_w = dict(red=r.red, spa=r.spa, exp=r.exp, squ=r.squ, mot=r.mot, con=r.con, gat=r.gat)
    chunk_refs = dict(
        a=SimpleNamespace(g=r.g_a, r0=r.r0_a, r1=r.r1_a, r2=r.r2_a, r3=r.r3_a),
        b=SimpleNamespace(g=r.g_b, r0=r.r0_b, r1=r.r1_b, r2=r.r2_b, r3=r.r3_b),
        c=SimpleNamespace(g=r.g_c, r0=r.r0_c, r1=r.r1_c, r2=r.r2_c, r3=r.r3_c),
    )
    fin = dict(red=r.fin_red, spa=r.fin_spa, exp=r.fin_exp, small=r.fin_small)
    ch, mid, red_w, segs, share = sizes
    pp = plan(n, ch, mid, red_w, segs, share)
    side, depth, slots, levels, parts = pp.side, pp.depth, pp.slots, pp.levels, pp.parts
    rows = PIX * segs
    full = up(rows, 16)
    pad = full - rows
    c = lax.axis_index("pipe")
    i = lax.axis_index("dp")
    x = lax.rem(i, side)
    y = lax.rem(lax.div(i, side), side)
    z = lax.div(i, side * side)
    fc = x * (1 - c) + y * c
    gc = y * (1 - c) + x * c
    other = (1 - c, i)

    def remote(src, dst, send, recv, device):
        return pltpu.make_async_remote_copy(
            src_ref=src,
            dst_ref=dst,
            send_sem=send,
            recv_sem=recv,
            device_id=device,
            device_id_type=MESH,
        )

    barrier = pltpu.get_barrier_semaphore()

    def greet(k, _):
        peer = lax.rem(i + k, n)
        pl.semaphore_signal(barrier, inc=1, device_id=(c, peer), device_id_type=MESH)
        pl.semaphore_signal(barrier, inc=1, device_id=(1 - c, peer), device_id_type=MESH)
        return 0

    pl.semaphore_signal(barrier, inc=1, device_id=other, device_id_type=MESH)
    lax.fori_loop(1, n, greet, 0)

    count_own = r.counts[c]
    segment = lax.broadcasted_iota(jnp.int32, (segs, LANES), 0)
    valid = jnp.where(segment < count_own, 1.0, 0.0).astype(F32)
    paired = jnp.where(segment + 1 < count_own, 1.0, 0.0).astype(F32)
    pixels_own = PIX * count_own.astype(F32)

    stage = r.stage
    v = r.v
    free = r.nh3.at[1]

    def tile(j):
        return pl.ds(pl.multiple_of(j * LANES, LANES), LANES)

    def view(j, base=0):
        return (
            pl.ds(pl.multiple_of(base + lax.div(j, 4) * full, 16), rows),
            tile(lax.rem(j, 4)),
        )

    def loop(count, body):
        def step(j, _):
            body(j)
            return 0

        lax.fori_loop(0, count, step, 0)

    def packed(values):
        flat = values.reshape(rows, values.shape[-1])
        return jnp.concatenate([flat, jnp.zeros((pad, flat.shape[-1]), F32)], axis=0).astype(BF)

    def cube(values):
        return values.reshape(PIX, segs, values.shape[-1])

    def fold(values):
        return jnp.sum(jnp.sum(values, axis=0), axis=0, keepdims=True)

    load_frames = pltpu.make_async_copy(r.frames.at[c], stage.at[0], r.load_sem.at[0])
    load_frames.start()

    def load_weight(name, s, first):
        @pl.when(c == s)
        def _():
            pltpu.make_async_copy(own_w[name], held_w[name], r.w_sem.at[WEIGHTS.index(name)]).start()

        @pl.when(c != s)
        def _():
            if first:
                k = WEIGHTS.index(name)
                remote(
                    own_w[name], sib_w[name], r.ws_sem.at[k], r.wr_sem.at[k], other
                ).wait_recv()
            pltpu.make_async_copy(
                sib_w[name], held_w[name], r.w_sem.at[WEIGHTS.index(name)]
            ).start()

    def wait_weight(name):
        pltpu.make_async_copy(own_w[name], held_w[name], r.w_sem.at[WEIGHTS.index(name)]).wait()

    own_params = [
        pltpu.make_async_copy(r.in_norm, r.norm.at[c], r.p_sem.at[0]),
        pltpu.make_async_copy(r.in_bias, r.bias.at[c], r.p_sem.at[1]),
    ]
    for copy in own_params:
        copy.start()

    r.grid[...] = jnp.zeros(r.grid.shape, F32)

    pl.semaphore_wait(barrier, 2 * n - 1)

    weight_sends = []
    for k, name in enumerate(WEIGHTS):
        copy = remote(
            own_w[name], sib_w[name], r.ws_sem.at[k], r.wr_sem.at[k], other
        )
        copy.start()
        weight_sends.append(copy)
    param_sends = [
        remote(r.in_norm, r.norm.at[c], r.ps_sem.at[0], r.pr_sem.at[0], other),
        remote(r.in_bias, r.bias.at[c], r.ps_sem.at[1], r.pr_sem.at[1], other),
    ]
    for copy in param_sends:
        copy.start()

    msg, inbox = r.msg, r.inbox
    exchanges = [0]

    def peer_of(level, k):
        size, stride = levels[level]
        here = lax.rem(lax.div(i, stride), size)
        return (c, i + (lax.rem(here + k, size) - here) * stride)

    def copies_of(par, level, size_rows):
        size, _ = levels[level]
        return [
            remote(
                msg.at[par, level, pl.ds(0, size_rows)],
                inbox.at[par, level, k, pl.ds(0, size_rows)],
                r.ms_sem.at[par, level, k],
                r.mr_sem.at[par, level, k],
                peer_of(level, k),
            )
            for k in range(1, size)
        ]

    def exchange_start(size_rows):
        par = exchanges[0] % 2
        exchanges[0] += 1
        copies = copies_of(par, 0, size_rows)
        for copy in copies:
            copy.start()
        return (par, size_rows, copies)

    def exchange_finish(handle, combine):
        par, size_rows, copies = handle
        for level in range(len(levels)):
            if level:
                copies = copies_of(par, level, size_rows)
                for copy in copies:
                    copy.start()
            for copy in copies:
                copy.wait_recv()
            result = combine(par, level)
            for copy in copies:
                copy.wait_send()
            if level + 1 < len(levels):
                msg[par, level + 1, 0:size_rows, :] = result
        return result

    cnt = r.cnt

    def count_copies(level):
        size, _ = levels[level]
        return [
            remote(
                cnt.at[level, 0],
                cnt.at[level, k],
                r.cs_sem.at[level, k],
                r.cr_sem.at[level, k],
                peer_of(level, k),
            )
            for k in range(1, size)
        ]

    cnt[0, 0] = jnp.full((8, LANES), pixels_own, F32)
    for copy in count_copies(0):
        copy.start()

    def count_finish():
        for level in range(len(levels)):
            copies = count_copies(level)
            if level:
                for copy in copies:
                    copy.start()
            total = cnt[level, 0]
            for k, copy in enumerate(copies):
                copy.wait()
                total = total + cnt[level, k + 1]
            if level + 1 < len(levels):
                cnt[level + 1, 0] = total
        r.total[...] = total

    def sum_combine(nt):
        def combine(par, level):
            size, _ = levels[level]
            total = msg[par, level, 0 : 2 * nt, :]
            for k in range(1, size):
                total = total + inbox[par, level, k, 0 : 2 * nt, :]
            return total

        return combine

    def moment_combine(nt):
        def combine(par, level):
            size, _ = levels[level]

            def slot(k):
                if k == 0:
                    return msg[par, level, 0 : 2 * nt, :]
                return inbox[par, level, k, 0 : 2 * nt, :]

            items = [slot(k) for k in range(size)]
            counts = [r.cnt[level, k, 0:1, :] for k in range(size)]
            total = items[0][0:nt]
            count = counts[0]
            for k in range(1, size):
                total = total + items[k][0:nt]
                count = count + counts[k]
            mean = total / count
            spread = jnp.zeros_like(total)
            for k in range(size):
                gap = items[k][0:nt] / counts[k] - mean
                spread = spread + items[k][nt : 2 * nt] + counts[k] * gap * gap
            return jnp.concatenate([total, spread], axis=0)

        return combine

    def norm_send(ref, nt):
        par = exchanges[0] % 2

        def body(j):
            values = cube(ref[view(j)])
            total = fold(values * valid)
            gap = (values - total / pixels_own) * valid
            msg[par, 0, pl.ds(j, 1), :] = total
            msg[par, 0, pl.ds(nt + j, 1), :] = fold(gap * gap)

        loop(nt, body)
        return exchange_start(2 * nt)

    def norm_receive(handle, nt, s, row0):
        result = exchange_finish(handle, moment_combine(nt))
        everyone = r.total[0:1, :]
        r.mean[0:nt, :] = result[0:nt] / everyone
        r.rstd[s, row0 : row0 + nt, :] = lax.rsqrt(result[nt : 2 * nt] / everyone + EPSILON)

    def gain_of(s, offset, j):
        lanes = pl.ds(pl.multiple_of(offset + j * LANES, LANES), LANES)
        return (r.norm[s, 0:1, lanes], r.norm[s, 1:2, lanes])

    def row_of(ref, j):
        return ref[pl.ds(j, 1), :]

    grid = r.grid

    def to_grid(values, lanes):
        for h in range(SIDE):
            at = ((h + 1) * GRID + 1) * segs
            grid[at : at + SIDE * segs, lanes] = values[h * SIDE * segs : (h + 1) * SIDE * segs]

    def patches(target, width, flip):
        def body(j):
            lanes = tile(j)
            for tap in range(9):
                down, right = tap // 3, tap % 3
                if flip:
                    down, right = 2 - down, 2 - right
                pieces = []
                for h in range(SIDE):
                    at = ((h + down) * GRID + right) * segs
                    pieces.append(grid[at : at + SIDE * segs, lanes])
                target[:, pl.ds(pl.multiple_of(tap * width + j * LANES, LANES), LANES)] = packed(
                    jnp.concatenate(pieces, axis=0)
                )

        loop(width // LANES, body)

    def put(slot, target, kind, s):
        @pl.when(c == s)
        def _():
            pltpu.make_async_copy(stage.at[slot], target.at[c], r.o_sem.at[kind, 0]).start()

        @pl.when(c != s)
        def _():
            remote(
                stage.at[slot],
                target.at[c],
                r.o_sem.at[kind, 1],
                r.o_sem.at[kind, 2],
                other,
            ).start()

    def put_wait(slot, target, kind, s):
        @pl.when(c == s)
        def _():
            pltpu.make_async_copy(stage.at[slot], target.at[c], r.o_sem.at[kind, 0]).wait()

        @pl.when(c != s)
        def _():
            remote(
                stage.at[slot],
                target.at[c],
                r.o_sem.at[kind, 1],
                r.o_sem.at[kind, 2],
                other,
            ).wait_send()

    def stage_to_v(slot):
        def body(j):
            v[:, tile(j)] = packed(stage[slot, :, :, tile(j)].astype(F32))

        loop(ch // LANES, body)

    n_mid = mid // LANES
    n_ch = ch // LANES

    for name in WEIGHTS:
        load_weight(name, 0, True)
    load_frames.wait()
    stage_to_v(0)
    for copy in own_params:
        copy.wait()
    for copy in param_sends:
        copy.wait_recv()

    for s in range(2):
        nh1, nh2, nh3 = r.nh1.at[s], r.nh2.at[s], r.nh3.at[s]
        wait_weight("red")
        nh1[...] = dot(v[...], r.red[...])
        if s == 0:
            load_weight("red", 1, True)
        handle = norm_send(nh1, n_mid)
        if s == 0:
            count_finish()
        norm_receive(handle, n_mid, s, 0)

        def act_one(j, s=s, nh1=nh1):
            gain, offset = gain_of(s, 0, j)
            normed = (nh1[view(j)] - row_of(r.mean, j)) * row_of(r.rstd.at[s], j)
            nh1[view(j)] = normed
            before = normed * gain + offset
            act = before * sigmoid(before)
            r.a1[s, :, tile(j)] = packed(act)
            to_grid(act, tile(j))

        loop(n_mid, act_one)
        patches(r.patch, mid, False)
        wait_weight("spa")
        nh2[...] = dot(r.patch[...], r.spa[...])
        if s == 0:
            load_weight("spa", 1, True)
        handle = norm_send(nh2, n_mid)
        norm_receive(handle, n_mid, s, n_mid)

        def act_two(j, s=s, nh2=nh2):
            gain, offset = gain_of(s, mid, j)
            normed = (nh2[view(j)] - row_of(r.mean, j)) * row_of(r.rstd.at[s], n_mid + j)
            nh2[view(j)] = normed
            before = normed * gain + offset
            r.h2[s, :, tile(j)] = packed(before * sigmoid(before))

        loop(n_mid, act_two)
        for name in SMALL:
            wait_weight(name)
        squeezed = cube(dot(r.h2[s], r.squ[...])[:rows])
        later = pltpu.roll(squeezed, segs - 1, 1)
        field = (paired * (later - squeezed)).reshape(rows, red_w)
        r.field[s] = packed(field)
        rounded = r.field[s].astype(F32)[:rows]
        to_grid(rounded, pl.ds(0, LANES))
        patches(r.patch_m, red_w, False)
        context_mean = jnp.sum(cube(rounded), axis=0) * (1.0 / PIX)
        r.cmean[s] = context_mean
        from_mean = jnp.dot(
            context_mean, r.con[...].astype(F32), precision=HIGH, preferred_element_type=F32
        )
        mixed = cube(dot(r.patch_m[...], r.mot[...])[:rows]) + from_mean
        r.score[s] = packed(mixed)
        free[0:full, :] = dot(r.score[s], r.gat[...])

        def gate(j, s=s):
            bias = r.bias[s, 0:1, tile(j)]
            sigma = sigmoid(free[view(j)] + bias)
            r.sigma[s, 0:rows, tile(j)] = sigma
            h2 = r.h2[s, :, tile(j)].astype(F32)[:rows]
            r.gated[s, :, tile(j)] = packed(h2 * (0.5 + sigma))

        loop(n_mid, gate)
        if s == 0:
            for name in SMALL:
                load_weight(name, 1, True)
        wait_weight("exp")
        for block in range(ch // ROW):
            nh3[block * full : (block + 1) * full, :] = dot(
                r.gated[s], r.exp[:, block * ROW : (block + 1) * ROW]
            )
        if s == 0:
            load_weight("exp", 1, True)
        handle = norm_send(nh3, n_ch)
        norm_receive(handle, n_ch, s, 2 * n_mid)
        slot = 1 - s

        def finish(j, s=s, nh3=nh3, slot=slot):
            gain, offset = gain_of(s, 2 * mid, j)
            normed = (nh3[view(j)] - row_of(r.mean, j)) * row_of(
                r.rstd.at[s], 2 * n_mid + j
            )
            nh3[view(j)] = normed
            before = v[:, tile(j)].astype(F32)[:rows] + normed * gain + offset
            out = cube(before * sigmoid(before)) * valid
            stage[slot, :, :, tile(j)] = out.astype(BF)
            if s == 0:
                v[:, tile(j)] = packed(out)

        loop(n_ch, finish)
        put(slot, r.out, s, s)
        if s == 0:
            put_wait(slot, r.out, 0, 0)
            load_grad = pltpu.make_async_copy(r.out_grad.at[c], stage.at[1], r.load_sem.at[1])
            load_grad.start()

    def send_sem(chunk, k):
        return r.rs_send.at[CHUNKS.index(chunk), k]

    def recv_sem(chunk, k):
        return r.rs_recv.at[CHUNKS.index(chunk), k]

    def add_loop(target, others, pieces):
        def body(j):
            at = target.at[j]
            total = at[...]
            for item in others:
                total = total + item.at[j][...]
            at[...] = total

        loop(pieces, body)

    def rs0(chunk):
        return [
            remote(
                chunk_refs[chunk].g.at[1 - c],
                chunk_refs[chunk].r0,
                send_sem(chunk, 0),
                recv_sem(chunk, 0),
                other,
            )
        ]

    def device_at(f, g, depth_at):
        px = f * (1 - c) + g * c
        py = g * (1 - c) + f * c
        return (c, depth_at * side * side + py * side + px)

    def rs1(chunk):
        found = []
        for k in range(1, side):
            f = lax.rem(fc + k, side)
            found.append(
                remote(
                    chunk_refs[chunk].g.at[c, f],
                    chunk_refs[chunk].r1.at[k - 1],
                    send_sem(chunk, k),
                    recv_sem(chunk, k),
                    device_at(f, gc, z),
                )
            )
        return found

    def rs2(chunk):
        found = []
        for k in range(1, side):
            g = lax.rem(gc + k, side)
            found.append(
                remote(
                    chunk_refs[chunk].g.at[c, fc, g],
                    chunk_refs[chunk].r2.at[k - 1],
                    send_sem(chunk, side - 1 + k),
                    recv_sem(chunk, side - 1 + k),
                    device_at(fc, g, z),
                )
            )
        return found

    def rs3(chunk):
        found = []
        for k in range(1, depth):
            to = lax.rem(z + k, depth)
            copy = remote(
                chunk_refs[chunk].g.at[c, fc, gc, lax.rem(to, slots)],
                chunk_refs[chunk].r3.at[k - 1],
                send_sem(chunk, 2 * (side - 1) + k),
                recv_sem(chunk, 2 * (side - 1) + k),
                device_at(fc, gc, to),
            )
            found.append((to, copy))
        return found

    def go(copies):
        for copy in copies:
            copy.start()

    def rs0_start(chunk):
        go(rs0(chunk))

    def rs1_start(chunk):
        for copy in rs0(chunk):
            copy.wait()
        own = chunk_refs[chunk].g.at[c]
        r0 = chunk_refs[chunk].r0
        for f in range(side):
            for g in range(side):
                add_loop(own.at[f, g], [r0.at[f, g]], slots)
        go(rs1(chunk))

    def rs2_start(chunk):
        copies = rs1(chunk)
        for copy in copies:
            copy.wait_recv()
        own = chunk_refs[chunk].g.at[c, fc]
        r1 = chunk_refs[chunk].r1
        for g in range(side):
            add_loop(own.at[g], [r1.at[k, g] for k in range(side - 1)], slots)
        for copy in copies:
            copy.wait_send()
        go(rs2(chunk))

    def rs3_start(chunk):
        copies = rs2(chunk)
        for copy in copies:
            copy.wait_recv()
        r2 = chunk_refs[chunk].r2
        add_loop(chunk_refs[chunk].g.at[c, fc, gc], [r2.at[k] for k in range(side - 1)], slots)
        for copy in copies:
            copy.wait_send()
        for to, copy in rs3(chunk):
            if slots == depth:
                copy.start()
            else:
                pl.when(to < slots)(copy.start)

    def owners(comp):
        start, size = parts[comp]
        at = start + size * i
        first = lax.div(at * ROW, share)
        last = lax.div(jnp.minimum((at + size) * ROW, pp.total) - 1, share)
        exists = jnp.logical_and(i < PIECES, at * ROW < pp.total)
        return at, first, last, exists

    def send_piece(comp, s, action):
        _, size = parts[comp]
        at, first, last, exists = owners(comp)
        which = COMPS.index(comp)
        for k in range(pp.reach):
            to = first + k
            base = lax.div(to * share, ROW * 16) * 16
            row = pl.multiple_of(pp.margin + at - base, 16)
            there = r.land.at[pl.ds(row, size), pl.ds(pl.multiple_of(c * HALF, HALF), HALF)]
            needed = jnp.logical_and(exists, to <= last)
            here = jnp.logical_and(c == s, to == i)
            source = fin[comp]
            arrival = r.land_sem.at[which, c, lax.rem(i, PIECES)]

            @pl.when(jnp.logical_and(needed, here))
            def _():
                copy = pltpu.make_async_copy(source, there, arrival)
                if action == "start":
                    copy.start()
                else:
                    copy.wait()

            @pl.when(jnp.logical_and(needed, jnp.logical_not(here)))
            def _():
                copy = remote(source, there, r.fin_sem.at[which, k], arrival, (s, to))
                if action == "start":
                    copy.start()
                else:
                    copy.wait_send()

    def finish_chunk(chunk, s):
        own = chunk_refs[chunk].g.at[c, fc, gc]
        r3 = chunk_refs[chunk].r3
        copies = rs3(chunk)

        def work():
            for _, copy in copies:
                copy.wait_recv()
            mine = own.at[lax.rem(z, slots)]

            def summed(first, count):
                total = mine[first : first + count, :].astype(F32)
                for k in range(depth - 1):
                    total = total + r3[k, first : first + count, :].astype(F32)
                return total

            mix = r.mix

            def weave(first, count, stride, value):
                for k in range(HALF // LANES):
                    mix[k, pl.ds(first, count, stride=stride), :] = value[
                        :, k * LANES : (k + 1) * LANES
                    ]

            def woven(target, size):
                for k in range(HALF // LANES):
                    target[:, k * LANES : (k + 1) * LANES] = mix[k, 0:size, :].astype(BF)

            cins = mid // PIECES
            if chunk == "a":
                size = parts["exp"][1]
                quarters = size // cins
                for q in range(quarters):
                    weave(q, cins, quarters, summed(q * cins, cins))
                woven(r.fin_exp, size)
                r.fin_small[...] = summed(size, parts["small"][1]).astype(BF)
            elif chunk == "b":
                size = parts["spa"][1]
                for tap in range(9):
                    weave(tap, cins, 9, summed(tap * cins, cins))
                woven(r.fin_spa, size)
            else:
                r.fin_red[...] = summed(0, parts["red"][1]).astype(BF)

        if slots == depth:
            work()
        else:
            pl.when(z < slots)(work)
        for to, copy in copies:
            if slots == depth:
                copy.wait_send()
            else:
                pl.when(to < slots)(copy.wait_send)
        for comp in HOLDS[chunk]:
            send_piece(comp, s, "start")

    def finish_sent(chunk, s):
        for comp in HOLDS[chunk]:
            send_piece(comp, s, "wait")

    def place(half, piece):
        px, py, pz = piece % side, (piece // side) % side, piece // (side * side)
        return (half, px, py, pz) if half == 0 else (half, py, px, pz)

    small_at = 2 * full

    def grads_a(s):
        cins = mid // PIECES
        g = r.g_a
        for q in range(ch // ROW):
            for half in range(2):
                lanes = slice(q * ROW + half * HALF, q * ROW + (half + 1) * HALF)
                value = dot_tn(r.gated[s], r.gz3[:, lanes]).astype(BF)
                for piece in range(PIECES):
                    where = place(half, piece)
                    g[where + (slice(q * cins, (q + 1) * cins),)] = value[
                        piece * cins : (piece + 1) * cins
                    ]
        tmp = r.tmp1
        at = small_at
        per = ROW // LANES

        def spread(count):
            for q in range(per):
                free[at : at + count, q * LANES : (q + 1) * LANES] = tmp[
                    pl.ds(q, count, stride=per), :
                ]

        tmp[0:mid, :] = dot_tn(r.h2[s], r.gr[...])
        spread(mid // per)
        at += mid // per
        moved = dot_tn(r.field[s], r.patch_m[...])
        for tap in range(9):
            tmp[pl.ds(tap, red_w, stride=9), :] = moved[:, tap * LANES : (tap + 1) * LANES]
        spread(9 * red_w // per)
        at += 9 * red_w // per
        tmp[0:red_w, :] = lax.dot_general(
            r.cmean[s],
            r.ssum[...],
            (((0,), (0,)), ((), ())),
            precision=HIGH,
            preferred_element_type=F32,
        )
        spread(red_w // per)
        at += red_w // per
        free[at : at + red_w, :] = dot_tn(r.score[s], r.gl[...])
        at += red_w
        free[at : at + 8, :] = jnp.broadcast_to(r.gbias[...], (8, mid))
        start = parts["exp"][1]
        size = parts["small"][1]
        used = -(-pp.small_rows // size)
        for piece in range(PIECES):
            for half in range(2):
                where = place(half, piece) + (slice(start, start + size),)
                if piece < used:
                    g[where] = free[
                        small_at + piece * size : small_at + (piece + 1) * size,
                        half * HALF : (half + 1) * HALF,
                    ].astype(BF)
                else:
                    g[where] = jnp.zeros((size, HALF), BF)

    def grads_b(s):
        cins = mid // PIECES
        g = r.g_b

        def body(tap):
            for half in range(2):
                lanes = pl.ds(pl.multiple_of(tap * mid + half * HALF, HALF), HALF)
                value = dot_tn(r.a1[s], r.patch[:, lanes]).astype(BF)
                for piece in range(PIECES):
                    where = place(half, piece)
                    g[where + (pl.ds(pl.multiple_of(tap * cins, cins), cins),)] = value[
                        piece * cins : (piece + 1) * cins
                    ]

        loop(9, body)

    def grads_c(s):
        g = r.g_c
        size = parts["red"][1]
        for half in range(2):
            value = dot_tn(v[...], r.gz1[:, half * HALF : (half + 1) * HALF]).astype(BF)
            for piece in range(PIECES):
                g[place(half, piece)] = value[piece * size : (piece + 1) * size]

    def back_receive(handle, nt, s, row0):
        result = exchange_finish(handle, sum_combine(nt))
        half_rows = 2 * n_mid + n_ch
        r.gnorm[s, row0 : row0 + nt, :] = result[nt : 2 * nt]
        r.gnorm[s, half_rows + row0 : half_rows + row0 + nt, :] = result[0:nt]
        r.bsum[0 : 2 * nt, :] = result / r.total[0:1, :]

    def norm_grad(grad, normed, s, offset, row0, nt, j):
        gain, _ = gain_of(s, offset, j)
        scale = gain * row_of(r.rstd.at[s], row0 + j)
        mean_grad = row_of(r.bsum, j)
        mean_cross = row_of(r.bsum, nt + j)
        return scale * (cube(grad) - valid * (mean_grad + cube(normed) * mean_cross))

    def slope_send(s, grad_at, normed_ref, offset, nt):
        par = exchanges[0] % 2

        def body(j):
            gain, shift = gain_of(s, offset, j)
            normed = normed_ref[view(j)]
            grad = free[view(j, grad_at)] * silu_slope(normed * gain + shift)
            free[view(j, grad_at)] = grad
            msg[par, 0, pl.ds(j, 1), :] = fold(cube(grad))
            msg[par, 0, pl.ds(nt + j, 1), :] = fold(cube(grad * normed))

        loop(nt, body)
        return exchange_start(2 * nt)

    gs = r.gs
    for s in (1, 0):
        nh1, nh2, nh3 = r.nh1.at[s], r.nh2.at[s], r.nh3.at[s]
        slot = s
        if s == 1:
            load_grad.wait()
        par = exchanges[0] % 2

        def back_three(j, s=s, nh3=nh3, slot=slot, par=par):
            gain, shift = gain_of(s, 2 * mid, j)
            normed = nh3[view(j)]
            before = v[:, tile(j)].astype(F32)[:rows] + normed * gain + shift
            grad = cube(silu_slope(before)) * valid * stage[slot, :, :, tile(j)].astype(F32)
            gs[view(j)] = grad.reshape(rows, LANES)
            msg[par, 0, pl.ds(j, 1), :] = fold(grad)
            msg[par, 0, pl.ds(n_ch + j, 1), :] = fold(grad * cube(normed))

        loop(n_ch, back_three)
        handle = exchange_start(2 * n_ch)
        if s == 0:
            rs1_start("c")
            rs3_start("a")
        back_receive(handle, n_ch, s, 2 * n_mid)

        def grad_three(j, s=s, nh3=nh3):
            r.gz3[:, tile(j)] = packed(
                norm_grad(gs[view(j)], nh3[view(j)], s, 2 * mid, 2 * n_mid, n_ch, j)
            )

        loop(n_ch, grad_three)
        if s == 0:
            wait_weight("exp")
        free[0:full, :] = dot_nt(r.gz3[...], r.exp[...])
        if s == 1:
            load_weight("exp", 0, False)

        def back_gate(j, s=s):
            grad = free[view(j)]
            sigma = r.sigma[s, 0:rows, tile(j)]
            h2 = r.h2[s, :, tile(j)].astype(F32)[:rows]
            free[view(j, full)] = grad * (0.5 + sigma)
            value = packed(grad * h2 * sigma * (1.0 - sigma))
            r.gl[:, tile(j)] = value
            r.gbias[0:1, tile(j)] = fold(cube(value.astype(F32)[:rows]))

        loop(n_mid, back_gate)
        if s == 0:
            for name in SMALL:
                wait_weight(name)
        r.gq[...] = dot_nt(r.gl[...], r.gat[...]).astype(BF)
        rounded = r.gq[...].astype(F32)[:rows]
        to_grid(rounded, pl.ds(0, LANES))
        patches(r.patch_m, red_w, True)
        score_sums = jnp.sum(cube(rounded), axis=0)
        r.ssum[...] = score_sums
        grad_field = None
        for tap in range(9):
            part = dot_nt(
                r.patch_m[:, tap * red_w : (tap + 1) * red_w],
                r.mot[tap * red_w : (tap + 1) * red_w, :],
            )
            grad_field = part if grad_field is None else grad_field + part
        from_mean = lax.dot_general(
            score_sums,
            r.con[...].astype(F32),
            (((1,), (1,)), ((), ())),
            precision=HIGH,
            preferred_element_type=F32,
        ) * (1.0 / PIX)
        weighted = paired * (cube(grad_field[:rows]) + from_mean)
        r.gr[...] = packed(pltpu.roll(weighted, 1, 1) - weighted)
        free[full : 2 * full, :] += dot_nt(r.gr[...], r.squ[...])
        if s == 1:
            for name in SMALL:
                load_weight(name, 0, False)
        handle = slope_send(s, full, nh2, mid, n_mid)
        if s == 0:
            finish_chunk("a", 1)
            rs3_start("b")
        grads_a(s)
        rs0_start("a")
        back_receive(handle, n_mid, s, n_mid)

        def grad_two(j, s=s, nh2=nh2):
            value = norm_grad(free[view(j, full)], nh2[view(j)], s, mid, n_mid, n_mid, j)
            to_grid(value.reshape(rows, LANES), tile(j))

        loop(n_mid, grad_two)
        patches(r.patch, mid, True)
        if s == 0:
            wait_weight("spa")
        acc = None
        for tap in range(9):
            part = dot_nt(
                r.patch[:, tap * mid : (tap + 1) * mid], r.spa[tap * mid : (tap + 1) * mid, :]
            )
            acc = part if acc is None else acc + part
        free[0:full, :] = acc
        if s == 1:
            load_weight("spa", 0, False)
        handle = slope_send(s, 0, nh1, 0, n_mid)
        if s == 0:
            finish_chunk("b", 1)
            rs2_start("c")
        grads_b(s)
        rs0_start("b")
        rs1_start("a")
        back_receive(handle, n_mid, s, 0)

        def grad_one(j, s=s, nh1=nh1):
            r.gz1[:, tile(j)] = packed(
                norm_grad(free[view(j)], nh1[view(j)], s, 0, 0, n_mid, j)
            )

        loop(n_mid, grad_one)
        if s == 0:
            rs3_start("c")
            finish_chunk("c", 1)
        rs1_start("b")
        grads_c(s)
        rs0_start("c")
        rs2_start("a")
        if s == 1:
            put_wait(0, r.out, 1, 1)
            reload = pltpu.make_async_copy(r.frames.at[c], stage.at[1], r.load_sem.at[0])
            reload.start()
        else:
            wait_weight("red")
        slot = 1 - s
        for block in range(ch // ROW):
            value = gs[block * full : block * full + rows, :] + dot_nt(
                r.gz1[...], r.red[block * ROW : (block + 1) * ROW, :]
            )[:rows]
            stage[slot, :, :, block * ROW : (block + 1) * ROW] = cube(value).astype(BF)
        put(slot, r.ing, 2 + s, s)
        if s == 1:
            load_weight("red", 0, False)
            rs2_start("b")
            reload.wait()
            stage_to_v(1)

    gn_send = remote(
        r.gnorm.at[1 - c], r.gnorm_in, r.gn_sem.at[0], r.gn_sem.at[1], other
    )
    gn_send.start()
    for chunk in CHUNKS:
        finish_sent(chunk, 1)
    rs1_start("c")
    rs3_start("a")
    rs2_start("b")
    rs2_start("c")
    finish_chunk("a", 0)
    rs3_start("b")
    rs3_start("c")
    finish_chunk("b", 0)
    finish_chunk("c", 0)
    gn_send.wait()
    r.gnorm_out[...] = r.gnorm[c] + r.gnorm_in[...]

    for copy in weight_sends + param_sends:
        copy.wait_send()
    put_wait(0, r.ing, 3, 1)
    put_wait(1, r.ing, 2, 0)
    for base, target in ((0, r.out), (2, r.ing)):
        for s in range(2):

            @pl.when(c == s)
            def _():
                remote(
                    stage.at[0],
                    target.at[1 - c],
                    r.o_sem.at[base + s, 1],
                    r.o_sem.at[base + s, 2],
                    other,
                ).wait_recv()

    for chunk in CHUNKS:
        finish_sent(chunk, 0)
    low = i * share
    high = low + share
    for which, comp in enumerate(COMPS):
        start, size = parts[comp]

        def arrive(piece, _):
            first = (start + size * piece) * ROW
            last = jnp.minimum(first + size * ROW, pp.total)

            @pl.when(jnp.logical_and(first < high, last > low))
            def _():
                for core in range(2):
                    own = jnp.logical_and(c == core, i == piece)

                    @pl.when(jnp.logical_not(own))
                    def _():
                        pltpu.make_async_copy(
                            fin[comp],
                            r.land.at[pl.ds(0, size), pl.ds(0, HALF)],
                            r.land_sem.at[which, core, piece],
                        ).wait()

            return 0

        lax.fori_loop(0, PIECES, arrive, 0)


def run(n, sizes, frames, out_grad, seg_counts, weights, bias, norm):
    ch, mid, red_w, segs, share = sizes
    pp = plan(n, ch, mid, red_w, segs, share)
    side, depth, slots, levels, parts = pp.side, pp.depth, pp.slots, pp.levels, pp.parts
    rows = PIX * segs
    full = up(rows, 16)
    norm_rows = 2 * (2 * mid + ch) // LANES
    group = max(size for size, _ in levels)
    any_spec = pl.BlockSpec(memory_space=pl.ANY)
    vmem_spec = pl.BlockSpec(memory_space=pltpu.VMEM)

    ins = dict(
        frames=frames,
        out_grad=out_grad,
        in_red=weights.red,
        in_spa=weights.spa,
        in_exp=weights.exp,
        in_squ=weights.squ,
        in_mot=weights.mot,
        in_con=weights.con,
        in_gat=weights.gat,
        counts=seg_counts,
        in_bias=bias,
        in_norm=norm,
    )
    in_specs = [any_spec] * 9 + [pl.BlockSpec(memory_space=pltpu.SMEM), vmem_spec, vmem_spec]

    def like(item):
        return jax.ShapeDtypeStruct(item.shape, item.dtype)

    outs = dict(
        out=like(frames),
        ing=like(frames),
        land=jax.ShapeDtypeStruct((pp.land, ROW), BF),
        sib_red=like(weights.red),
        sib_spa=like(weights.spa),
        sib_exp=like(weights.exp),
        sib_squ=like(weights.squ),
        sib_mot=like(weights.mot),
        sib_con=like(weights.con),
        sib_gat=like(weights.gat),
        gnorm_out=jax.ShapeDtypeStruct((norm_rows, LANES), F32),
    )
    out_specs = [any_spec] * 10 + [vmem_spec]

    def low(*dims):
        return pltpu.VMEM(dims, BF)

    def wide(*dims):
        return pltpu.VMEM(dims, F32)

    def sems(*dims):
        return pltpu.SemaphoreType.DMA(dims)

    def piled(size):
        return (
            low(2, side, side, slots, size, HALF),
            low(side, side, slots, size, HALF),
            low(max(side - 1, 1), side, slots, size, HALF),
            low(max(side - 1, 1), slots, size, HALF),
            low(max(depth - 1, 1), size, HALF),
        )

    pile_a = piled(parts["exp"][1] + parts["small"][1])
    pile_b = piled(parts["spa"][1])
    pile_c = piled(parts["red"][1])
    hops = 2 * (side - 1) + depth
    scratch = dict(
        red=low(*weights.red.shape),
        spa=low(*weights.spa.shape),
        exp=low(*weights.exp.shape),
        squ=low(*weights.squ.shape),
        mot=low(*weights.mot.shape),
        con=low(*weights.con.shape),
        gat=low(*weights.gat.shape),
        bias=wide(2, *bias.shape),
        norm=wide(2, *norm.shape),
        stage=low(2, *frames.shape[1:]),
        v=low(full, ch),
        nh1=wide(2, full, mid),
        nh2=wide(2, full, mid),
        nh3=wide(2, full * ch // ROW, ROW),
        gs=wide(full * ch // ROW, ROW),
        sigma=wide(2, full, mid),
        a1=low(2, full, mid),
        h2=low(2, full, mid),
        gated=low(2, full, mid),
        field=low(2, full, red_w),
        score=low(2, full, red_w),
        cmean=wide(2, segs, red_w),
        ssum=wide(segs, red_w),
        gbias=wide(1, mid),
        gz3=low(full, ch),
        gz1=low(full, mid),
        gl=low(full, mid),
        gq=low(full, red_w),
        gr=low(full, red_w),
        patch=low(full, 9 * mid),
        patch_m=low(full, 9 * red_w),
        grid=wide(GRID * GRID * segs, mid),
        tmp1=wide(9 * red_w, LANES),
        mix=wide(HALF // LANES, max(parts["spa"][1], parts["exp"][1]), LANES),
        msg=wide(2, len(levels), 2 * ch // LANES, LANES),
        inbox=wide(2, len(levels), group, 2 * ch // LANES, LANES),
        cnt=wide(len(levels), group, 8, LANES),
        total=wide(8, LANES),
        mean=wide(ch // LANES, LANES),
        bsum=wide(2 * ch // LANES, LANES),
        rstd=wide(2, norm_rows // 2, LANES),
        gnorm=wide(2, norm_rows, LANES),
        gnorm_in=wide(norm_rows, LANES),
        g_a=pile_a[0],
        r0_a=pile_a[1],
        r1_a=pile_a[2],
        r2_a=pile_a[3],
        r3_a=pile_a[4],
        g_b=pile_b[0],
        r0_b=pile_b[1],
        r1_b=pile_b[2],
        r2_b=pile_b[3],
        r3_b=pile_b[4],
        g_c=pile_c[0],
        r0_c=pile_c[1],
        r1_c=pile_c[2],
        r2_c=pile_c[3],
        r3_c=pile_c[4],
        fin_red=low(parts["red"][1], HALF),
        fin_spa=low(parts["spa"][1], HALF),
        fin_exp=low(parts["exp"][1], HALF),
        fin_small=low(parts["small"][1], HALF),
        load_sem=sems(2),
        w_sem=sems(len(WEIGHTS)),
        ws_sem=sems(len(WEIGHTS)),
        wr_sem=sems(len(WEIGHTS)),
        p_sem=sems(2),
        ps_sem=sems(2),
        pr_sem=sems(2),
        ms_sem=sems(2, len(levels), group),
        mr_sem=sems(2, len(levels), group),
        cs_sem=sems(len(levels), group),
        cr_sem=sems(len(levels), group),
        o_sem=sems(4, 3),
        rs_send=sems(3, hops),
        rs_recv=sems(3, hops),
        fin_sem=sems(4, pp.reach),
        land_sem=sems(4, 2, PIECES),
        gn_sem=sems(2),
    )
    names = list(ins) + list(outs) + list(scratch)
    results = pl.pallas_call(
        functools.partial(kernel, n, sizes, names),
        out_shape=list(outs.values()),
        in_specs=in_specs,
        out_specs=out_specs,
        scratch_shapes=list(scratch.values()),
        cost_estimate=pl.CostEstimate(
            flops=22 * 10**9, bytes_accessed=10**8, transcendentals=10**7
        ),
        compiler_params=pltpu.CompilerParams(
            collective_id=0, has_side_effects=True, vmem_limit_bytes=64 * 2**20 - 2**17
        ),
    )(*ins.values())
    return results[0], results[1], results[2], results[-1]


def on_device(n, share, frames, out_grad, seg_counts, *params):
    reducer, spatial, expander, squeezer, motion, context, gating, bias, norm = params
    _, segs, pixels, ch = frames.shape
    mid, red_w = reducer.shape[-1], squeezer.shape[-1]
    sizes = (ch, mid, red_w, segs, share)
    weights = SimpleNamespace(
        red=reducer[0],
        spa=spatial[0].transpose(1, 0, 2).reshape(9 * mid, mid),
        exp=expander[0],
        squ=squeezer[0],
        mot=motion[0].transpose(1, 0, 2).reshape(9 * red_w, red_w),
        con=context[0],
        gat=gating[0],
    )
    out, ing, land, gnorm = run(
        n,
        sizes,
        frames.transpose(0, 2, 1, 3),
        out_grad.transpose(0, 2, 1, 3),
        seg_counts,
        weights,
        bias,
        norm[0],
    )
    pp = plan(n, ch, mid, red_w, segs, share)
    start = pp.margin * ROW + lax.rem(lax.axis_index("dp") * share, ROW * 16)
    flat = lax.dynamic_slice(land.astype(F32).reshape(-1), (start,), (share,))
    return (
        out.transpose(0, 2, 1, 3)[None],
        ing.transpose(0, 2, 1, 3)[None],
        flat[None],
        gnorm.reshape(norm.shape),
    )


def solution(mesh):
    n = mesh.shape["dp"]

    def whole(*args):
        entries = sum(item.size // item.shape[0] for item in args[3:11])
        share = up(entries, n) // n
        body = jax.shard_map(
            functools.partial(on_device, n, share),
            mesh=mesh,
            in_specs=(
                P("dp", None, None, None),
                P("dp", None, None, None),
                P("dp"),
                P("pipe", None, None),
                P("pipe", None, None, None),
                P("pipe", None, None),
                P("pipe", None, None),
                P("pipe", None, None, None),
                P("pipe", None, None),
                P("pipe", None, None),
                P("pipe", None),
                P("pipe", None, None),
            ),
            out_specs=(
                P("pipe", "dp", None, None, None),
                P("pipe", "dp", None, None, None),
                P("pipe", "dp"),
                P("pipe", None, None),
            ),
            check_vma=False,
        )
        return body(*args)

    return whole
```

```python
import functools
from types import SimpleNamespace

import jax
import jax.numpy as jnp
from jax import lax
from jax.experimental import pallas as pl
from jax.experimental.pallas import tpu as pltpu
from jax.sharding import PartitionSpec as P

SIDE = 7
PIX = 49
MICRO = 2
PIECES = 16
EPSILON = 1e-05
HIGH = lax.Precision.HIGHEST
BF = jnp.bfloat16
F32 = jnp.float32
MESH = pl.DeviceIdType.MESH
LANES = 128
GROUP = 4
HALF = 256
ROW = 512
GRID = SIDE + 2
WEIGHTS = ("red", "spa", "exp", "squ", "mot", "con", "gat")
SMALL = ("squ", "mot", "con", "gat")
CHUNKS = ("e", "m", "t", "c")
SPLIT = 5
COMPS = ("red", "spa", "exp", "small")
HOLDS = dict(e=("exp",), m=(), t=("spa", "small"), c=("red",))


def sigmoid(values):
    return 0.5 * jnp.tanh(0.5 * values) + 0.5


def silu_slope(values):
    sigma = sigmoid(values)
    return sigma * (1.0 + values * (1.0 - sigma))


def dot(a, b):
    return jnp.dot(a, b, preferred_element_type=F32)


def dot_nt(a, b):
    return lax.dot_general(a, b, (((1,), (1,)), ((), ())), preferred_element_type=F32)


def dot_tn(a, b):
    return lax.dot_general(a, b, (((0,), (0,)), ((), ())), preferred_element_type=F32)


def up(value, step):
    return -(-value // step) * step


def plan(n, ch, mid, red, segs, share):
    side = 4 if n % 64 == 0 else 2 if n % 4 == 0 else 1
    depth = n // (side * side)
    slots = PIECES // (side * side)
    levels = [(n, 1)] if n <= 16 else [(side * side, 1), (depth, side * side)]
    rows = dict(red=ch * mid // ROW, spa=9 * mid * mid // ROW, exp=mid * ch // ROW)
    small = mid * red + 9 * red * red + red * red + red * mid + mid
    small_rows = up(small, ROW) // ROW
    parts = dict(
        red=(0, rows["red"] // PIECES),
        spa=(rows["red"], rows["spa"] // PIECES),
        exp=(rows["red"] + rows["spa"], rows["exp"] // PIECES),
        small=(rows["red"] + rows["spa"] + rows["exp"], up(up(small_rows, PIECES) // PIECES, 16)),
    )
    total = (parts["small"][0] + small_rows) * ROW
    margin = max(size for _, size in parts.values())
    reach = 1
    for start, size in parts.values():
        for piece in range(PIECES):
            first = (start + size * piece) * ROW
            if first < total:
                last = min((start + size * (piece + 1)) * ROW, total) - 1
                reach = max(reach, last // share - first // share + 1)
    land = margin + up(share // ROW + 22, 16) + margin
    return SimpleNamespace(
        side=side,
        depth=depth,
        slots=slots,
        levels=levels,
        parts=parts,
        total=total,
        margin=margin,
        reach=reach,
        land=land,
        small_rows=small_rows,
    )


def kernel(n, sizes, names, *refs):
    r = SimpleNamespace(**dict(zip(names, refs)))
    own_w = dict(
        red=r.in_red, spa=r.in_spa, exp=r.in_exp, squ=r.in_squ, mot=r.in_mot, con=r.in_con, gat=r.in_gat
    )
    sib_w = dict(
        red=r.sib_red, spa=r.sib_spa, exp=r.sib_exp, squ=r.sib_squ, mot=r.sib_mot, con=r.sib_con, gat=r.sib_gat
    )
    held_w = dict(red=r.red, spa=r.spa, exp=r.exp, squ=r.squ, mot=r.mot, con=r.con, gat=r.gat)
    chunk_refs = dict(
        e=SimpleNamespace(g=r.g_e, far=r.far_e, near=r.near_e, r1=r.r1_e, r2=r.r2_e, r3=r.r3_e),
        m=SimpleNamespace(g=r.g_m, far=r.far_m, near=r.near_m, r1=r.r1_m, r2=r.r2_m, r3=r.r3_m),
        t=SimpleNamespace(g=r.g_t, far=r.far_t, near=r.near_t, r1=r.r1_t, r2=r.r2_t, r3=r.r3_t),
        c=SimpleNamespace(g=r.g_c, far=r.far_c, near=r.near_c, r1=r.r1_c, r2=r.r2_c, r3=r.r3_c),
    )
    fin = dict(red=r.fin_red, spa=r.fin_spa, exp=r.fin_exp, small=r.fin_small)
    ch, mid, red_w, segs, share = sizes
    pp = plan(n, ch, mid, red_w, segs, share)
    side, depth, slots, levels, parts = pp.side, pp.depth, pp.slots, pp.levels, pp.parts
    rows = PIX * segs
    full = up(rows, 16)
    pad = full - rows
    c = lax.axis_index("pipe")
    i = lax.axis_index("dp")
    x = lax.rem(i, side)
    y = lax.rem(lax.div(i, side), side)
    z = lax.div(i, side * side)
    fc = x * (1 - c) + y * c
    gc = y * (1 - c) + x * c
    other = (1 - c, i)

    def remote(src, dst, send, recv, device):
        return pltpu.make_async_remote_copy(
            src_ref=src,
            dst_ref=dst,
            send_sem=send,
            recv_sem=recv,
            device_id=device,
            device_id_type=MESH,
        )

    barrier = pltpu.get_barrier_semaphore()

    def greet(k, _):
        peer = lax.rem(i + k, n)
        pl.semaphore_signal(barrier, inc=1, device_id=(c, peer), device_id_type=MESH)
        pl.semaphore_signal(barrier, inc=1, device_id=(1 - c, peer), device_id_type=MESH)
        return 0

    pl.semaphore_signal(barrier, inc=1, device_id=other, device_id_type=MESH)
    lax.fori_loop(1, n, greet, 0)

    count_own = r.counts[c]
    segment = lax.broadcasted_iota(jnp.int32, (segs, LANES), 0)
    valid = jnp.where(segment < count_own, 1.0, 0.0).astype(F32)
    paired = jnp.where(segment + 1 < count_own, 1.0, 0.0).astype(F32)
    pixels_own = PIX * count_own.astype(F32)

    stage = r.stage
    v = r.v
    free = r.nh3.at[1]

    def tile(j):
        return pl.ds(pl.multiple_of(j * LANES, LANES), LANES)

    def view(j, base=0):
        return (
            pl.ds(pl.multiple_of(base + lax.div(j, 4) * full, 16), rows),
            tile(lax.rem(j, 4)),
        )

    def loop(count, body):
        def step(j, _):
            body(j)
            return 0

        lax.fori_loop(0, count, step, 0)

    def packed(values):
        flat = values.reshape(rows, values.shape[-1])
        return jnp.concatenate([flat, jnp.zeros((pad, flat.shape[-1]), F32)], axis=0).astype(BF)

    def cube(values):
        return values.reshape(PIX, segs, values.shape[-1])

    def fold(values):
        return jnp.sum(jnp.sum(values, axis=0), axis=0, keepdims=True)

    def stage_to_v(slot):
        def body(j):
            v[:, tile(j)] = packed(stage[slot, :, :, tile(j)].astype(F32))

        loop(ch // LANES, body)

    load_frames = pltpu.make_async_copy(r.frames.at[c], stage.at[0], r.load_sem.at[0])
    load_frames.start()

    def weight_index(name):
        return WEIGHTS.index(name)

    def held_copy(source, name):
        return pltpu.make_async_copy(source, held_w[name], r.w_sem.at[weight_index(name)])

    def wait_weight(name):
        held_copy(own_w[name], name).wait()

    def first_send(name):
        k = weight_index(name)
        return remote(own_w[name], held_w[name], r.vs_sem.at[k], r.w_sem.at[k], other)

    def first_sends(*chosen):
        @pl.when(c == 0)
        def _():
            for name in chosen:
                first_send(name).start()

    def kept_send(name):
        k = weight_index(name)
        return remote(own_w[name], sib_w[name], r.ws_sem.at[k], r.wr_sem.at[k], other)

    def kept_sends(core):
        @pl.when(c == core)
        def _():
            for name in WEIGHTS:
                kept_send(name).start()

    def load_weight(name, s):
        @pl.when(c == s)
        def _():
            held_copy(own_w[name], name).start()

        @pl.when(c != s)
        def _():
            kept_send(name).wait_recv()
            held_copy(sib_w[name], name).start()

    @pl.when(c == 0)
    def _():
        for name in WEIGHTS:
            held_copy(own_w[name], name).start()

    own_params = [
        pltpu.make_async_copy(r.in_norm, r.norm.at[c], r.p_sem.at[0]),
        pltpu.make_async_copy(r.in_bias, r.bias.at[c], r.p_sem.at[1]),
    ]
    for copy in own_params:
        copy.start()

    r.grid[...] = jnp.zeros(r.grid.shape, F32)
    load_frames.wait()
    stage_to_v(0)

    pl.semaphore_wait(barrier, 2 * n - 1)

    first_sends("red")
    param_sends = [
        remote(r.in_norm, r.norm.at[c], r.ps_sem.at[0], r.pr_sem.at[0], other),
        remote(r.in_bias, r.bias.at[c], r.ps_sem.at[1], r.pr_sem.at[1], other),
    ]
    for copy in param_sends:
        copy.start()
    kept_sends(1)

    msg, inbox = r.msg, r.inbox

    def peer_of(level, k):
        size, stride = levels[level]
        here = lax.rem(lax.div(i, stride), size)
        return (c, i + (lax.rem(here + k, size) - here) * stride)

    def copies_of(bank, level):
        size, _ = levels[level]
        return [
            remote(
                msg.at[bank, level],
                inbox.at[bank, level, k],
                r.ms_sem.at[bank, level, k],
                r.mr_sem.at[bank, level, k],
                peer_of(level, k),
            )
            for k in range(1, size)
        ]

    def exchange_start(bank):
        for copy in copies_of(bank, 0):
            copy.start()

    def routed(core):
        size = levels[0][0]
        return [k for k in range(1, size) if (k % side == 0) == (core == 0)]

    def hand_over(bank):
        return remote(
            msg.at[bank, 0], r.relay.at[bank], r.hs_sem.at[bank], r.hr_sem.at[bank], other
        )

    def passed_on(bank, k):
        core, peer = peer_of(0, k)
        return remote(
            r.relay.at[bank],
            inbox.at[bank, 0, k],
            r.fs_sem.at[bank, k],
            r.mr_sem.at[bank, 0, k],
            (1 - core, peer),
        )

    def relay_start(bank):
        hand_over(bank).start()
        copies = copies_of(bank, 0)
        for core in range(2):

            @pl.when(c == core)
            def _():
                for k in routed(core):
                    copies[k - 1].start()

    def relay_pass(bank):
        hand_over(bank).wait_recv()
        for core in range(2):

            @pl.when(c == core)
            def _():
                for k in routed(core):
                    passed_on(bank, k).start()

    def exchange_finish(bank, combine, relayed=False):
        for level in range(len(levels)):
            copies = copies_of(bank, level)
            if level:
                for copy in copies:
                    copy.start()
            for copy in copies:
                copy.wait_recv()
            result = combine(bank, level)
            if level == 0 and relayed:
                hand_over(bank).wait_send()
                for core in range(2):

                    @pl.when(c == core)
                    def _():
                        for k in routed(core):
                            copies[k - 1].wait_send()
                            passed_on(bank, k).wait_send()
            else:
                for copy in copies:
                    copy.wait_send()
            if level + 1 < len(levels):
                msg[bank, level + 1] = result
        return result

    cnt = r.cnt

    def count_copies(level):
        size, _ = levels[level]
        return [
            remote(
                cnt.at[level, 0],
                cnt.at[level, k],
                r.cs_sem.at[level, k],
                r.cr_sem.at[level, k],
                peer_of(level, k),
            )
            for k in range(1, size)
        ]

    cnt[0, 0] = jnp.full((8, LANES), pixels_own, F32)
    for copy in count_copies(0):
        copy.start()

    def count_finish():
        for level in range(len(levels)):
            copies = count_copies(level)
            if level:
                for copy in copies:
                    copy.start()
            total = cnt[level, 0]
            for k, copy in enumerate(copies):
                copy.wait()
                total = total + cnt[level, k + 1]
            if level + 1 < len(levels):
                cnt[level + 1, 0] = total
        r.total[...] = total

    def sum_combine(bank, level):
        total = msg[bank, level]
        for k in range(1, levels[level][0]):
            total = total + inbox[bank, level, k]
        return total

    def moment_combine(bank, level):
        size, _ = levels[level]
        nt = GROUP
        items = [msg[bank, level]] + [inbox[bank, level, k] for k in range(1, size)]
        counts = [cnt[level, k, 0:1, :] for k in range(size)]
        total = items[0][0:nt]
        count = counts[0]
        for k in range(1, size):
            total = total + items[k][0:nt]
            count = count + counts[k]
        mean = total / count
        spread = jnp.zeros_like(total)
        for k in range(size):
            gap = items[k][0:nt] / counts[k] - mean
            spread = spread + items[k][nt : 2 * nt] + counts[k] * gap * gap
        return jnp.concatenate([total, spread], axis=0)

    def moments(values):
        origin = values[0, 0:1, :]
        gaps = values - origin
        first = jnp.sum(valid * jnp.sum(gaps, axis=0), axis=0, keepdims=True)
        second = jnp.sum(valid * jnp.sum(gaps * gaps, axis=0), axis=0, keepdims=True)
        mean_gap = first / pixels_own
        return first + pixels_own * origin, second - first * mean_gap

    def norm_send(ref, block, bank):
        def body(j):
            total, spread = moments(cube(ref[view(block * GROUP + j)]))
            msg[bank, 0, pl.ds(j, 1), :] = total
            msg[bank, 0, pl.ds(GROUP + j, 1), :] = spread

        loop(GROUP, body)
        exchange_start(bank)

    def norm_receive(bank, s, block, row0):
        result = exchange_finish(bank, moment_combine)
        everyone = r.total[0:1, :]
        at = block * GROUP
        r.mean[at : at + GROUP, :] = result[0:GROUP] / everyone
        r.rstd[s, row0 + at : row0 + at + GROUP, :] = lax.rsqrt(
            result[GROUP : 2 * GROUP] / everyone + EPSILON
        )

    def gain_of(s, offset, j):
        lanes = pl.ds(pl.multiple_of(offset + j * LANES, LANES), LANES)
        return (r.norm[s, 0:1, lanes], r.norm[s, 1:2, lanes])

    def row_of(ref, j):
        return ref[pl.ds(j, 1), :]

    grid = r.grid

    def to_grid(values, lanes):
        for h in range(SIDE):
            at = ((h + 1) * GRID + 1) * segs
            grid[at : at + SIDE * segs, lanes] = values[h * SIDE * segs : (h + 1) * SIDE * segs]

    def patches(target, width, flip):
        def body(j):
            lanes = tile(j)
            for tap in range(9):
                down, right = tap // 3, tap % 3
                if flip:
                    down, right = 2 - down, 2 - right
                pieces = []
                for h in range(SIDE):
                    at = ((h + down) * GRID + right) * segs
                    pieces.append(grid[at : at + SIDE * segs, lanes])
                target[:, pl.ds(pl.multiple_of(tap * width + j * LANES, LANES), LANES)] = packed(
                    jnp.concatenate(pieces, axis=0)
                )

        loop(width // LANES, body)

    def put(slot, target, kind, s):
        @pl.when(c == s)
        def _():
            pltpu.make_async_copy(stage.at[slot], target.at[c], r.o_sem.at[kind, 0]).start()

        @pl.when(c != s)
        def _():
            remote(
                stage.at[slot],
                target.at[c],
                r.o_sem.at[kind, 1],
                r.o_sem.at[kind, 2],
                other,
            ).start()

    def put_wait(slot, target, kind, s):
        @pl.when(c == s)
        def _():
            pltpu.make_async_copy(stage.at[slot], target.at[c], r.o_sem.at[kind, 0]).wait()

        @pl.when(c != s)
        def _():
            remote(
                stage.at[slot],
                target.at[c],
                r.o_sem.at[kind, 1],
                r.o_sem.at[kind, 2],
                other,
            ).wait_send()

    n_mid = mid // LANES
    n_ch = ch // LANES
    n_blocks = ch // ROW

    for copy in own_params:
        copy.wait()
    for s in range(2):
        nh1, nh2, nh3 = r.nh1.at[s], r.nh2.at[s], r.nh3.at[s]
        wait_weight("red")
        nh1[...] = dot(v[...], r.red[...])
        if s == 0:
            first_sends("spa", *SMALL)
            load_weight("red", 1)
        else:
            kept_sends(0)
        norm_send(nh1, 0, 0)
        if s == 0:
            for copy in param_sends:
                copy.wait_recv()
            count_finish()
        norm_receive(0, s, 0, 0)

        def act_one(j, s=s, nh1=nh1):
            gain, offset = gain_of(s, 0, j)
            normed = (nh1[view(j)] - row_of(r.mean, j)) * row_of(r.rstd.at[s], j)
            nh1[view(j)] = normed
            before = normed * gain + offset
            act = before * sigmoid(before)
            r.a1[s, :, tile(j)] = packed(act)
            to_grid(act, tile(j))

        loop(n_mid, act_one)
        patches(r.patch, mid, False)
        wait_weight("spa")
        nh2[...] = dot(r.patch[...], r.spa[...])
        if s == 0:
            first_sends("exp")
            load_weight("spa", 1)
        norm_send(nh2, 0, 1)
        norm_receive(1, s, 0, n_mid)

        def act_two(j, s=s, nh2=nh2):
            gain, offset = gain_of(s, mid, j)
            normed = (nh2[view(j)] - row_of(r.mean, j)) * row_of(r.rstd.at[s], n_mid + j)
            nh2[view(j)] = normed
            before = normed * gain + offset
            r.h2[s, :, tile(j)] = packed(before * sigmoid(before))

        loop(n_mid, act_two)
        for name in SMALL:
            wait_weight(name)
        squeezed = cube(dot(r.h2[s], r.squ[...])[:rows])
        later = pltpu.roll(squeezed, segs - 1, 1)
        field = (paired * (later - squeezed)).reshape(rows, red_w)
        r.field[s] = packed(field)
        rounded = r.field[s].astype(F32)[:rows]
        to_grid(rounded, pl.ds(0, LANES))
        patches(r.patch_m, red_w, False)
        context_mean = jnp.sum(cube(rounded), axis=0) * (1.0 / PIX)
        r.cmean[s] = context_mean
        from_mean = jnp.dot(
            context_mean, r.con[...].astype(F32), precision=HIGH, preferred_element_type=F32
        )
        mixed = cube(dot(r.patch_m[...], r.mot[...])[:rows]) + from_mean
        r.score[s] = packed(mixed)
        free[0:full, :] = dot(r.score[s], r.gat[...])

        def gate(j, s=s):
            bias = r.bias[s, 0:1, tile(j)]
            sigma = sigmoid(free[view(j)] + bias)
            r.sigma[s, :, tile(j)] = packed(sigma)
            h2 = r.h2[s, :, tile(j)].astype(F32)[:rows]
            r.gated[s, :, tile(j)] = packed(h2 * (0.5 + sigma))

        loop(n_mid, gate)
        if s == 0:
            for name in SMALL:
                load_weight(name, 1)
        wait_weight("exp")
        for block in range(n_blocks):
            nh3[block * full : (block + 1) * full, :] = dot(
                r.gated[s], r.exp[:, block * ROW : (block + 1) * ROW]
            )
            norm_send(nh3, block, 2 + block)
        if s == 0:
            load_weight("exp", 1)
        slot = 1 - s

        def finish(j, s=s, nh3=nh3, slot=slot):
            gain, offset = gain_of(s, 2 * mid, j)
            normed = (nh3[view(j)] - row_of(r.mean, j)) * row_of(
                r.rstd.at[s], 2 * n_mid + j
            )
            nh3[view(j)] = normed
            before = v[:, tile(j)].astype(F32)[:rows] + normed * gain + offset
            out = cube(before * sigmoid(before)) * valid
            stage[slot, :, :, tile(j)] = out.astype(BF)
            if s == 0:
                v[:, tile(j)] = packed(out)

        for block in range(n_blocks):
            norm_receive(2 + block, s, block, 2 * n_mid)
            loop(GROUP, lambda j, block=block: finish(block * GROUP + j))
        put(slot, r.out, s, s)
        if s == 0:
            put_wait(slot, r.out, 0, 0)
            load_grad = pltpu.make_async_copy(r.out_grad.at[c], stage.at[1], r.load_sem.at[1])
            load_grad.start()

    def send_sem(chunk, k):
        return r.rs_send.at[CHUNKS.index(chunk), k]

    def recv_sem(chunk, k):
        return r.rs_recv.at[CHUNKS.index(chunk), k]

    def add_loop(target, others, pieces):
        def body(j):
            at = target.at[j]
            total = at[...]
            for item in others:
                total = total + item.at[j][...]
            at[...] = total

        loop(pieces, body)

    def along(to):
        px = to * (1 - c) + x * c
        py = y * (1 - c) + to * c
        return z * side * side + py * side + px

    def rs0(chunk):
        ref = chunk_refs[chunk]
        found = []
        for k in range(1, side):
            sems = (send_sem(chunk, k), recv_sem(chunk, k))
            source = ref.g.at[1 - c, lax.rem(gc + k, side)]
            found.append(remote(source, ref.far.at[k - 1], *sems, other))
        sems = (send_sem(chunk, 0), recv_sem(chunk, 0))
        return found, remote(ref.g.at[c, fc], ref.near, *sems, other)

    def rs1(chunk):
        ref = chunk_refs[chunk]
        found = []
        for k in range(1, side):
            at = side - 1 + k
            sems = (send_sem(chunk, at), recv_sem(chunk, at))
            device = (1 - c, along(lax.rem(fc + k, side)))
            found.append(remote(ref.far.at[k - 1], ref.r1.at[k - 1], *sems, device))
        return found

    def rs2(chunk):
        ref = chunk_refs[chunk]
        found = []
        for k in range(1, side):
            to = lax.rem(fc + k, side)
            at = 2 * (side - 1) + k
            sems = (send_sem(chunk, at), recv_sem(chunk, at))
            found.append(remote(ref.near.at[to], ref.r2.at[k - 1], *sems, (c, along(to))))
        return found

    def rs3(chunk):
        ref = chunk_refs[chunk]
        found = []
        for k in range(1, depth):
            to = lax.rem(z + k, depth)
            at = 3 * (side - 1) + k
            sems = (send_sem(chunk, at), recv_sem(chunk, at))
            source = ref.near.at[fc, lax.rem(to, slots)]
            device = (c, to * side * side + y * side + x)
            found.append((to, remote(source, ref.r3.at[k - 1], *sems, device)))
        return found

    def credit(chunk):
        return r.credit.at[CHUNKS.index(chunk)]

    def rs0_start(chunk, s):
        if s == 0:
            pl.semaphore_wait(credit(chunk), 1)
        far, near = rs0(chunk)
        for copy in far:
            copy.start()
        near.start()

    def rs1_start(chunk):
        ref = chunk_refs[chunk]
        far, near = rs0(chunk)
        for k, copy in enumerate(far):
            copy.wait()
            to = lax.rem(fc + k + 1, side)
            for b in range(side):
                add_loop(ref.far.at[k, b], [ref.g.at[c, to, b]], slots)
        for copy in rs1(chunk):
            copy.start()
        near.wait()
        for b in range(side):
            add_loop(ref.near.at[b], [ref.g.at[1 - c, gc, b]], slots)

    def rs2_start(chunk):
        ref = chunk_refs[chunk]
        copies = rs1(chunk)
        for copy in copies:
            copy.wait_recv()
        for b in range(side):
            add_loop(ref.near.at[b], [ref.r1.at[k, b] for k in range(side - 1)], slots)
        for copy in copies:
            copy.wait_send()
        for copy in rs2(chunk):
            copy.start()

    def rs3_start(chunk):
        ref = chunk_refs[chunk]
        copies = rs2(chunk)
        for copy in copies:
            copy.wait_recv()
        add_loop(ref.near.at[fc], [ref.r2.at[k] for k in range(side - 1)], slots)
        for copy in copies:
            copy.wait_send()
        for to, copy in rs3(chunk):
            if slots == depth:
                copy.start()
            else:
                pl.when(to < slots)(copy.start)

    def owners(comp):
        start, size = parts[comp]
        at = start + size * i
        first = lax.div(at * ROW, share)
        last = lax.div(jnp.minimum((at + size) * ROW, pp.total) - 1, share)
        exists = jnp.logical_and(i < PIECES, at * ROW < pp.total)
        return at, first, last, exists

    def send_piece(comp, s, action):
        _, size = parts[comp]
        at, first, last, exists = owners(comp)
        which = COMPS.index(comp)
        for k in range(pp.reach):
            to = first + k
            base = lax.div(to * share, ROW * 16) * 16
            row = pl.multiple_of(pp.margin + at - base, 16)
            there = r.land.at[pl.ds(row, size), pl.ds(pl.multiple_of((1 - c) * HALF, HALF), HALF)]
            needed = jnp.logical_and(exists, to <= last)
            here = jnp.logical_and(c == s, to == i)
            source = fin[comp]
            arrival = r.land_sem.at[which, c, lax.rem(i, PIECES)]

            @pl.when(jnp.logical_and(needed, here))
            def _():
                copy = pltpu.make_async_copy(source, there, arrival)
                if action == "start":
                    copy.start()
                else:
                    copy.wait()

            @pl.when(jnp.logical_and(needed, jnp.logical_not(here)))
            def _():
                copy = remote(source, there, r.fin_sem.at[which, k], arrival, (s, to))
                if action == "start":
                    copy.start()
                else:
                    copy.wait_send()

    def finish_chunk(chunk, s):
        ref = chunk_refs[chunk]
        own = ref.near.at[fc]
        r3 = ref.r3
        copies = rs3(chunk)
        cins = mid // PIECES
        if s == 0:
            finish_sent(chunk, 1)

        def work():
            for _, copy in copies:
                copy.wait_recv()
            mine = own.at[lax.rem(z, slots)]

            def summed(first, count):
                total = mine[first : first + count, :].astype(F32)
                for k in range(depth - 1):
                    total = total + r3[k, first : first + count, :].astype(F32)
                return total

            def weave(mix, first, count, stride, value):
                for k in range(HALF // LANES):
                    mix[k, pl.ds(first, count, stride=stride), :] = value[
                        :, k * LANES : (k + 1) * LANES
                    ]

            def woven(mix, target, size):
                for k in range(HALF // LANES):
                    target[:, k * LANES : (k + 1) * LANES] = mix[k, 0:size, :].astype(BF)

            if chunk == "e":
                size = parts["exp"][1]
                quarters = size // cins
                for q in range(quarters):
                    weave(r.mix_e, q, cins, quarters, summed(q * cins, cins))
                woven(r.mix_e, r.fin_exp, size)
            elif chunk == "m":
                for tap in range(SPLIT):
                    weave(r.mix, tap, cins, 9, summed(tap * cins, cins))
            elif chunk == "t":
                for tap in range(SPLIT, 9):
                    weave(r.mix, tap, cins, 9, summed((tap - SPLIT) * cins, cins))
                woven(r.mix, r.fin_spa, parts["spa"][1])
                r.fin_small[...] = summed((9 - SPLIT) * cins, parts["small"][1]).astype(BF)
            else:
                r.fin_red[...] = summed(0, parts["red"][1]).astype(BF)

        if slots == depth:
            work()
        else:
            pl.when(z < slots)(work)
        for to, copy in copies:
            if slots == depth:
                copy.wait_send()
            else:
                pl.when(to < slots)(copy.wait_send)
        if s == 1:
            pl.semaphore_signal(credit(chunk), inc=1, device_id=other, device_id_type=MESH)
        for comp in HOLDS[chunk]:
            send_piece(comp, s, "start")

    def finish_sent(chunk, s):
        for comp in HOLDS[chunk]:
            send_piece(comp, s, "wait")

    def place(half, piece):
        px, py, pz = piece % side, (piece // side) % side, piece // (side * side)
        return (half, px, py, pz) if half == 0 else (half, py, px, pz)

    small_at = 2 * full

    def grads_e(s):
        cins = mid // PIECES
        g = r.g_e
        for q in range(ch // ROW):
            for half in range(2):
                lanes = slice(q * ROW + half * HALF, q * ROW + (half + 1) * HALF)
                value = dot_tn(r.gated[s], r.gz3[:, lanes]).astype(BF)
                for piece in range(PIECES):
                    where = place(half, piece)
                    g[where + (slice(q * cins, (q + 1) * cins),)] = value[
                        piece * cins : (piece + 1) * cins
                    ]

    def grads_small(s):
        g = r.g_t
        tmp = r.tmp1
        at = small_at
        per = ROW // LANES

        def spread(count):
            for q in range(per):
                free[at : at + count, q * LANES : (q + 1) * LANES] = tmp[
                    pl.ds(q, count, stride=per), :
                ]

        tmp[0:mid, :] = dot_tn(r.h2[s], r.gr[...])
        spread(mid // per)
        at += mid // per
        moved = dot_tn(r.field[s], r.patch_m[...])
        for tap in range(9):
            tmp[pl.ds(tap, red_w, stride=9), :] = moved[:, tap * LANES : (tap + 1) * LANES]
        spread(9 * red_w // per)
        at += 9 * red_w // per
        tmp[0:red_w, :] = lax.dot_general(
            r.cmean[s],
            r.ssum[...],
            (((0,), (0,)), ((), ())),
            precision=HIGH,
            preferred_element_type=F32,
        )
        spread(red_w // per)
        at += red_w // per
        free[at : at + red_w, :] = dot_tn(r.score[s], r.gl[...])
        at += red_w
        free[at : at + 8, :] = jnp.broadcast_to(r.gbias[...], (8, mid))
        start = (9 - SPLIT) * (mid // PIECES)
        size = parts["small"][1]
        used = -(-pp.small_rows // size)
        for piece in range(PIECES):
            for half in range(2):
                where = place(half, piece) + (slice(start, start + size),)
                if piece < used:
                    g[where] = free[
                        small_at + piece * size : small_at + (piece + 1) * size,
                        half * HALF : (half + 1) * HALF,
                    ].astype(BF)
                else:
                    g[where] = jnp.zeros((size, HALF), BF)

    def grads_taps(s, g, first, count):
        cins = mid // PIECES

        def body(tap):
            for half in range(2):
                lanes = pl.ds(pl.multiple_of((first + tap) * mid + half * HALF, HALF), HALF)
                value = dot_tn(r.a1[s], r.patch[:, lanes]).astype(BF)
                for piece in range(PIECES):
                    where = place(half, piece)
                    g[where + (pl.ds(pl.multiple_of(tap * cins, cins), cins),)] = value[
                        piece * cins : (piece + 1) * cins
                    ]

        loop(count, body)

    def grads_c(s):
        g = r.g_c
        size = parts["red"][1]
        for half in range(2):
            value = dot_tn(v[...], r.gz1[:, half * HALF : (half + 1) * HALF]).astype(BF)
            for piece in range(PIECES):
                g[place(half, piece)] = value[piece * size : (piece + 1) * size]

    def back_receive(bank, s, block, row0, relayed=True):
        result = exchange_finish(bank, sum_combine, relayed)
        half_rows = 2 * n_mid + n_ch
        at = row0 + block * GROUP
        r.gnorm[s, at : at + GROUP, :] = result[GROUP : 2 * GROUP]
        r.gnorm[s, half_rows + at : half_rows + at + GROUP, :] = result[0:GROUP]
        r.bsum[block] = result / r.total[0:1, :]

    def norm_grad(grad, normed, s, offset, row0, j):
        gain, _ = gain_of(s, offset, j)
        scale = gain * row_of(r.rstd.at[s], row0 + j)
        means = r.bsum.at[lax.div(j, GROUP)]
        mean_grad = row_of(means, lax.rem(j, GROUP))
        mean_cross = row_of(means, GROUP + lax.rem(j, GROUP))
        return scale * (cube(grad) - valid * (mean_grad + cube(normed) * mean_cross))

    def slope_send(s, grad_at, normed_ref, offset, bank):
        def body(j):
            gain, shift = gain_of(s, offset, j)
            normed = normed_ref[view(j)]
            grad = free[view(j, grad_at)] * silu_slope(normed * gain + shift)
            free[view(j, grad_at)] = grad
            msg[bank, 0, pl.ds(j, 1), :] = fold(cube(grad))
            msg[bank, 0, pl.ds(GROUP + j, 1), :] = fold(cube(grad * normed))

        loop(GROUP, body)
        relay_start(bank)
        relay_pass(bank)

    gs = r.gs
    for s in (1, 0):
        nh1, nh2, nh3 = r.nh1.at[s], r.nh2.at[s], r.nh3.at[s]
        slot = s
        bank0 = 2 + n_blocks * s
        if s == 1:
            load_grad.wait()

        def back_three(j, block, s=s, nh3=nh3, slot=slot, bank0=bank0):
            at = block * GROUP + j
            gain, shift = gain_of(s, 2 * mid, at)
            normed = nh3[view(at)]
            before = v[:, tile(at)].astype(F32)[:rows] + normed * gain + shift
            grad = cube(silu_slope(before)) * valid * stage[slot, :, :, tile(at)].astype(F32)
            gs[view(at)] = grad.reshape(rows, LANES)
            msg[bank0 + block, 0, pl.ds(j, 1), :] = fold(grad)
            msg[bank0 + block, 0, pl.ds(GROUP + j, 1), :] = fold(grad * cube(normed))

        for block in range(n_blocks):
            loop(GROUP, functools.partial(back_three, block=block))
            if s == 1:
                exchange_start(bank0 + block)
                continue
            relay_start(bank0 + block)
            if block:
                relay_pass(bank0 + block - 1)
        if s == 0:
            relay_pass(bank0 + n_blocks - 1)
        if s == 0:
            finish_chunk("e", 1)

        def grad_three(j, s=s, nh3=nh3):
            r.gz3[:, tile(j)] = packed(
                norm_grad(gs[view(j)], nh3[view(j)], s, 2 * mid, 2 * n_mid, j)
            )

        for block in range(n_blocks):
            back_receive(bank0 + block, s, block, 2 * n_mid, s == 0)
            loop(GROUP, lambda j, block=block: grad_three(block * GROUP + j))
        grads_e(s)
        rs0_start("e", s)
        if s == 0:
            rs3_start("m")
            rs2_start("t")
            wait_weight("exp")
        free[0:full, :] = dot_nt(r.gz3[...], r.exp[...])
        if s == 1:
            load_weight("exp", 0)

        def back_gate(j, s=s):
            grad = free[view(j)]
            sigma = r.sigma[s, :, tile(j)].astype(F32)[:rows]
            h2 = r.h2[s, :, tile(j)].astype(F32)[:rows]
            free[view(j, full)] = grad * (0.5 + sigma)
            value = packed(grad * h2 * sigma * (1.0 - sigma))
            r.gl[:, tile(j)] = value
            r.gbias[0:1, tile(j)] = fold(cube(value.astype(F32)[:rows]))

        loop(n_mid, back_gate)
        rs1_start("e")
        if s == 0:
            for name in SMALL:
                wait_weight(name)
        r.gq[...] = dot_nt(r.gl[...], r.gat[...]).astype(BF)
        rounded = r.gq[...].astype(F32)[:rows]
        to_grid(rounded, pl.ds(0, LANES))
        patches(r.patch_m, red_w, True)
        score_sums = jnp.sum(cube(rounded), axis=0)
        r.ssum[...] = score_sums
        grad_field = None
        for tap in range(9):
            part = dot_nt(
                r.patch_m[:, tap * red_w : (tap + 1) * red_w],
                r.mot[tap * red_w : (tap + 1) * red_w, :],
            )
            grad_field = part if grad_field is None else grad_field + part
        from_mean = lax.dot_general(
            score_sums,
            r.con[...].astype(F32),
            (((1,), (1,)), ((), ())),
            precision=HIGH,
            preferred_element_type=F32,
        ) * (1.0 / PIX)
        weighted = paired * (cube(grad_field[:rows]) + from_mean)
        r.gr[...] = packed(pltpu.roll(weighted, 1, 1) - weighted)
        free[full : 2 * full, :] += dot_nt(r.gr[...], r.squ[...])
        if s == 1:
            for name in SMALL:
                load_weight(name, 0)
        slope_send(s, full, nh2, mid, 1)
        grads_small(s)
        if s == 0:
            finish_chunk("m", 1)
            rs2_start("c")
            rs3_start("t")
        back_receive(1, s, 0, n_mid)

        def grad_two(j, s=s, nh2=nh2):
            value = norm_grad(free[view(j, full)], nh2[view(j)], s, mid, n_mid, j)
            to_grid(value.reshape(rows, LANES), tile(j))

        loop(n_mid, grad_two)
        patches(r.patch, mid, True)
        grads_taps(s, r.g_m, 0, SPLIT)
        rs0_start("m", s)
        if s == 0:
            wait_weight("spa")
        acc = None
        for tap in range(9):
            part = dot_nt(
                r.patch[:, tap * mid : (tap + 1) * mid], r.spa[tap * mid : (tap + 1) * mid, :]
            )
            acc = part if acc is None else acc + part
        free[0:full, :] = acc
        if s == 1:
            load_weight("spa", 0)
        rs1_start("m")
        slope_send(s, 0, nh1, 0, 0)
        grads_taps(s, r.g_t, SPLIT, 9 - SPLIT)
        if s == 0:
            finish_chunk("t", 1)
            rs3_start("c")
        rs0_start("t", s)
        rs2_start("e")
        back_receive(0, s, 0, 0)

        def grad_one(j, s=s, nh1=nh1):
            r.gz1[:, tile(j)] = packed(norm_grad(free[view(j)], nh1[view(j)], s, 0, 0, j))

        loop(n_mid, grad_one)
        rs1_start("t")
        grads_c(s)
        if s == 0:
            finish_chunk("c", 1)
        rs0_start("c", s)
        rs3_start("e")
        if s == 1:
            put_wait(0, r.out, 1, 1)
            reload = pltpu.make_async_copy(r.frames.at[c], stage.at[1], r.load_sem.at[0])
            reload.start()
        else:
            wait_weight("red")
        slot = 1 - s
        for block in range(n_blocks):
            value = gs[block * full : block * full + rows, :] + dot_nt(
                r.gz1[...], r.red[block * ROW : (block + 1) * ROW, :]
            )[:rows]
            stage[slot, :, :, block * ROW : (block + 1) * ROW] = cube(value).astype(BF)
        put(slot, r.ing, 2 + s, s)
        rs1_start("c")
        if s == 1:
            load_weight("red", 0)
            reload.wait()
            stage_to_v(1)
        rs2_start("m")

    gn_send = remote(
        r.gnorm.at[1 - c], r.gnorm_in, r.gn_sem.at[0], r.gn_sem.at[1], other
    )
    gn_send.start()
    finish_chunk("e", 0)
    rs3_start("m")
    rs2_start("t")
    rs2_start("c")
    rs3_start("t")
    finish_chunk("m", 0)
    rs3_start("c")
    finish_chunk("t", 0)
    finish_chunk("c", 0)
    gn_send.wait()
    r.gnorm_out[...] = r.gnorm[c] + r.gnorm_in[...]

    for copy in param_sends:
        copy.wait_send()
    for name in WEIGHTS:
        kept_send(name).wait_send()

    @pl.when(c == 0)
    def _():
        for name in WEIGHTS:
            first_send(name).wait_send()

    put_wait(0, r.ing, 3, 1)
    put_wait(1, r.ing, 2, 0)
    for base, target in ((0, r.out), (2, r.ing)):
        for s in range(2):

            @pl.when(c == s)
            def _():
                remote(
                    stage.at[0],
                    target.at[1 - c],
                    r.o_sem.at[base + s, 1],
                    r.o_sem.at[base + s, 2],
                    other,
                ).wait_recv()

    for chunk in CHUNKS:
        finish_sent(chunk, 0)
    low = i * share
    high = low + share
    for which, comp in enumerate(COMPS):
        start, size = parts[comp]

        def arrive(piece, _):
            first = (start + size * piece) * ROW
            last = jnp.minimum(first + size * ROW, pp.total)

            @pl.when(jnp.logical_and(first < high, last > low))
            def _():
                for core in range(2):
                    own = jnp.logical_and(c == core, i == piece)

                    @pl.when(jnp.logical_not(own))
                    def _():
                        pltpu.make_async_copy(
                            fin[comp],
                            r.land.at[pl.ds(0, size), pl.ds(0, HALF)],
                            r.land_sem.at[which, core, piece],
                        ).wait()

            return 0

        lax.fori_loop(0, PIECES, arrive, 0)


def run(n, sizes, frames, out_grad, seg_counts, weights, bias, norm):
    ch, mid, red_w, segs, share = sizes
    pp = plan(n, ch, mid, red_w, segs, share)
    side, depth, slots, levels, parts = pp.side, pp.depth, pp.slots, pp.levels, pp.parts
    rows = PIX * segs
    full = up(rows, 16)
    norm_rows = 2 * (2 * mid + ch) // LANES
    group = max(size for size, _ in levels)
    any_spec = pl.BlockSpec(memory_space=pl.ANY)
    vmem_spec = pl.BlockSpec(memory_space=pltpu.VMEM)

    ins = dict(
        frames=frames,
        out_grad=out_grad,
        in_red=weights.red,
        in_spa=weights.spa,
        in_exp=weights.exp,
        in_squ=weights.squ,
        in_mot=weights.mot,
        in_con=weights.con,
        in_gat=weights.gat,
        counts=seg_counts,
        in_bias=bias,
        in_norm=norm,
    )
    in_specs = [any_spec] * 9 + [pl.BlockSpec(memory_space=pltpu.SMEM), any_spec, any_spec]

    def like(item):
        return jax.ShapeDtypeStruct(item.shape, item.dtype)

    outs = dict(
        out=like(frames),
        ing=like(frames),
        land=jax.ShapeDtypeStruct((pp.land, ROW), BF),
        sib_red=like(weights.red),
        sib_spa=like(weights.spa),
        sib_exp=like(weights.exp),
        sib_squ=like(weights.squ),
        sib_mot=like(weights.mot),
        sib_con=like(weights.con),
        sib_gat=like(weights.gat),
        gnorm_out=jax.ShapeDtypeStruct((norm_rows, LANES), F32),
    )
    out_specs = [any_spec] * 10 + [vmem_spec]

    def low(*dims):
        return pltpu.VMEM(dims, BF)

    def wide(*dims):
        return pltpu.VMEM(dims, F32)

    def sems(*dims):
        return pltpu.SemaphoreType.DMA(dims)

    def piled(size):
        return (
            low(2, side, side, slots, size, HALF),
            low(max(side - 1, 1), side, slots, size, HALF),
            low(side, slots, size, HALF),
            low(max(side - 1, 1), side, slots, size, HALF),
            low(max(side - 1, 1), slots, size, HALF),
            low(max(depth - 1, 1), size, HALF),
        )

    cins = mid // PIECES
    pile_e = piled(parts["exp"][1])
    pile_m = piled(SPLIT * cins)
    pile_t = piled((9 - SPLIT) * cins + parts["small"][1])
    pile_c = piled(parts["red"][1])
    hops = 3 * (side - 1) + depth
    banks = 2 + 2 * (ch // ROW)
    scratch = dict(
        red=low(*weights.red.shape),
        spa=low(*weights.spa.shape),
        exp=low(*weights.exp.shape),
        squ=low(*weights.squ.shape),
        mot=low(*weights.mot.shape),
        con=low(*weights.con.shape),
        gat=low(*weights.gat.shape),
        bias=wide(2, *bias.shape),
        norm=wide(2, *norm.shape),
        stage=low(2, *frames.shape[1:]),
        v=low(full, ch),
        nh1=wide(2, full, mid),
        nh2=wide(2, full, mid),
        nh3=wide(2, full * ch // ROW, ROW),
        gs=wide(full * ch // ROW, ROW),
        sigma=low(2, full, mid),
        a1=low(2, full, mid),
        h2=low(2, full, mid),
        gated=low(2, full, mid),
        field=low(2, full, red_w),
        score=low(2, full, red_w),
        cmean=wide(2, segs, red_w),
        ssum=wide(segs, red_w),
        gbias=wide(1, mid),
        gz3=low(full, ch),
        gz1=low(full, mid),
        gl=low(full, mid),
        gq=low(full, red_w),
        gr=low(full, red_w),
        patch=low(full, 9 * mid),
        patch_m=low(full, 9 * red_w),
        grid=wide(GRID * GRID * segs, mid),
        tmp1=wide(9 * red_w, LANES),
        mix=wide(HALF // LANES, parts["spa"][1], LANES),
        mix_e=wide(HALF // LANES, parts["exp"][1], LANES),
        msg=wide(banks, len(levels), 2 * GROUP, LANES),
        inbox=wide(banks, len(levels), group, 2 * GROUP, LANES),
        cnt=wide(len(levels), group, 8, LANES),
        relay=wide(banks, 2 * GROUP, LANES),
        total=wide(8, LANES),
        mean=wide(ch // LANES, LANES),
        bsum=wide(ch // ROW, 2 * GROUP, LANES),
        rstd=wide(2, norm_rows // 2, LANES),
        gnorm=wide(2, norm_rows, LANES),
        gnorm_in=wide(norm_rows, LANES),
        g_e=pile_e[0],
        far_e=pile_e[1],
        near_e=pile_e[2],
        r1_e=pile_e[3],
        r2_e=pile_e[4],
        r3_e=pile_e[5],
        g_m=pile_m[0],
        far_m=pile_m[1],
        near_m=pile_m[2],
        r1_m=pile_m[3],
        r2_m=pile_m[4],
        r3_m=pile_m[5],
        g_t=pile_t[0],
        far_t=pile_t[1],
        near_t=pile_t[2],
        r1_t=pile_t[3],
        r2_t=pile_t[4],
        r3_t=pile_t[5],
        g_c=pile_c[0],
        far_c=pile_c[1],
        near_c=pile_c[2],
        r1_c=pile_c[3],
        r2_c=pile_c[4],
        r3_c=pile_c[5],
        fin_red=low(parts["red"][1], HALF),
        fin_spa=low(parts["spa"][1], HALF),
        fin_exp=low(parts["exp"][1], HALF),
        fin_small=low(parts["small"][1], HALF),
        load_sem=sems(2),
        w_sem=sems(len(WEIGHTS)),
        vs_sem=sems(len(WEIGHTS)),
        ws_sem=sems(len(WEIGHTS)),
        wr_sem=sems(len(WEIGHTS)),
        p_sem=sems(2),
        ps_sem=sems(2),
        pr_sem=sems(2),
        ms_sem=sems(banks, len(levels), group),
        mr_sem=sems(banks, len(levels), group),
        cs_sem=sems(len(levels), group),
        hs_sem=sems(banks),
        hr_sem=sems(banks),
        fs_sem=sems(banks, group),
        cr_sem=sems(len(levels), group),
        o_sem=sems(4, 3),
        rs_send=sems(4, hops),
        rs_recv=sems(4, hops),
        fin_sem=sems(4, pp.reach),
        land_sem=sems(4, 2, PIECES),
        gn_sem=sems(2),
        credit=pltpu.SemaphoreType.REGULAR((4,)),
    )
    names = list(ins) + list(outs) + list(scratch)
    results = pl.pallas_call(
        functools.partial(kernel, n, sizes, names),
        out_shape=list(outs.values()),
        in_specs=in_specs,
        out_specs=out_specs,
        scratch_shapes=list(scratch.values()),
        cost_estimate=pl.CostEstimate(
            flops=22 * 10**9, bytes_accessed=10**8, transcendentals=10**7
        ),
        compiler_params=pltpu.CompilerParams(
            collective_id=0, has_side_effects=True, vmem_limit_bytes=64 * 2**20 - 2**17
        ),
    )(*ins.values())
    return results[0], results[1], results[2], results[-1]


def on_device(n, share, frames, out_grad, seg_counts, *params):
    reducer, spatial, expander, squeezer, motion, context, gating, bias, norm = params
    _, segs, pixels, ch = frames.shape
    mid, red_w = reducer.shape[-1], squeezer.shape[-1]
    sizes = (ch, mid, red_w, segs, share)
    weights = SimpleNamespace(
        red=reducer[0],
        spa=spatial[0].transpose(1, 0, 2).reshape(9 * mid, mid),
        exp=expander[0],
        squ=squeezer[0],
        mot=motion[0].transpose(1, 0, 2).reshape(9 * red_w, red_w),
        con=context[0],
        gat=gating[0],
    )
    out, ing, land, gnorm = run(
        n,
        sizes,
        frames.transpose(0, 2, 1, 3),
        out_grad.transpose(0, 2, 1, 3),
        seg_counts,
        weights,
        bias,
        norm[0],
    )
    margin = plan(n, ch, mid, red_w, segs, share).margin
    window = land[margin : land.shape[0] - margin].astype(F32).reshape(-1, LANES)
    start = lax.rem(lax.axis_index("dp") * share, ROW * 16)
    flat = lax.dynamic_slice(window.reshape(1, -1), (0, start), (1, share))
    return (
        out.transpose(0, 2, 1, 3)[None],
        ing.transpose(0, 2, 1, 3)[None],
        flat,
        gnorm.reshape(norm.shape),
    )


def solution(mesh):
    n = mesh.shape["dp"]

    def whole(*args):
        entries = sum(item.size // item.shape[0] for item in args[3:11])
        share = up(entries, n) // n
        body = jax.shard_map(
            functools.partial(on_device, n, share),
            mesh=mesh,
            in_specs=(
                P("dp", None, None, None),
                P("dp", None, None, None),
                P("dp"),
                P("pipe", None, None),
                P("pipe", None, None, None),
                P("pipe", None, None),
                P("pipe", None, None),
                P("pipe", None, None, None),
                P("pipe", None, None),
                P("pipe", None, None),
                P("pipe", None),
                P("pipe", None, None),
            ),
            out_specs=(
                P("pipe", "dp", None, None, None),
                P("pipe", "dp", None, None, None),
                P("pipe", "dp"),
                P("pipe", None, None),
            ),
            check_vma=False,
        )
        return body(*args)

    return whole
```

```python
import functools
from types import SimpleNamespace

import jax
import jax.numpy as jnp
from jax import lax
from jax.experimental import pallas as pl
from jax.experimental.pallas import tpu as pltpu
from jax.sharding import PartitionSpec as P

SIDE = 7
PIX = 49
MICRO = 2
PIECES = 16
EPSILON = 1e-05
HIGH = lax.Precision.HIGHEST
BF = jnp.bfloat16
F32 = jnp.float32
MESH = pl.DeviceIdType.MESH
LANES = 128
GROUP = 4
HALF = 256
ROW = 512
GRID = SIDE + 2
WEIGHTS = ("red", "spa", "exp", "squ", "mot", "con", "gat")
SMALL = ("squ", "mot", "con", "gat")
COMPS = ("red", "spa", "exp", "small")
CHUNKS = ("e", "c", "d")
TAPS = dict(m=(0, 5), t=(5, 9))
ROWS = dict(c=(0, 1), d=(1, 2))
CUTS = 2
OPENS = dict(e=("exp", "small"), c=("red",), m=("spa",))
CLOSES = dict(e=("exp", "small"), d=("red",), t=("spa",))
RELAYED = ()
ORDER = (
    "s01", "x01", "s11", "x11", "s21", "x21", "s31", "x31", "m01", "w01", "w11", "w21", "w31",
    "a1", "b1", "q1", "l21", "y21", "m11", "Gs1", "Ge1", "z21", "p1", "v1", "l11", "y11",
    "g1", "0e1", "1e1", "z11", "o1", "i1", "Gc1", "r1", "Gb1", "s00", "x00", "s10", "0c1",
    "x10", "s20", "x20", "s30", "x30", "3b1", "2e1", "w00", "w10", "w20", "w30", "0d1", "a0",
    "1c1", "b0", "q0", "l20", "y20", "3e1", "1d1", "Ge0", "4b1", "Gs0", "2c1", "z20", "p0",
    "g0", "v0", "4e1", "l10", "0e0", "y10", "3c1", "2d1", "1e0", "Gb0", "3d1", "3b0", "z10",
    "o0", "Gc0", "4c1", "4d1", "0c0", "0d0", "2e0", "1d0", "3e0", "1c0", "2d0", "2c0", "3d0",
    "3c0", "i0", "4e0", "4c0", "4d0", "4b0",
)


def sigmoid(values):
    return 0.5 * jnp.tanh(0.5 * values) + 0.5


def silu_slope(values):
    sigma = sigmoid(values)
    return sigma * (1.0 + values * (1.0 - sigma))


def dot(a, b):
    return jnp.dot(a, b, preferred_element_type=F32)


def dot_nt(a, b):
    return lax.dot_general(a, b, (((1,), (1,)), ((), ())), preferred_element_type=F32)


def dot_tn(a, b):
    return lax.dot_general(a, b, (((0,), (0,)), ((), ())), preferred_element_type=F32)


def up(value, step):
    return -(-value // step) * step


def plan(n, ch, mid, red, segs, share):
    side = 4 if n % 64 == 0 else 2 if n % 4 == 0 else 1
    depth = n // (side * side)
    slots = PIECES // (side * side)
    levels = [(n, 1)] if n <= 16 else [(side * side, 1), (depth, side * side)]
    rows = dict(red=ch * mid // ROW, spa=9 * mid * mid // ROW, exp=mid * ch // ROW)
    small = mid * red + 9 * red * red + red * red + red * mid + mid
    small_rows = up(small, ROW) // ROW
    grouped = side == 2
    spa_size = rows["spa"] // (2 * depth if grouped else PIECES)
    parts = dict(
        red=(0, rows["red"] // PIECES),
        spa=(rows["red"], spa_size),
        exp=(rows["red"] + rows["spa"], rows["exp"] // PIECES),
        small=(rows["red"] + rows["spa"] + rows["exp"], up(up(small_rows, PIECES) // PIECES, 16)),
    )
    total = (parts["small"][0] + small_rows) * ROW
    margin = max(size for _, size in parts.values())
    reach = 1
    for comp, (start, size) in parts.items():
        for piece in range(rows[comp] // size if comp in rows else PIECES):
            first = (start + size * piece) * ROW
            if first < total:
                last = min((start + size * (piece + 1)) * ROW, total) - 1
                reach = max(reach, last // share - first // share + 1)
    land = margin + up(share // ROW + 22, 16) + margin
    return SimpleNamespace(
        side=side,
        depth=depth,
        slots=slots,
        levels=levels,
        parts=parts,
        total=total,
        margin=margin,
        reach=reach,
        grouped=grouped,
        land=land,
        small_rows=small_rows,
    )


def chunk_names(n):
    grouped = n % 64 and n % 4 == 0
    return CHUNKS if grouped else CHUNKS + tuple(TAPS)


def kernel(n, sizes, names, *refs):
    r = SimpleNamespace(**dict(zip(names, refs)))
    rest = refs[len(names) :]
    chunks = chunk_names(n)
    piles = {chunk: rest[6 * k : 6 * k + 6] for k, chunk in enumerate(chunks)}
    own_w = dict(
        red=r.in_red, spa=r.in_spa, exp=r.in_exp, squ=r.in_squ, mot=r.in_mot, con=r.in_con, gat=r.in_gat
    )
    sib_w = dict(
        red=r.sib_red, spa=r.sib_spa, exp=r.sib_exp, squ=r.sib_squ, mot=r.sib_mot, con=r.sib_con, gat=r.sib_gat
    )
    held_w = dict(red=r.red, spa=r.spa, exp=r.exp, squ=r.squ, mot=r.mot, con=r.con, gat=r.gat)
    chunk_refs = {
        chunk: SimpleNamespace(g=part[0], far=part[1], near=part[2], r1=part[3], r2=part[4], r3=part[5])
        for chunk, part in piles.items()
    }
    fin = dict(red=r.fin_red, spa=r.fin_spa, exp=r.fin_exp, small=r.fin_small)
    ch, mid, red_w, segs, share = sizes
    pp = plan(n, ch, mid, red_w, segs, share)
    side, depth, slots, levels, parts = pp.side, pp.depth, pp.slots, pp.levels, pp.parts
    grouped = pp.grouped
    rows = PIX * segs
    full = up(rows, 16)
    pad = full - rows
    c = lax.axis_index("pipe")
    i = lax.axis_index("dp")
    x = lax.rem(i, side)
    y = lax.rem(lax.div(i, side), side)
    z = lax.div(i, side * side)
    fc = x * (1 - c) + y * c
    gc = y * (1 - c) + x * c
    other = (1 - c, i)

    def remote(src, dst, send, recv, device):
        return pltpu.make_async_remote_copy(
            src_ref=src,
            dst_ref=dst,
            send_sem=send,
            recv_sem=recv,
            device_id=device,
            device_id_type=MESH,
        )

    def everybody(semaphore):
        def greet(k, _):
            peer = lax.rem(i + k, n)
            for core in (c, 1 - c):
                pl.semaphore_signal(
                    semaphore, inc=1, device_id=(core, peer), device_id_type=MESH
                )
            return 0

        pl.semaphore_signal(semaphore, inc=1, device_id=other, device_id_type=MESH)
        lax.fori_loop(1, n, greet, 0)

    barrier = pltpu.get_barrier_semaphore()
    everybody(barrier)

    count_own = r.counts[c]
    segment = lax.broadcasted_iota(jnp.int32, (segs, LANES), 0)

    def valid_for(count):
        return jnp.where(segment < count, 1.0, 0.0).astype(F32)

    valid = valid_for(count_own)
    paired = jnp.where(segment + 1 < count_own, 1.0, 0.0).astype(F32)
    pixels_own = PIX * count_own.astype(F32)

    stage = r.stage
    v = r.v
    free = r.nh3.at[1]

    def tile(j):
        return pl.ds(pl.multiple_of(j * LANES, LANES), LANES)

    def view(j, base=0):
        return (
            pl.ds(pl.multiple_of(base + lax.div(j, 4) * full, 16), rows),
            tile(lax.rem(j, 4)),
        )

    def loop(count, body):
        def step(j, _):
            body(j)
            return 0

        lax.fori_loop(0, count, step, 0)

    def packed(values):
        flat = values.reshape(rows, values.shape[-1])
        return jnp.concatenate([flat, jnp.zeros((pad, flat.shape[-1]), F32)], axis=0).astype(BF)

    def cube(values):
        return values.reshape(PIX, segs, values.shape[-1])

    def fold(values):
        return jnp.sum(jnp.sum(values, axis=0), axis=0, keepdims=True)

    def stage_to(slot, target):
        def body(j):
            target[:, tile(j)] = packed(stage[slot, :, :, tile(j)].astype(F32))

        loop(ch // LANES, body)

    def moments(values, mask=None, pixels=None):
        mask = valid if mask is None else mask
        pixels = pixels_own if pixels is None else pixels
        origin = values[0, 0:1, :]
        gaps = values - origin
        first = jnp.sum(mask * jnp.sum(gaps, axis=0), axis=0, keepdims=True)
        second = jnp.sum(mask * jnp.sum(gaps * gaps, axis=0), axis=0, keepdims=True)
        return first + pixels * origin, second - first * (first / pixels)

    load_frames = pltpu.make_async_copy(r.frames.at[c], stage.at[0], r.load_sem.at[0])
    load_frames.start()
    load_other = pltpu.make_async_copy(r.frames.at[1], stage.at[1], r.load_sem.at[1])
    pl.when(c == 0)(load_other.start)

    def weight_index(name):
        return WEIGHTS.index(name)

    def held_copy(source, name):
        return pltpu.make_async_copy(source, held_w[name], r.w_sem.at[weight_index(name)])

    def wait_weight(name):
        held_copy(own_w[name], name).wait()

    def first_send(name):
        k = weight_index(name)
        return remote(own_w[name], held_w[name], r.vs_sem.at[k], r.w_sem.at[k], other)

    def first_sends(*chosen):
        @pl.when(c == 0)
        def _():
            for name in chosen:
                first_send(name).start()

    def kept_send(name):
        k = weight_index(name)
        return remote(own_w[name], sib_w[name], r.ws_sem.at[k], r.wr_sem.at[k], other)

    def kept_sends(core):
        @pl.when(c == core)
        def _():
            for name in WEIGHTS:
                kept_send(name).start()

    def load_weight(name, s):
        @pl.when(c == s)
        def _():
            held_copy(own_w[name], name).start()

        @pl.when(c != s)
        def _():
            kept_send(name).wait_recv()
            held_copy(sib_w[name], name).start()

    @pl.when(c == 0)
    def _():
        for name in WEIGHTS:
            held_copy(own_w[name], name).start()

    own_params = [
        pltpu.make_async_copy(r.in_norm, r.norm.at[c], r.p_sem.at[0]),
        pltpu.make_async_copy(r.in_bias, r.bias.at[c], r.p_sem.at[1]),
    ]
    for copy in own_params:
        copy.start()

    r.grid[...] = jnp.zeros(r.grid.shape, F32)
    load_frames.wait()
    stage_to(0, v)
    msg, inbox = r.msg, r.inbox

    @pl.when(c == 0)
    def _():
        load_other.wait()
        stage_to(1, r.gz3)
        wait_weight("red")
        r.nh1[0] = dot(v[...], r.red[...])
        r.gs[0:full, :] = dot(r.gz3[...], r.red[...])
        count_other = r.counts[1]
        mask_other = valid_for(count_other)
        pixels_other = PIX * count_other.astype(F32)

        def body(j):
            for ref, target, with_other in (
                (r.nh1.at[0], msg.at[0, 0], ()),
                (r.gs, r.relay.at[0], (mask_other, pixels_other)),
            ):
                total, spread = moments(cube(ref[view(j)]), *with_other)
                target[pl.ds(j, 1), :] = total
                target[pl.ds(GROUP + j, 1), :] = spread

        loop(GROUP, body)

    pl.semaphore_wait(barrier, 2 * n - 1)

    param_sends = [
        remote(r.in_norm, r.norm.at[c], r.ps_sem.at[0], r.pr_sem.at[0], other),
        remote(r.in_bias, r.bias.at[c], r.ps_sem.at[1], r.pr_sem.at[1], other),
    ]
    for copy in param_sends:
        copy.start()

    def peer_of(level, k):
        size, stride = levels[level]
        here = lax.rem(lax.div(i, stride), size)
        return (c, i + (lax.rem(here + k, size) - here) * stride)

    def copies_of(bank, level):
        size, _ = levels[level]
        return [
            remote(
                msg.at[bank, level],
                inbox.at[bank, level, k],
                r.ms_sem.at[bank, level, k],
                r.mr_sem.at[bank, level, k],
                peer_of(level, k),
            )
            for k in range(1, size)
        ]

    def exchange_start(bank):
        for copy in copies_of(bank, 0):
            copy.start()

    def routed(core):
        size = levels[0][0]
        return [k for k in range(1, size) if (k % side == 0) == (core == 0)]

    def hand_over(bank):
        return remote(
            msg.at[bank, 0], r.relay.at[bank], r.hs_sem.at[bank], r.hr_sem.at[bank], other
        )

    def passed_on(bank, k):
        core, peer = peer_of(0, k)
        return remote(
            r.relay.at[bank],
            inbox.at[bank, 0, k],
            r.fs_sem.at[bank, k],
            r.mr_sem.at[bank, 0, k],
            (1 - core, peer),
        )

    def relay_start(bank):
        hand_over(bank).start()
        copies = copies_of(bank, 0)
        for core in range(2):

            @pl.when(c == core)
            def _():
                for k in routed(core):
                    copies[k - 1].start()

    def relay_pass(bank):
        hand_over(bank).wait_recv()
        for core in range(2):

            @pl.when(c == core)
            def _():
                for k in routed(core):
                    passed_on(bank, k).start()

    def exchange_finish(bank, combine, relayed=False, first=False):
        for level in range(len(levels)):
            copies = copies_of(bank, level)
            if level:
                for copy in copies:
                    copy.start()
            for copy in copies:
                copy.wait_recv()
            result = combine(bank, level)
            if level == 0 and relayed:
                hand_over(bank).wait_send()
                for core in range(2):

                    @pl.when(c == core)
                    def _():
                        for k in routed(core):
                            copies[k - 1].wait_send()
                            passed_on(bank, k).wait_send()
            elif level == 0 and first:

                @pl.when(c == 0)
                def _():
                    for k, copy in enumerate(copies):
                        copy.wait_send()
                        passed_on(bank, k + 1).wait_send()
                    for copy in first_moves:
                        copy.wait_send()
            else:
                for copy in copies:
                    copy.wait_send()
            if level + 1 < len(levels):
                msg[bank, level + 1] = result
        return result

    first_moves = [
        remote(r.relay.at[0], msg.at[0, 0], r.b_sem.at[0], r.b_sem.at[1], other),
        remote(r.gs.at[pl.ds(0, full)], r.nh1.at[0], r.b_sem.at[2], r.b_sem.at[3], other),
    ]

    @pl.when(c == 0)
    def _():
        exchange_start(0)
        for k in range(1, levels[0][0]):
            passed_on(0, k).start()
        for copy in first_moves:
            copy.start()

    cnt = r.cnt

    def count_copies(level):
        size, _ = levels[level]
        return [
            remote(
                cnt.at[level, 0],
                cnt.at[level, k],
                r.cs_sem.at[level, k],
                r.cr_sem.at[level, k],
                peer_of(level, k),
            )
            for k in range(1, size)
        ]

    cnt[0, 0] = jnp.full((8, LANES), pixels_own, F32)
    for copy in count_copies(0):
        copy.start()
    first_sends("spa", *SMALL)
    kept_sends(1)

    def count_finish():
        for level in range(len(levels)):
            copies = count_copies(level)
            if level:
                for copy in copies:
                    copy.start()
            total = cnt[level, 0]
            for k, copy in enumerate(copies):
                copy.wait()
                total = total + cnt[level, k + 1]
            if level + 1 < len(levels):
                cnt[level + 1, 0] = total
        r.total[...] = total

    def sum_combine(bank, level):
        total = msg[bank, level]
        for k in range(1, levels[level][0]):
            total = total + inbox[bank, level, k]
        return total

    def moment_combine(bank, level):
        size, _ = levels[level]
        nt = GROUP
        items = [msg[bank, level]] + [inbox[bank, level, k] for k in range(1, size)]
        counts = [cnt[level, k, 0:1, :] for k in range(size)]
        total = items[0][0:nt]
        count = counts[0]
        for k in range(1, size):
            total = total + items[k][0:nt]
            count = count + counts[k]
        mean = total / count
        spread = jnp.zeros_like(total)
        for k in range(size):
            gap = items[k][0:nt] / counts[k] - mean
            spread = spread + items[k][nt : 2 * nt] + counts[k] * gap * gap
        return jnp.concatenate([total, spread], axis=0)

    def norm_send(ref, block, bank):
        def body(j):
            total, spread = moments(cube(ref[view(block * GROUP + j)]))
            msg[bank, 0, pl.ds(j, 1), :] = total
            msg[bank, 0, pl.ds(GROUP + j, 1), :] = spread

        loop(GROUP, body)
        exchange_start(bank)

    def norm_receive(bank, s, block, row0, first=False):
        result = exchange_finish(bank, moment_combine, first=first)
        everyone = r.total[0:1, :]
        at = block * GROUP
        r.mean[at : at + GROUP, :] = result[0:GROUP] / everyone
        r.rstd[s, row0 + at : row0 + at + GROUP, :] = lax.rsqrt(
            result[GROUP : 2 * GROUP] / everyone + EPSILON
        )

    def gain_of(s, offset, j):
        lanes = pl.ds(pl.multiple_of(offset + j * LANES, LANES), LANES)
        return (r.norm[s, 0:1, lanes], r.norm[s, 1:2, lanes])

    def row_of(ref, j):
        return ref[pl.ds(j, 1), :]

    grid = r.grid

    def to_grid(values, lanes):
        for h in range(SIDE):
            at = ((h + 1) * GRID + 1) * segs
            grid[at : at + SIDE * segs, lanes] = values[h * SIDE * segs : (h + 1) * SIDE * segs]

    def patches(target, width, flip):
        def body(j):
            lanes = tile(j)
            for tap in range(9):
                down, right = tap // 3, tap % 3
                if flip:
                    down, right = 2 - down, 2 - right
                pieces = []
                for h in range(SIDE):
                    at = ((h + down) * GRID + right) * segs
                    pieces.append(grid[at : at + SIDE * segs, lanes])
                target[:, pl.ds(pl.multiple_of(tap * width + j * LANES, LANES), LANES)] = packed(
                    jnp.concatenate(pieces, axis=0)
                )

        loop(width // LANES, body)

    def put(slot, target, kind, s):
        @pl.when(c == s)
        def _():
            pltpu.make_async_copy(stage.at[slot], target.at[c], r.o_sem.at[kind, 0]).start()

        @pl.when(c != s)
        def _():
            remote(
                stage.at[slot],
                target.at[c],
                r.o_sem.at[kind, 1],
                r.o_sem.at[kind, 2],
                other,
            ).start()

    def put_wait(slot, target, kind, s):
        @pl.when(c == s)
        def _():
            pltpu.make_async_copy(stage.at[slot], target.at[c], r.o_sem.at[kind, 0]).wait()

        @pl.when(c != s)
        def _():
            remote(
                stage.at[slot],
                target.at[c],
                r.o_sem.at[kind, 1],
                r.o_sem.at[kind, 2],
                other,
            ).wait_send()

    n_mid = mid // LANES
    n_ch = ch // LANES
    n_blocks = ch // ROW

    def across(k):
        to_y = y + k // 2 - 2 * y * (k // 2)
        to_x = x + k % 2 - 2 * x * (k % 2)
        return to_y * 2 + to_x, (c, z * 4 + to_y * 2 + to_x)

    def act_move(s, k, half):
        lanes = pl.ds(half * HALF, HALF)
        sems = (r.as_sem.at[s, k, half], r.ar_sem.at[s, k, half])
        return remote(r.a1g.at[s, 0, :, lanes], r.a1g.at[s, k, :, lanes], *sems, across(k)[1])

    def grad_move(s, k):
        to_q, device = across(k)
        sems = (r.gs_sem.at[s, k], r.gr_sem.at[s, k])
        return remote(r.gz2q.at[to_q], r.gzg.at[s, k - 1], *sems, device)

    def act_moves(*chosen):
        if grouped:
            for move in chosen:
                act_move(*move).start()

    for copy in own_params:
        copy.wait()
    for s in range(2):
        nh1, nh2, nh3 = r.nh1.at[s], r.nh2.at[s], r.nh3.at[s]
        if s == 0:
            load_weight("red", 1)
            for copy in param_sends:
                copy.wait_recv()

            @pl.when(c == 1)
            def _():
                for copy in first_moves:
                    copy.wait_recv()

            count_finish()
        else:
            wait_weight("red")
            nh1[...] = dot(v[...], r.red[...])
            kept_sends(0)
            norm_send(nh1, 0, 0)
            act_moves((0, 3, 0))
        norm_receive(0, s, 0, 0, s == 0)

        def act_one(j, s=s, nh1=nh1):
            gain, offset = gain_of(s, 0, j)
            normed = (nh1[view(j)] - row_of(r.mean, j)) * row_of(r.rstd.at[s], j)
            nh1[view(j)] = normed
            before = normed * gain + offset
            act = before * sigmoid(before)
            r.a1g[s, 0, :, tile(j)] = packed(act)
            to_grid(act, tile(j))

        loop(n_mid, act_one)
        patches(r.patch, mid, False)
        wait_weight("spa")
        nh2[...] = dot(r.patch[...], r.spa[...])
        if s == 0:
            first_sends("exp")
            load_weight("spa", 1)
        norm_send(nh2, 0, 1)
        if s == 0:
            act_moves((0, 1, 0), (0, 2, 0))
        else:
            act_moves((0, 3, 1), (1, 1, 0), (1, 2, 0))
        norm_receive(1, s, 0, n_mid)

        def act_two(j, s=s, nh2=nh2):
            gain, offset = gain_of(s, mid, j)
            normed = (nh2[view(j)] - row_of(r.mean, j)) * row_of(r.rstd.at[s], n_mid + j)
            nh2[view(j)] = normed
            before = normed * gain + offset
            r.h2[s, :, tile(j)] = packed(before * sigmoid(before))

        loop(n_mid, act_two)
        for name in SMALL:
            wait_weight(name)
        squeezed = cube(dot(r.h2[s], r.squ[...])[:rows])
        later = pltpu.roll(squeezed, segs - 1, 1)
        field = (paired * (later - squeezed)).reshape(rows, red_w)
        r.field[s] = packed(field)
        rounded = r.field[s].astype(F32)[:rows]
        to_grid(rounded, pl.ds(0, LANES))
        patches(r.patch_m, red_w, False)
        context_mean = jnp.sum(cube(rounded), axis=0) * (1.0 / PIX)
        r.cmean[s] = context_mean
        from_mean = jnp.dot(
            context_mean, r.con[...].astype(F32), precision=HIGH, preferred_element_type=F32
        )
        mixed = cube(dot(r.patch_m[...], r.mot[...])[:rows]) + from_mean
        r.score[s] = packed(mixed)
        free[0:full, :] = dot(r.score[s], r.gat[...])

        def gate(j, s=s):
            bias = r.bias[s, 0:1, tile(j)]
            sigma = sigmoid(free[view(j)] + bias)
            r.sigma[s, :, tile(j)] = packed(sigma)
            h2 = r.h2[s, :, tile(j)].astype(F32)[:rows]
            r.gated[s, :, tile(j)] = packed(h2 * (0.5 + sigma))

        loop(n_mid, gate)
        if s == 0:
            for name in SMALL:
                load_weight(name, 1)
        wait_weight("exp")
        for block in range(n_blocks):
            nh3[block * full : (block + 1) * full, :] = dot(
                r.gated[s], r.exp[:, block * ROW : (block + 1) * ROW]
            )
            norm_send(nh3, block, 2 + block)
        act_moves((s, 1, 1), (s, 2, 1))
        if s == 0:
            load_weight("exp", 1)
        slot = 1 - s

        def finish(j, s=s, nh3=nh3, slot=slot):
            gain, offset = gain_of(s, 2 * mid, j)
            normed = (nh3[view(j)] - row_of(r.mean, j)) * row_of(
                r.rstd.at[s], 2 * n_mid + j
            )
            nh3[view(j)] = normed
            before = v[:, tile(j)].astype(F32)[:rows] + normed * gain + offset
            out = cube(before * sigmoid(before)) * valid
            stage[slot, :, :, tile(j)] = out.astype(BF)
            if s == 0:
                v[:, tile(j)] = packed(out)

        for block in range(n_blocks):
            norm_receive(2 + block, s, block, 2 * n_mid)
            loop(GROUP, lambda j, block=block: finish(block * GROUP + j))
        put(slot, r.out, s, s)
        if s == 0:
            put_wait(slot, r.out, 0, 0)
            load_grad = pltpu.make_async_copy(r.out_grad.at[c], stage.at[1], r.load_sem.at[1])
            load_grad.start()

    def send_sem(chunk, s, k):
        return r.rs_send.at[s, chunks.index(chunk), k]

    def recv_sem(chunk, s, k):
        return r.rs_recv.at[s, chunks.index(chunk), k]

    def add_loop(target, others, pieces):
        def body(j):
            at = target.at[j]
            total = at[...]
            for item in others:
                total = total + item.at[j][...]
            at[...] = total

        loop(pieces, body)

    def along(to):
        px = to * (1 - c) + x * c
        py = y * (1 - c) + to * c
        return z * side * side + py * side + px

    def rs0(chunk, s):
        ref = chunk_refs[chunk]
        found = []
        for k in range(1, side):
            sems = (send_sem(chunk, s, k), recv_sem(chunk, s, k))
            source = ref.g.at[1 - c, lax.rem(gc + k, side)]
            found.append(remote(source, ref.far.at[k - 1], *sems, other))
        sems = (send_sem(chunk, s, 0), recv_sem(chunk, s, 0))
        return found, remote(ref.g.at[c, fc], ref.near, *sems, other)

    def rs1(chunk, s):
        ref = chunk_refs[chunk]
        found = []
        for k in range(1, side):
            at = side - 1 + k
            sems = (send_sem(chunk, s, at), recv_sem(chunk, s, at))
            device = (1 - c, along(lax.rem(fc + k, side)))
            found.append(remote(ref.far.at[k - 1], ref.r1.at[s * grouped, k - 1], *sems, device))
        return found

    def rs2(chunk, s):
        ref = chunk_refs[chunk]
        found = []
        for k in range(1, side):
            to = lax.rem(fc + k, side)
            at = 2 * (side - 1) + k
            sems = (send_sem(chunk, s, at), recv_sem(chunk, s, at))
            found.append(remote(ref.near.at[to], ref.r2.at[s * grouped, k - 1], *sems, (c, along(to))))
        return found

    def rs3(chunk, s):
        ref = chunk_refs[chunk]
        found = []
        for k in range(1, depth):
            to = lax.rem(z + k, depth)
            at = 3 * (side - 1) + k
            sems = (send_sem(chunk, s, at), recv_sem(chunk, s, at))
            source = ref.near.at[fc, lax.rem(to, slots)]
            device = (c, to * side * side + y * side + x)
            found.append((to, remote(source, ref.r3.at[s * grouped, k - 1], *sems, device)))
        return found

    def credit(chunk):
        return r.credit.at[chunks.index(chunk)]

    def rs0_start(chunk, s):
        if s == 0:
            pl.semaphore_wait(credit(chunk), 1)
        far, near = rs0(chunk, s)
        for copy in far:
            copy.start()
        near.start()

    def rs1_start(chunk, s):
        ref = chunk_refs[chunk]
        far, near = rs0(chunk, s)
        for k, copy in enumerate(far):
            copy.wait()
            to = lax.rem(fc + k + 1, side)
            for b in range(side):
                add_loop(ref.far.at[k, b], [ref.g.at[c, to, b]], slots)
        for copy in rs1(chunk, s):
            copy.start()
        near.wait()
        for b in range(side):
            add_loop(ref.near.at[b], [ref.g.at[1 - c, gc, b]], slots)

    def rs2_start(chunk, s):
        ref = chunk_refs[chunk]
        copies = rs1(chunk, s)
        for copy in copies:
            copy.wait_recv()
        for b in range(side):
            add_loop(ref.near.at[b], [ref.r1.at[s * grouped, k, b] for k in range(side - 1)], slots)
        for copy in copies:
            copy.wait_send()
        for copy in rs2(chunk, s):
            copy.start()

    def rs3_start(chunk, s):
        ref = chunk_refs[chunk]
        copies = rs2(chunk, s)
        for copy in copies:
            copy.wait_recv()
        add_loop(ref.near.at[fc], [ref.r2.at[s * grouped, k] for k in range(side - 1)], slots)
        for copy in copies:
            copy.wait_send()
        for to, copy in rs3(chunk, s):
            if slots == depth:
                copy.start()
            else:
                pl.when(to < slots)(copy.start)

    def row_of_piece(comp, core, piece):
        start, size = parts[comp]
        if grouped and comp == "spa":
            return start + size * (core * depth + lax.div(piece, side * side))
        return start + size * piece

    def send_piece(comp, s, action):
        _, size = parts[comp]
        at = row_of_piece(comp, c, i)
        first = lax.div(at * ROW, share)
        last = lax.div(jnp.minimum((at + size) * ROW, pp.total) - 1, share)
        exists = jnp.logical_and(i < PIECES, at * ROW < pp.total)
        which = COMPS.index(comp)
        width = fin[comp].shape[1]
        lanes = lax.rem(i, side * side) * LANES if width == LANES else (1 - c) * HALF
        for k in range(pp.reach):
            to = first + k
            base = lax.div(to * share, ROW * 16) * 16
            row = pl.multiple_of(pp.margin + at - base, 16)
            there = r.land.at[pl.ds(row, size), pl.ds(pl.multiple_of(lanes, width), width)]
            needed = jnp.logical_and(exists, to <= last)
            here = jnp.logical_and(c == s, to == i)
            source = fin[comp]
            arrival = r.land_sem.at[which, c, lax.rem(i, PIECES)]

            @pl.when(jnp.logical_and(needed, here))
            def _():
                copy = pltpu.make_async_copy(source, there, arrival)
                if action == "start":
                    copy.start()
                else:
                    copy.wait()

            @pl.when(jnp.logical_and(needed, jnp.logical_not(here)))
            def _():
                copy = remote(source, there, r.fin_sem.at[which, k], arrival, (s, to))
                if action == "start":
                    copy.start()
                else:
                    copy.wait_send()

    def finish_chunk(chunk, s):
        ref = chunk_refs[chunk]
        own = ref.near.at[fc]
        r3 = ref.r3
        copies = rs3(chunk, s)
        cins = mid // PIECES
        if s == 0 and chunk in OPENS:
            for comp in OPENS[chunk]:
                send_piece(comp, 1, "wait")

        def work():
            for _, copy in copies:
                copy.wait_recv()
            mine = own.at[lax.rem(z, slots)]

            def summed(first, count):
                total = mine[first : first + count, :].astype(F32)
                for k in range(depth - 1):
                    total = total + r3[s * grouped, k, first : first + count, :].astype(F32)
                return total

            def weave(mix, first, count, stride, value):
                for k in range(HALF // LANES):
                    mix[k, pl.ds(first, count, stride=stride), :] = value[
                        :, k * LANES : (k + 1) * LANES
                    ]

            def woven(mix, target, size):
                for k in range(HALF // LANES):
                    target[:, k * LANES : (k + 1) * LANES] = mix[k, 0:size, :].astype(BF)

            if chunk == "e":
                size = parts["exp"][1]
                quarters = size // cins
                for q in range(quarters):
                    weave(r.mix_e, q, cins, quarters, summed(q * cins, cins))
                woven(r.mix_e, r.fin_exp, size)
                r.fin_small[...] = summed(size, parts["small"][1]).astype(BF)
            elif chunk in TAPS:
                first, end = TAPS[chunk]
                for tap in range(first, end):
                    weave(r.mix, tap, cins, 9, summed((tap - first) * cins, cins))
                if end == 9:
                    woven(r.mix, r.fin_spa, parts["spa"][1])
            else:
                first, end = (k * parts["red"][1] // CUTS for k in ROWS[chunk])
                r.fin_red[first:end, :] = summed(0, end - first).astype(BF)

        if slots == depth:
            work()
        else:
            pl.when(z < slots)(work)
        for to, copy in copies:
            if slots == depth:
                copy.wait_send()
            else:
                pl.when(to < slots)(copy.wait_send)
        if s == 1:
            pl.semaphore_signal(credit(chunk), inc=1, device_id=other, device_id_type=MESH)
        for comp in CLOSES.get(chunk, ()):
            send_piece(comp, s, "start")

    def place(half, piece):
        px, py, pz = piece % side, (piece // side) % side, piece // (side * side)
        return (half, px, py, pz) if half == 0 else (half, py, px, pz)

    small_at = 2 * full

    def grads_e(s):
        cins = mid // PIECES
        g = chunk_refs["e"].g
        for q in range(ch // ROW):
            for half in range(2):
                lanes = slice(q * ROW + half * HALF, q * ROW + (half + 1) * HALF)
                value = dot_tn(r.gated[s], r.gz3[:, lanes]).astype(BF)
                for piece in range(PIECES):
                    where = place(half, piece)
                    g[where + (slice(q * cins, (q + 1) * cins),)] = value[
                        piece * cins : (piece + 1) * cins
                    ]

    def grads_small(s):
        g = chunk_refs["e"].g
        tmp = r.tmp1
        at = small_at
        per = ROW // LANES

        def spread(count):
            for q in range(per):
                free[at : at + count, q * LANES : (q + 1) * LANES] = tmp[
                    pl.ds(q, count, stride=per), :
                ]

        tmp[0:mid, :] = dot_tn(r.h2[s], r.gr[...])
        spread(mid // per)
        at += mid // per
        moved = dot_tn(r.field[s], r.patch_m[...])
        for tap in range(9):
            tmp[pl.ds(tap, red_w, stride=9), :] = moved[:, tap * LANES : (tap + 1) * LANES]
        spread(9 * red_w // per)
        at += 9 * red_w // per
        tmp[0:red_w, :] = lax.dot_general(
            r.cmean[s],
            r.ssum[...],
            (((0,), (0,)), ((), ())),
            precision=HIGH,
            preferred_element_type=F32,
        )
        spread(red_w // per)
        at += red_w // per
        free[at : at + red_w, :] = dot_tn(r.score[s], r.gl[...])
        at += red_w
        free[at : at + 8, :] = jnp.broadcast_to(r.gbias[...], (8, mid))
        start = parts["exp"][1]
        size = parts["small"][1]
        used = -(-pp.small_rows // size)
        for piece in range(PIECES):
            for half in range(2):
                where = place(half, piece) + (slice(start, start + size),)
                if piece < used:
                    g[where] = free[
                        small_at + piece * size : small_at + (piece + 1) * size,
                        half * HALF : (half + 1) * HALF,
                    ].astype(BF)
                else:
                    g[where] = jnp.zeros((size, HALF), BF)

    def grads_taps(chunk, s):
        cins = mid // PIECES
        g = chunk_refs[chunk].g
        first, end = TAPS[chunk]

        def body(tap):
            for half in range(2):
                lanes = pl.ds(pl.multiple_of((first + tap) * mid + half * HALF, HALF), HALF)
                value = dot_tn(r.a1g[s, 0], r.patch[:, lanes]).astype(BF)
                for piece in range(PIECES):
                    where = place(half, piece)
                    g[where + (pl.ds(pl.multiple_of(tap * cins, cins), cins),)] = value[
                        piece * cins : (piece + 1) * cins
                    ]

        loop(end - first, body)

    def grads_group(s):
        total = None
        for k in range(4):
            if k:
                act_move(s, k, 0).wait_recv()
                act_move(s, k, 1).wait_recv()
                grad_move(s, k).wait_recv()
                grad = r.gzg[s, k - 1]
            else:
                grad = r.gz2q[lax.rem(i, 4)]
            to_grid(grad.astype(F32)[:rows], pl.ds(0, LANES))
            patches(r.patch.at[:, pl.ds(k * 9 * LANES, 9 * LANES)], LANES, True)
        for k in range(4):
            part = dot_tn(r.a1g[s, k], r.patch[:, k * 9 * LANES : (k + 1) * 9 * LANES])
            total = part if total is None else total + part
        r.sum_g[...] = total
        r.out_g[...] = r.sum_g[pl.ds(pl.multiple_of((1 - c) * HALF, HALF), HALF), :].astype(BF)
        if s == 0:
            pl.semaphore_wait(r.credit.at[len(chunks)], 1)
        group_swap(s).start()

    def group_swap(s):
        return remote(r.out_g, r.in_g, r.g3_sem.at[s, 0, 0], r.g3_sem.at[s, 1, 0], other)

    def group_moves(s):
        found = []
        for k in range(1, depth):
            to = lax.rem(z + k, depth)
            device = (c, to * 4 + lax.rem(i, 4))
            found.append(
                remote(
                    r.pile_g.at[to],
                    r.r3_g.at[s, k - 1],
                    r.g3_sem.at[s, 0, k],
                    r.g3_sem.at[s, 1, k],
                    device,
                )
            )
        return found

    def group_start(s):
        cins = HALF // depth
        group_swap(s).wait()
        for to in range(depth):
            at = pl.ds(pl.multiple_of(c * HALF + to * cins, cins), cins)
            for tap in range(9):
                lanes = slice(tap * LANES, (tap + 1) * LANES)
                theirs = r.in_g[to * cins : (to + 1) * cins, lanes].astype(F32)
                value = r.sum_g[at, lanes] + theirs
                r.pile_g[to, tap * cins : (tap + 1) * cins, :] = value.astype(BF)
        if s == 1:
            pl.semaphore_signal(
                r.credit.at[len(chunks)], inc=1, device_id=other, device_id_type=MESH
            )
        for copy in group_moves(s):
            copy.start()

    def group_finish(s):
        cins = HALF // depth
        copies = group_moves(s)
        for copy in copies:
            copy.wait_recv()
        for tap in range(9):
            at = slice(tap * cins, (tap + 1) * cins)
            total = r.pile_g[z, at, :].astype(F32)
            for k in range(depth - 1):
                total = total + r.r3_g[s, k, at, :].astype(F32)
            r.mix[0, pl.ds(tap, cins, stride=9), :] = total
        if s == 0:
            send_piece("spa", 1, "wait")
        r.fin_spa[...] = r.mix[0].astype(BF)
        for copy in copies:
            copy.wait_send()
        send_piece("spa", s, "start")

    def grads_c(s):
        size = parts["red"][1]
        for half in range(2):
            value = dot_tn(v[...], r.gz1[:, half * HALF : (half + 1) * HALF]).astype(BF)
            for chunk, cut in ROWS.items():
                first, end = (k * size // CUTS for k in cut)
                for piece in range(PIECES):
                    chunk_refs[chunk].g[place(half, piece)] = value[
                        piece * size + first : piece * size + end
                    ]

    def back_receive(bank, s, block, row0, relayed=True):
        result = exchange_finish(bank, sum_combine, relayed)
        half_rows = 2 * n_mid + n_ch
        at = row0 + block * GROUP
        r.gnorm[s, at : at + GROUP, :] = result[GROUP : 2 * GROUP]
        r.gnorm[s, half_rows + at : half_rows + at + GROUP, :] = result[0:GROUP]
        r.bsum[block] = result / r.total[0:1, :]

    def norm_grad(grad, normed, s, offset, row0, j):
        gain, _ = gain_of(s, offset, j)
        scale = gain * row_of(r.rstd.at[s], row0 + j)
        means = r.bsum.at[lax.div(j, GROUP)]
        mean_grad = row_of(means, lax.rem(j, GROUP))
        mean_cross = row_of(means, GROUP + lax.rem(j, GROUP))
        return scale * (cube(grad) - valid * (mean_grad + cube(normed) * mean_cross))

    def slope(s, grad_at, normed_ref, offset, bank):
        def body(j):
            gain, shift = gain_of(s, offset, j)
            normed = normed_ref[view(j)]
            grad = free[view(j, grad_at)] * silu_slope(normed * gain + shift)
            free[view(j, grad_at)] = grad
            msg[bank, 0, pl.ds(j, 1), :] = fold(cube(grad))
            msg[bank, 0, pl.ds(GROUP + j, 1), :] = fold(cube(grad * normed))

        loop(GROUP, body)

    gs = r.gs
    reload = pltpu.make_async_copy(r.frames.at[c], stage.at[1], r.load_sem.at[0])

    def bank_three(s, block):
        return 2 + n_blocks * s + block

    def back_three(s, block):
        if s == 1 and block == 0:
            load_grad.wait()
        nh3 = r.nh3.at[s]
        bank = bank_three(s, block)

        def body(j):
            at = block * GROUP + j
            gain, shift = gain_of(s, 2 * mid, at)
            normed = nh3[view(at)]
            before = v[:, tile(at)].astype(F32)[:rows] + normed * gain + shift
            grad = cube(silu_slope(before)) * valid * stage[s, :, :, tile(at)].astype(F32)
            gs[view(at)] = grad.reshape(rows, LANES)
            msg[bank, 0, pl.ds(j, 1), :] = fold(grad)
            msg[bank, 0, pl.ds(GROUP + j, 1), :] = fold(grad * cube(normed))

        loop(GROUP, body)

    def send_sums(bank, relayed):
        if relayed:
            relay_start(bank)
            relay_pass(bank)
        else:
            exchange_start(bank)

    def grad_three(s, block, relayed):
        nh3 = r.nh3.at[s]
        back_receive(bank_three(s, block), s, block, 2 * n_mid, relayed)

        def body(j):
            at = block * GROUP + j
            r.gz3[:, tile(at)] = packed(
                norm_grad(gs[view(at)], nh3[view(at)], s, 2 * mid, 2 * n_mid, at)
            )

        loop(GROUP, body)

    def back_expander(s):
        if s == 0:
            wait_weight("exp")
        free[0:full, :] = dot_nt(r.gz3[...], r.exp[...])
        if s == 1:
            load_weight("exp", 0)

    def back_gate(s):
        def body(j):
            grad = free[view(j)]
            sigma = r.sigma[s, :, tile(j)].astype(F32)[:rows]
            h2 = r.h2[s, :, tile(j)].astype(F32)[:rows]
            free[view(j, full)] = grad * (0.5 + sigma)
            value = packed(grad * h2 * sigma * (1.0 - sigma))
            r.gl[:, tile(j)] = value
            r.gbias[0:1, tile(j)] = fold(cube(value.astype(F32)[:rows]))

        loop(n_mid, body)

    def back_motion(s):
        if s == 0:
            for name in SMALL:
                wait_weight(name)
        r.gq[...] = dot_nt(r.gl[...], r.gat[...]).astype(BF)
        rounded = r.gq[...].astype(F32)[:rows]
        to_grid(rounded, pl.ds(0, LANES))
        patches(r.patch_m, red_w, True)
        score_sums = jnp.sum(cube(rounded), axis=0)
        r.ssum[...] = score_sums
        grad_field = None
        for tap in range(9):
            part = dot_nt(
                r.patch_m[:, tap * red_w : (tap + 1) * red_w],
                r.mot[tap * red_w : (tap + 1) * red_w, :],
            )
            grad_field = part if grad_field is None else grad_field + part
        from_mean = lax.dot_general(
            score_sums,
            r.con[...].astype(F32),
            (((1,), (1,)), ((), ())),
            precision=HIGH,
            preferred_element_type=F32,
        ) * (1.0 / PIX)
        weighted = paired * (cube(grad_field[:rows]) + from_mean)
        r.gr[...] = packed(pltpu.roll(weighted, 1, 1) - weighted)
        free[full : 2 * full, :] += dot_nt(r.gr[...], r.squ[...])
        if s == 1:
            for name in SMALL:
                load_weight(name, 0)

    def back_spread(s):
        nh2 = r.nh2.at[s]

        def body(j):
            value = norm_grad(free[view(j, full)], nh2[view(j)], s, mid, n_mid, j)
            to_grid(value.reshape(rows, LANES), tile(j))
            if grouped:
                r.gz2q[j] = packed(value)

        if grouped and s == 0:
            for k in range(1, 4):
                grad_move(1, k).wait_send()
        loop(n_mid, body)
        patches(r.patch, mid, True)

    def back_conv(s):
        if s == 0:
            wait_weight("spa")
        acc = None
        for tap in range(9):
            part = dot_nt(
                r.patch[:, tap * mid : (tap + 1) * mid], r.spa[tap * mid : (tap + 1) * mid, :]
            )
            acc = part if acc is None else acc + part
        free[0:full, :] = acc
        if s == 1:
            load_weight("spa", 0)

    def grad_one(s):
        nh1 = r.nh1.at[s]

        def body(j):
            r.gz1[:, tile(j)] = packed(norm_grad(free[view(j)], nh1[view(j)], s, 0, 0, j))

        loop(n_mid, body)

    def back_input(s):
        if s == 1:
            put_wait(0, r.out, 1, 1)
            reload.start()
        else:
            wait_weight("red")
        for block in range(n_blocks):
            value = gs[block * full : block * full + rows, :] + dot_nt(
                r.gz1[...], r.red[block * ROW : (block + 1) * ROW, :]
            )[:rows]
            stage[1 - s, :, :, block * ROW : (block + 1) * ROW] = cube(value).astype(BF)
        put(1 - s, r.ing, 2 + s, s)
        if s == 1:
            load_weight("red", 0)

    def back_reload(s):
        reload.wait()
        stage_to(1, v)

    def perform(token):
        op, s = token[:-1], int(token[-1])
        kind, rest = op[0], op[1:]
        if kind == "s":
            back_three(s, int(rest))
        elif kind == "x":
            send_sums(bank_three(s, int(rest)), kind + token[-1] in RELAYED)
        elif kind == "w":
            grad_three(s, int(rest), "x" + token[-1] in RELAYED)
        elif kind == "y":
            send_sums(int(rest) - 1, token in RELAYED)
        elif op == "z2":
            back_receive(1, s, 0, n_mid, "y" + token[1:] in RELAYED)
        elif op == "z1":
            back_receive(0, s, 0, 0, "y" + token[1:] in RELAYED)
        elif op == "g":
            if grouped:
                for k in range(1, 4):
                    grad_move(s, k).start()
        elif kind == "m":
            act_moves((s, 3, int(rest)))
        elif rest == "b" and grouped:
            if kind == "G":
                grads_group(s)
            elif kind == "3":
                group_start(s)
            else:
                group_finish(s)
        elif rest == "b":
            for chunk in TAPS:
                if kind == "G":
                    grads_taps(chunk, s)
                    rs0_start(chunk, s)
                    rs1_start(chunk, s)
                    rs2_start(chunk, s)
                elif kind == "3":
                    rs3_start(chunk, s)
                else:
                    finish_chunk(chunk, s)
        elif kind == "G":
            if rest == "e":
                grads_e(s)
            elif rest == "s":
                grads_small(s)
            else:
                grads_c(s)
        elif kind == "0":
            rs0_start(rest, s)
        elif kind == "1":
            rs1_start(rest, s)
        elif kind == "2":
            rs2_start(rest, s)
        elif kind == "3":
            rs3_start(rest, s)
        elif kind == "4":
            finish_chunk(rest, s)
        elif op == "l2":
            slope(s, full, r.nh2.at[s], mid, 1)
        elif op == "l1":
            slope(s, 0, r.nh1.at[s], 0, 0)
        else:
            table[op](s)

    table = dict(
        a=back_expander,
        b=back_gate,
        q=back_motion,
        p=back_spread,
        v=back_conv,
        o=grad_one,
        i=back_input,
        r=back_reload,
    )
    if grouped:
        for token in ORDER:
            perform(token)
    else:
        for token in ORDER:
            if token[-1] == "1":
                perform(token)
        everybody(r.between.at[0])
        pl.semaphore_wait(r.between.at[0], 2 * n - 1)
        for token in ORDER:
            if token[-1] == "0":
                perform(token)

    gn_send = remote(
        r.gnorm.at[1 - c], r.gnorm_in, r.gn_sem.at[0], r.gn_sem.at[1], other
    )
    gn_send.start()
    gn_send.wait()
    r.gnorm_out[...] = r.gnorm[c] + r.gnorm_in[...]

    if grouped:
        for k in range(1, 4):
            for s in range(2):
                act_move(s, k, 0).wait_send()
                act_move(s, k, 1).wait_send()
            grad_move(0, k).wait_send()
    for copy in param_sends:
        copy.wait_send()
    for name in WEIGHTS:
        kept_send(name).wait_send()

    @pl.when(c == 0)
    def _():
        for name in WEIGHTS[1:]:
            first_send(name).wait_send()

    put_wait(0, r.ing, 3, 1)
    put_wait(1, r.ing, 2, 0)
    for base, target in ((0, r.out), (2, r.ing)):
        for s in range(2):

            @pl.when(c == s)
            def _():
                remote(
                    stage.at[0],
                    target.at[1 - c],
                    r.o_sem.at[base + s, 1],
                    r.o_sem.at[base + s, 2],
                    other,
                ).wait_recv()

    for comp in COMPS:
        send_piece(comp, 0, "wait")
    low = i * share
    high = low + share
    for which, comp in enumerate(COMPS):
        _, size = parts[comp]
        width = fin[comp].shape[1]
        for core in range(2):

            def arrive(piece, _):
                first = row_of_piece(comp, core, piece) * ROW
                last = jnp.minimum(first + size * ROW, pp.total)
                near = jnp.logical_and(first < high, last > low)
                own = jnp.logical_and(c == core, i == piece)

                @pl.when(jnp.logical_and(near, jnp.logical_not(own)))
                def _():
                    pltpu.make_async_copy(
                        fin[comp],
                        r.land.at[pl.ds(0, size), pl.ds(0, width)],
                        r.land_sem.at[which, core, piece],
                    ).wait()

                return 0

            lax.fori_loop(0, PIECES, arrive, 0)


def run(n, sizes, frames, out_grad, seg_counts, weights, bias, norm):
    ch, mid, red_w, segs, share = sizes
    pp = plan(n, ch, mid, red_w, segs, share)
    side, depth, slots, levels, parts = pp.side, pp.depth, pp.slots, pp.levels, pp.parts
    rows = PIX * segs
    full = up(rows, 16)
    norm_rows = 2 * (2 * mid + ch) // LANES
    group = max(size for size, _ in levels)
    any_spec = pl.BlockSpec(memory_space=pl.ANY)
    vmem_spec = pl.BlockSpec(memory_space=pltpu.VMEM)

    ins = dict(
        frames=frames,
        out_grad=out_grad,
        in_red=weights.red,
        in_spa=weights.spa,
        in_exp=weights.exp,
        in_squ=weights.squ,
        in_mot=weights.mot,
        in_con=weights.con,
        in_gat=weights.gat,
        counts=seg_counts,
        in_bias=bias,
        in_norm=norm,
    )
    in_specs = [any_spec] * 9 + [pl.BlockSpec(memory_space=pltpu.SMEM), any_spec, any_spec]

    def like(item):
        return jax.ShapeDtypeStruct(item.shape, item.dtype)

    outs = dict(
        out=like(frames),
        ing=like(frames),
        land=jax.ShapeDtypeStruct((pp.land, ROW), BF),
        sib_red=like(weights.red),
        sib_spa=like(weights.spa),
        sib_exp=like(weights.exp),
        sib_squ=like(weights.squ),
        sib_mot=like(weights.mot),
        sib_con=like(weights.con),
        sib_gat=like(weights.gat),
        gnorm_out=jax.ShapeDtypeStruct((norm_rows, LANES), F32),
    )
    out_specs = [any_spec] * 10 + [vmem_spec]

    def low(*dims):
        return pltpu.VMEM(dims, BF)

    def wide(*dims):
        return pltpu.VMEM(dims, F32)

    def sems(*dims):
        return pltpu.SemaphoreType.DMA(dims)

    def piled(size):
        return (
            low(2, side, side, slots, size, HALF),
            low(max(side - 1, 1), side, slots, size, HALF),
            low(side, slots, size, HALF),
            low(1 + pp.grouped, max(side - 1, 1), side, slots, size, HALF),
            low(1 + pp.grouped, max(side - 1, 1), slots, size, HALF),
            low(1 + pp.grouped, max(depth - 1, 1), size, HALF),
        )

    cins = mid // PIECES
    sizes_of = dict(e=parts["exp"][1] + parts["small"][1])
    for chunk, (first, end) in TAPS.items():
        sizes_of[chunk] = (end - first) * cins
    for chunk, (first, end) in ROWS.items():
        sizes_of[chunk] = (end - first) * parts["red"][1] // CUTS
    chunks = chunk_names(n)
    piles = [item for chunk in chunks for item in piled(sizes_of[chunk])]
    spa_width = LANES if pp.grouped else HALF
    spa_size = parts["spa"][1]
    hops = 3 * (side - 1) + depth
    banks = 2 + 2 * (ch // ROW)
    scratch = dict(
        red=low(*weights.red.shape),
        spa=low(*weights.spa.shape),
        exp=low(*weights.exp.shape),
        squ=low(*weights.squ.shape),
        mot=low(*weights.mot.shape),
        con=low(*weights.con.shape),
        gat=low(*weights.gat.shape),
        bias=wide(2, *bias.shape),
        norm=wide(2, *norm.shape),
        stage=low(2, *frames.shape[1:]),
        v=low(full, ch),
        nh1=wide(2, full, mid),
        nh2=wide(2, full, mid),
        nh3=wide(2, full * ch // ROW, ROW),
        gs=wide(full * ch // ROW, ROW),
        sigma=low(2, full, mid),
        a1g=low(2, 4 if pp.grouped else 1, full, mid),
        h2=low(2, full, mid),
        gated=low(2, full, mid),
        field=low(2, full, red_w),
        score=low(2, full, red_w),
        cmean=wide(2, segs, red_w),
        ssum=wide(segs, red_w),
        gbias=wide(1, mid),
        gz3=low(full, ch),
        gz1=low(full, mid),
        gl=low(full, mid),
        gq=low(full, red_w),
        gr=low(full, red_w),
        patch=low(full, 9 * mid),
        patch_m=low(full, 9 * red_w),
        grid=wide(GRID * GRID * segs, mid),
        tmp1=wide(9 * red_w, LANES),
        mix=wide(spa_width // LANES, spa_size, LANES),
        mix_e=wide(HALF // LANES, parts["exp"][1], LANES),
        msg=wide(banks, len(levels), 2 * GROUP, LANES),
        inbox=wide(banks, len(levels), group, 2 * GROUP, LANES),
        cnt=wide(len(levels), group, 8, LANES),
        relay=wide(banks, 2 * GROUP, LANES),
        total=wide(8, LANES),
        mean=wide(ch // LANES, LANES),
        bsum=wide(ch // ROW, 2 * GROUP, LANES),
        rstd=wide(2, norm_rows // 2, LANES),
        gnorm=wide(2, norm_rows, LANES),
        gnorm_in=wide(norm_rows, LANES),
        fin_red=low(parts["red"][1], HALF),
        fin_spa=low(spa_size, spa_width),
        fin_exp=low(parts["exp"][1], HALF),
        fin_small=low(parts["small"][1], HALF),
        load_sem=sems(2),
        w_sem=sems(len(WEIGHTS)),
        vs_sem=sems(len(WEIGHTS)),
        ws_sem=sems(len(WEIGHTS)),
        wr_sem=sems(len(WEIGHTS)),
        p_sem=sems(2),
        ps_sem=sems(2),
        pr_sem=sems(2),
        ms_sem=sems(banks, len(levels), group),
        mr_sem=sems(banks, len(levels), group),
        cs_sem=sems(len(levels), group),
        hs_sem=sems(banks),
        hr_sem=sems(banks),
        fs_sem=sems(banks, group),
        cr_sem=sems(len(levels), group),
        o_sem=sems(4, 3),
        rs_send=sems(2, len(chunks), hops),
        rs_recv=sems(2, len(chunks), hops),
        fin_sem=sems(4, pp.reach),
        land_sem=sems(4, 2, PIECES),
        gn_sem=sems(2),
        b_sem=sems(4),
        between=pltpu.SemaphoreType.REGULAR((1,)),
        credit=pltpu.SemaphoreType.REGULAR((len(chunks) + 1,)),
    )
    if pp.grouped:
        scratch |= dict(
            gzg=low(2, 3, full, LANES),
            gz2q=low(mid // LANES, full, LANES),
            sum_g=wide(mid, 9 * LANES),
            out_g=low(HALF, 9 * LANES),
            in_g=low(HALF, 9 * LANES),
            pile_g=low(depth, spa_size, LANES),
            r3_g=low(2, max(depth - 1, 1), spa_size, LANES),
            as_sem=sems(2, 4, 2),
            ar_sem=sems(2, 4, 2),
            gs_sem=sems(2, 4),
            gr_sem=sems(2, 4),
            g3_sem=sems(2, 2, depth),
        )
    names = list(ins) + list(outs) + list(scratch)
    results = pl.pallas_call(
        functools.partial(kernel, n, sizes, names),
        out_shape=list(outs.values()),
        in_specs=in_specs,
        out_specs=out_specs,
        scratch_shapes=list(scratch.values()) + piles,
        cost_estimate=pl.CostEstimate(
            flops=22 * 10**9, bytes_accessed=10**8, transcendentals=10**7
        ),
        compiler_params=pltpu.CompilerParams(
            collective_id=0, has_side_effects=True, vmem_limit_bytes=64 * 2**20 - 2**17
        ),
    )(*ins.values())
    return results[0], results[1], results[2], results[-1]


def on_device(n, share, frames, out_grad, seg_counts, *params):
    reducer, spatial, expander, squeezer, motion, context, gating, bias, norm = params
    _, segs, pixels, ch = frames.shape
    mid, red_w = reducer.shape[-1], squeezer.shape[-1]
    sizes = (ch, mid, red_w, segs, share)
    weights = SimpleNamespace(
        red=reducer[0],
        spa=spatial[0].transpose(1, 0, 2).reshape(9 * mid, mid),
        exp=expander[0],
        squ=squeezer[0],
        mot=motion[0].transpose(1, 0, 2).reshape(9 * red_w, red_w),
        con=context[0],
        gat=gating[0],
    )
    out, ing, land, gnorm = run(
        n,
        sizes,
        frames.transpose(0, 2, 1, 3),
        out_grad.transpose(0, 2, 1, 3),
        seg_counts,
        weights,
        bias,
        norm[0],
    )
    margin = plan(n, ch, mid, red_w, segs, share).margin
    window = land[margin : land.shape[0] - margin].astype(F32).reshape(-1, LANES)
    start = lax.rem(lax.axis_index("dp") * share, ROW * 16)
    flat = lax.dynamic_slice(window.reshape(1, -1), (0, start), (1, share))
    return (
        out.transpose(0, 2, 1, 3)[None],
        ing.transpose(0, 2, 1, 3)[None],
        flat,
        gnorm.reshape(norm.shape),
    )


def solution(mesh):
    n = mesh.shape["dp"]

    def whole(*args):
        entries = sum(item.size // item.shape[0] for item in args[3:11])
        share = up(entries, n) // n
        body = jax.shard_map(
            functools.partial(on_device, n, share),
            mesh=mesh,
            in_specs=(
                P("dp", None, None, None),
                P("dp", None, None, None),
                P("dp"),
                P("pipe", None, None),
                P("pipe", None, None, None),
                P("pipe", None, None),
                P("pipe", None, None),
                P("pipe", None, None, None),
                P("pipe", None, None),
                P("pipe", None, None),
                P("pipe", None),
                P("pipe", None, None),
            ),
            out_specs=(
                P("pipe", "dp", None, None, None),
                P("pipe", "dp", None, None, None),
                P("pipe", "dp"),
                P("pipe", None, None),
            ),
            check_vma=False,
        )
        return body(*args)

    return whole
```

```python
import functools
from types import SimpleNamespace

import jax
import jax.numpy as jnp
from jax import lax
from jax.experimental import pallas as pl
from jax.experimental.pallas import tpu as pltpu
from jax.sharding import PartitionSpec as P

SIDE = 7
PIX = 49
MICRO = 2
PIECES = 16
EPSILON = 1e-05
HIGH = lax.Precision.HIGHEST
BF = jnp.bfloat16
F32 = jnp.float32
MESH = pl.DeviceIdType.MESH
LANES = 128
GROUP = 4
HALF = 256
ROW = 512
GRID = SIDE + 2
WEIGHTS = ("red", "spa", "exp", "squ", "mot", "con", "gat")
SMALL = ("squ", "mot", "con", "gat")
COMPS = ("red", "spa", "exp", "small")
CHUNKS = ("e", "c", "d")
TAPS = dict(m=(0, 5), t=(5, 9))
ROWS = dict(c=(0, 1), d=(1, 2))
CUTS = 2
OPENS = dict(e=("exp", "small"), c=("red",), m=("spa",))
CLOSES = dict(e=("exp", "small"), d=("red",), t=("spa",))
RELAYED = ()
ORDER = (
    "s01", "x01", "s11", "x11", "s21", "x21", "s31", "x31", "m01", "w01", "w11", "w21", "w31",
    "a1", "b1", "q1", "l21", "y21", "m11", "Gs1", "Ge1", "z21", "p1", "v1", "l11", "y11",
    "g1", "0e1", "1e1", "z11", "o1", "i1", "Gc1", "r1", "Gb1", "s00", "x00", "s10", "0c1",
    "x10", "s20", "x20", "s30", "x30", "3b1", "2e1", "w00", "w10", "w20", "w30", "0d1", "a0",
    "1c1", "b0", "q0", "l20", "y20", "3e1", "1d1", "Ge0", "4b1", "Gs0", "2c1", "z20", "p0",
    "g0", "v0", "4e1", "l10", "0e0", "y10", "3c1", "2d1", "1e0", "Gb0", "3d1", "3b0", "z10",
    "o0", "Gc0", "4c1", "4d1", "0c0", "0d0", "2e0", "1d0", "3e0", "1c0", "2d0", "2c0", "3d0",
    "3c0", "i0", "4e0", "4c0", "4d0", "4b0",
)


def sigmoid(values):
    return 0.5 * jnp.tanh(0.5 * values) + 0.5


def silu_slope(values):
    sigma = sigmoid(values)
    return sigma * (1.0 + values * (1.0 - sigma))


def dot(a, b):
    return jnp.dot(a, b, preferred_element_type=F32)


def dot_nt(a, b):
    return lax.dot_general(a, b, (((1,), (1,)), ((), ())), preferred_element_type=F32)


def dot_tn(a, b):
    return lax.dot_general(a, b, (((0,), (0,)), ((), ())), preferred_element_type=F32)


def up(value, step):
    return -(-value // step) * step


def plan(n, ch, mid, red, segs, share):
    side = 4 if n % 64 == 0 else 2 if n % 4 == 0 else 1
    depth = n // (side * side)
    slots = PIECES // (side * side)
    levels = [(n, 1)] if n <= 16 else [(side * side, 1), (depth, side * side)]
    rows = dict(red=ch * mid // ROW, spa=9 * mid * mid // ROW, exp=mid * ch // ROW)
    small = mid * red + 9 * red * red + red * red + red * mid + mid
    small_rows = up(small, ROW) // ROW
    grouped = side == 2
    spa_size = rows["spa"] // (2 * depth if grouped else PIECES)
    parts = dict(
        red=(0, rows["red"] // PIECES),
        spa=(rows["red"], spa_size),
        exp=(rows["red"] + rows["spa"], rows["exp"] // PIECES),
        small=(rows["red"] + rows["spa"] + rows["exp"], up(up(small_rows, PIECES) // PIECES, 16)),
    )
    total = (parts["small"][0] + small_rows) * ROW
    margin = max(size for _, size in parts.values())
    reach = 1
    for comp, (start, size) in parts.items():
        for piece in range(rows[comp] // size if comp in rows else PIECES):
            first = (start + size * piece) * ROW
            if first < total:
                last = min((start + size * (piece + 1)) * ROW, total) - 1
                reach = max(reach, last // share - first // share + 1)
    land = margin + up(share // ROW + 22, 16) + margin
    return SimpleNamespace(
        side=side,
        depth=depth,
        slots=slots,
        levels=levels,
        parts=parts,
        total=total,
        margin=margin,
        reach=reach,
        grouped=grouped,
        land=land,
        small_rows=small_rows,
    )


def chunk_names(n):
    grouped = n % 64 and n % 4 == 0
    return CHUNKS if grouped else CHUNKS + tuple(TAPS)


def kernel(n, sizes, names, *refs):
    r = SimpleNamespace(**dict(zip(names, refs)))
    rest = refs[len(names) :]
    chunks = chunk_names(n)
    piles = {chunk: rest[6 * k : 6 * k + 6] for k, chunk in enumerate(chunks)}
    own_w = dict(
        red=r.in_red, spa=r.in_spa, exp=r.in_exp, squ=r.in_squ, mot=r.in_mot, con=r.in_con, gat=r.in_gat
    )
    sib_w = dict(
        red=r.sib_red, spa=r.sib_spa, exp=r.sib_exp, squ=r.sib_squ, mot=r.sib_mot, con=r.sib_con, gat=r.sib_gat
    )
    held_w = dict(red=r.red, spa=r.spa, exp=r.exp, squ=r.squ, mot=r.mot, con=r.con, gat=r.gat)
    chunk_refs = {
        chunk: SimpleNamespace(g=part[0], far=part[1], near=part[2], r1=part[3], r2=part[4], r3=part[5])
        for chunk, part in piles.items()
    }
    fin = dict(red=r.fin_red, spa=r.fin_spa, exp=r.fin_exp, small=r.fin_small)
    ch, mid, red_w, segs, share = sizes
    pp = plan(n, ch, mid, red_w, segs, share)
    side, depth, slots, levels, parts = pp.side, pp.depth, pp.slots, pp.levels, pp.parts
    grouped = pp.grouped
    rows = PIX * segs
    full = up(rows, 16)
    pad = full - rows
    c = lax.axis_index("pipe")
    i = lax.axis_index("dp")
    x = lax.rem(i, side)
    y = lax.rem(lax.div(i, side), side)
    z = lax.div(i, side * side)
    fc = x * (1 - c) + y * c
    gc = y * (1 - c) + x * c
    other = (1 - c, i)

    def remote(src, dst, send, recv, device):
        return pltpu.make_async_remote_copy(
            src_ref=src,
            dst_ref=dst,
            send_sem=send,
            recv_sem=recv,
            device_id=device,
            device_id_type=MESH,
        )

    def everybody(semaphore):
        def greet(k, _):
            peer = lax.rem(i + k, n)
            for core in (c, 1 - c):
                pl.semaphore_signal(
                    semaphore, inc=1, device_id=(core, peer), device_id_type=MESH
                )
            return 0

        pl.semaphore_signal(semaphore, inc=1, device_id=other, device_id_type=MESH)
        lax.fori_loop(1, n, greet, 0)

    barrier = pltpu.get_barrier_semaphore()
    everybody(barrier)

    count_own = r.counts[c]
    segment = lax.broadcasted_iota(jnp.int32, (segs, LANES), 0)

    def valid_for(count):
        return jnp.where(segment < count, 1.0, 0.0).astype(F32)

    valid = valid_for(count_own)
    paired = jnp.where(segment + 1 < count_own, 1.0, 0.0).astype(F32)
    pixels_own = PIX * count_own.astype(F32)

    stage = r.stage
    v = r.v
    free = r.nh3.at[1]

    def tile(j):
        return pl.ds(pl.multiple_of(j * LANES, LANES), LANES)

    def view(j, base=0):
        return (
            pl.ds(pl.multiple_of(base + lax.div(j, 4) * full, 16), rows),
            tile(lax.rem(j, 4)),
        )

    def loop(count, body):
        def step(j, _):
            body(j)
            return 0

        lax.fori_loop(0, count, step, 0)

    def packed(values):
        flat = values.reshape(rows, values.shape[-1])
        return jnp.concatenate([flat, jnp.zeros((pad, flat.shape[-1]), F32)], axis=0).astype(BF)

    def cube(values):
        return values.reshape(PIX, segs, values.shape[-1])

    def fold(values):
        return jnp.sum(jnp.sum(values, axis=0), axis=0, keepdims=True)

    def stage_to(slot, target):
        def body(j):
            target[:, tile(j)] = packed(stage[slot, :, :, tile(j)].astype(F32))

        loop(ch // LANES, body)

    def moments(values, mask=None, pixels=None):
        mask = valid if mask is None else mask
        pixels = pixels_own if pixels is None else pixels
        origin = values[0, 0:1, :]
        gaps = values - origin
        first = jnp.sum(mask * jnp.sum(gaps, axis=0), axis=0, keepdims=True)
        second = jnp.sum(mask * jnp.sum(gaps * gaps, axis=0), axis=0, keepdims=True)
        return first + pixels * origin, second - first * (first / pixels)

    load_frames = pltpu.make_async_copy(r.frames.at[c], stage.at[0], r.load_sem.at[0])
    load_frames.start()
    load_other = pltpu.make_async_copy(r.frames.at[1], stage.at[1], r.load_sem.at[1])
    pl.when(c == 0)(load_other.start)

    def weight_index(name):
        return WEIGHTS.index(name)

    def held_copy(source, name):
        return pltpu.make_async_copy(source, held_w[name], r.w_sem.at[weight_index(name)])

    def wait_weight(name):
        held_copy(own_w[name], name).wait()

    def first_send(name):
        k = weight_index(name)
        return remote(own_w[name], held_w[name], r.vs_sem.at[k], r.w_sem.at[k], other)

    def first_sends(*chosen):
        @pl.when(c == 0)
        def _():
            for name in chosen:
                first_send(name).start()

    def kept_send(name):
        k = weight_index(name)
        return remote(own_w[name], sib_w[name], r.ws_sem.at[k], r.wr_sem.at[k], other)

    def kept_sends(core):
        @pl.when(c == core)
        def _():
            for name in WEIGHTS:
                kept_send(name).start()

    def load_weight(name, s):
        @pl.when(c == s)
        def _():
            held_copy(own_w[name], name).start()

        @pl.when(c != s)
        def _():
            kept_send(name).wait_recv()
            held_copy(sib_w[name], name).start()

    @pl.when(c == 0)
    def _():
        for name in WEIGHTS:
            held_copy(own_w[name], name).start()

    own_params = [
        pltpu.make_async_copy(r.in_norm, r.norm.at[c], r.p_sem.at[0]),
        pltpu.make_async_copy(r.in_bias, r.bias.at[c], r.p_sem.at[1]),
    ]
    for copy in own_params:
        copy.start()

    r.grid[...] = jnp.zeros(r.grid.shape, F32)
    load_frames.wait()
    stage_to(0, v)
    msg, inbox = r.msg, r.inbox

    @pl.when(c == 0)
    def _():
        load_other.wait()
        stage_to(1, r.gz3)
        wait_weight("red")
        r.nh1[0] = dot(v[...], r.red[...])
        r.gs[0:full, :] = dot(r.gz3[...], r.red[...])
        count_other = r.counts[1]
        mask_other = valid_for(count_other)
        pixels_other = PIX * count_other.astype(F32)

        def body(j):
            for ref, target, with_other in (
                (r.nh1.at[0], msg.at[0, 0], ()),
                (r.gs, r.relay.at[0], (mask_other, pixels_other)),
            ):
                total, spread = moments(cube(ref[view(j)]), *with_other)
                target[pl.ds(j, 1), :] = total
                target[pl.ds(GROUP + j, 1), :] = spread

        loop(GROUP, body)

    pl.semaphore_wait(barrier, 2 * n - 1)

    param_sends = [
        remote(r.in_norm, r.norm.at[c], r.ps_sem.at[0], r.pr_sem.at[0], other),
        remote(r.in_bias, r.bias.at[c], r.ps_sem.at[1], r.pr_sem.at[1], other),
    ]
    for copy in param_sends:
        copy.start()

    def peer_of(level, k):
        size, stride = levels[level]
        here = lax.rem(lax.div(i, stride), size)
        return (c, i + (lax.rem(here + k, size) - here) * stride)

    def copies_of(bank, level):
        size, _ = levels[level]
        return [
            remote(
                msg.at[bank, level],
                inbox.at[bank, level, k],
                r.ms_sem.at[bank, level, k],
                r.mr_sem.at[bank, level, k],
                peer_of(level, k),
            )
            for k in range(1, size)
        ]

    def exchange_start(bank):
        for copy in copies_of(bank, 0):
            copy.start()

    def routed(core):
        size = levels[0][0]
        return [k for k in range(1, size) if (k % side == 0) == (core == 0)]

    def hand_over(bank):
        return remote(
            msg.at[bank, 0], r.relay.at[bank], r.hs_sem.at[bank], r.hr_sem.at[bank], other
        )

    def passed_on(bank, k):
        core, peer = peer_of(0, k)
        return remote(
            r.relay.at[bank],
            inbox.at[bank, 0, k],
            r.fs_sem.at[bank, k],
            r.mr_sem.at[bank, 0, k],
            (1 - core, peer),
        )

    def relay_start(bank):
        hand_over(bank).start()
        copies = copies_of(bank, 0)
        for core in range(2):

            @pl.when(c == core)
            def _():
                for k in routed(core):
                    copies[k - 1].start()

    def relay_pass(bank):
        hand_over(bank).wait_recv()
        for core in range(2):

            @pl.when(c == core)
            def _():
                for k in routed(core):
                    passed_on(bank, k).start()

    def exchange_finish(bank, combine, relayed=False, first=False):
        for level in range(len(levels)):
            copies = copies_of(bank, level)
            if level:
                for copy in copies:
                    copy.start()
            for copy in copies:
                copy.wait_recv()
            result = combine(bank, level)
            if level == 0 and relayed:
                hand_over(bank).wait_send()
                for core in range(2):

                    @pl.when(c == core)
                    def _():
                        for k in routed(core):
                            copies[k - 1].wait_send()
                            passed_on(bank, k).wait_send()
            elif level == 0 and first:

                @pl.when(c == 0)
                def _():
                    for k, copy in enumerate(copies):
                        copy.wait_send()
                        passed_on(bank, k + 1).wait_send()
                    for copy in first_moves:
                        copy.wait_send()
            else:
                for copy in copies:
                    copy.wait_send()
            if level + 1 < len(levels):
                msg[bank, level + 1] = result
        return result

    first_moves = [
        remote(r.relay.at[0], msg.at[0, 0], r.b_sem.at[0], r.b_sem.at[1], other),
        remote(r.gs.at[pl.ds(0, full)], r.nh1.at[0], r.b_sem.at[2], r.b_sem.at[3], other),
    ]

    @pl.when(c == 0)
    def _():
        exchange_start(0)
        for k in range(1, levels[0][0]):
            passed_on(0, k).start()
        for copy in first_moves:
            copy.start()

    cnt = r.cnt

    def count_copies(level):
        size, _ = levels[level]
        return [
            remote(
                cnt.at[level, 0],
                cnt.at[level, k],
                r.cs_sem.at[level, k],
                r.cr_sem.at[level, k],
                peer_of(level, k),
            )
            for k in range(1, size)
        ]

    cnt[0, 0] = jnp.full((8, LANES), pixels_own, F32)
    for copy in count_copies(0):
        copy.start()
    first_sends("spa", *SMALL)
    kept_sends(1)

    def count_finish():
        for level in range(len(levels)):
            copies = count_copies(level)
            if level:
                for copy in copies:
                    copy.start()
            total = cnt[level, 0]
            for k, copy in enumerate(copies):
                copy.wait()
                total = total + cnt[level, k + 1]
            if level + 1 < len(levels):
                cnt[level + 1, 0] = total
        r.total[...] = total

    def sum_combine(bank, level):
        total = msg[bank, level]
        for k in range(1, levels[level][0]):
            total = total + inbox[bank, level, k]
        return total

    def moment_combine(bank, level):
        size, _ = levels[level]
        nt = GROUP
        items = [msg[bank, level]] + [inbox[bank, level, k] for k in range(1, size)]
        counts = [cnt[level, k, 0:1, :] for k in range(size)]
        total = items[0][0:nt]
        count = counts[0]
        for k in range(1, size):
            total = total + items[k][0:nt]
            count = count + counts[k]
        mean = total / count
        spread = jnp.zeros_like(total)
        for k in range(size):
            gap = items[k][0:nt] / counts[k] - mean
            spread = spread + items[k][nt : 2 * nt] + counts[k] * gap * gap
        return jnp.concatenate([total, spread], axis=0)

    def norm_send(ref, block, bank):
        def body(j):
            total, spread = moments(cube(ref[view(block * GROUP + j)]))
            msg[bank, 0, pl.ds(j, 1), :] = total
            msg[bank, 0, pl.ds(GROUP + j, 1), :] = spread

        loop(GROUP, body)
        exchange_start(bank)

    def norm_receive(bank, s, block, row0, first=False):
        result = exchange_finish(bank, moment_combine, first=first)
        everyone = r.total[0:1, :]
        at = block * GROUP
        r.mean[at : at + GROUP, :] = result[0:GROUP] / everyone
        r.rstd[s, row0 + at : row0 + at + GROUP, :] = lax.rsqrt(
            result[GROUP : 2 * GROUP] / everyone + EPSILON
        )

    def gain_of(s, offset, j):
        lanes = pl.ds(pl.multiple_of(offset + j * LANES, LANES), LANES)
        return (r.norm[s, 0:1, lanes], r.norm[s, 1:2, lanes])

    def row_of(ref, j):
        return ref[pl.ds(j, 1), :]

    grid = r.grid

    def to_grid(values, lanes):
        for h in range(SIDE):
            at = ((h + 1) * GRID + 1) * segs
            grid[at : at + SIDE * segs, lanes] = values[h * SIDE * segs : (h + 1) * SIDE * segs]

    def patches(target, width, flip):
        def body(j):
            lanes = tile(j)
            for tap in range(9):
                down, right = tap // 3, tap % 3
                if flip:
                    down, right = 2 - down, 2 - right
                pieces = []
                for h in range(SIDE):
                    at = ((h + down) * GRID + right) * segs
                    pieces.append(grid[at : at + SIDE * segs, lanes])
                target[:, pl.ds(pl.multiple_of(tap * width + j * LANES, LANES), LANES)] = packed(
                    jnp.concatenate(pieces, axis=0)
                )

        loop(width // LANES, body)

    def put(slot, target, kind, s):
        @pl.when(c == s)
        def _():
            pltpu.make_async_copy(stage.at[slot], target.at[c], r.o_sem.at[kind, 0]).start()

        @pl.when(c != s)
        def _():
            remote(
                stage.at[slot],
                target.at[c],
                r.o_sem.at[kind, 1],
                r.o_sem.at[kind, 2],
                other,
            ).start()

    def put_wait(slot, target, kind, s):
        @pl.when(c == s)
        def _():
            pltpu.make_async_copy(stage.at[slot], target.at[c], r.o_sem.at[kind, 0]).wait()

        @pl.when(c != s)
        def _():
            remote(
                stage.at[slot],
                target.at[c],
                r.o_sem.at[kind, 1],
                r.o_sem.at[kind, 2],
                other,
            ).wait_send()

    n_mid = mid // LANES
    n_ch = ch // LANES
    n_blocks = ch // ROW

    def across(k):
        to_y = y + k // 2 - 2 * y * (k // 2)
        to_x = x + k % 2 - 2 * x * (k % 2)
        return to_y * 2 + to_x, (c, z * 4 + to_y * 2 + to_x)

    def act_move(s, k, half):
        lanes = pl.ds(half * HALF, HALF)
        sems = (r.as_sem.at[s, k, half], r.ar_sem.at[s, k, half])
        return remote(r.a1g.at[s, 0, :, lanes], r.a1g.at[s, k, :, lanes], *sems, across(k)[1])

    def grad_move(s, k):
        to_q, device = across(k)
        sems = (r.gs_sem.at[s, k], r.gr_sem.at[s, k])
        return remote(r.gz2q.at[to_q], r.gzg.at[s, k - 1], *sems, device)

    def act_moves(*chosen):
        if grouped:
            for move in chosen:
                act_move(*move).start()

    for copy in own_params:
        copy.wait()
    for s in range(2):
        nh1, nh2, nh3 = r.nh1.at[s], r.nh2.at[s], r.nh3.at[s]
        if s == 0:
            load_weight("red", 1)
            for copy in param_sends:
                copy.wait_recv()

            @pl.when(c == 1)
            def _():
                for copy in first_moves:
                    copy.wait_recv()

            count_finish()
        else:
            wait_weight("red")
            nh1[...] = dot(v[...], r.red[...])
            kept_sends(0)
            norm_send(nh1, 0, 0)
            act_moves((0, 3, 0))
        norm_receive(0, s, 0, 0, s == 0)

        def act_one(j, s=s, nh1=nh1):
            gain, offset = gain_of(s, 0, j)
            normed = (nh1[view(j)] - row_of(r.mean, j)) * row_of(r.rstd.at[s], j)
            nh1[view(j)] = normed
            before = normed * gain + offset
            act = before * sigmoid(before)
            r.a1g[s, 0, :, tile(j)] = packed(act)
            to_grid(act, tile(j))

        loop(n_mid, act_one)
        patches(r.patch, mid, False)
        wait_weight("spa")
        nh2[...] = dot(r.patch[...], r.spa[...])
        if s == 0:
            first_sends("exp")
            load_weight("spa", 1)
        norm_send(nh2, 0, 1)
        if s == 0:
            act_moves((0, 1, 0), (0, 2, 0))
        else:
            act_moves((0, 3, 1), (1, 1, 0), (1, 2, 0))
        norm_receive(1, s, 0, n_mid)

        def act_two(j, s=s, nh2=nh2):
            gain, offset = gain_of(s, mid, j)
            normed = (nh2[view(j)] - row_of(r.mean, j)) * row_of(r.rstd.at[s], n_mid + j)
            nh2[view(j)] = normed
            before = normed * gain + offset
            r.h2[s, :, tile(j)] = packed(before * sigmoid(before))

        loop(n_mid, act_two)
        for name in SMALL:
            wait_weight(name)
        squeezed = cube(dot(r.h2[s], r.squ[...])[:rows])
        later = pltpu.roll(squeezed, segs - 1, 1)
        field = (paired * (later - squeezed)).reshape(rows, red_w)
        r.field[s] = packed(field)
        rounded = r.field[s].astype(F32)[:rows]
        to_grid(rounded, pl.ds(0, LANES))
        patches(r.patch_m, red_w, False)
        context_mean = jnp.sum(cube(rounded), axis=0) * (1.0 / PIX)
        r.cmean[s] = context_mean
        from_mean = jnp.dot(
            context_mean, r.con[...].astype(F32), precision=HIGH, preferred_element_type=F32
        )
        mixed = cube(dot(r.patch_m[...], r.mot[...])[:rows]) + from_mean
        r.score[s] = packed(mixed)
        free[0:full, :] = dot(r.score[s], r.gat[...])

        def gate(j, s=s):
            bias = r.bias[s, 0:1, tile(j)]
            sigma = sigmoid(free[view(j)] + bias)
            r.sigma[s, :, tile(j)] = packed(sigma)
            h2 = r.h2[s, :, tile(j)].astype(F32)[:rows]
            r.gated[s, :, tile(j)] = packed(h2 * (0.5 + sigma))

        loop(n_mid, gate)
        if s == 0:
            for name in SMALL:
                load_weight(name, 1)
        wait_weight("exp")
        for block in range(n_blocks):
            nh3[block * full : (block + 1) * full, :] = dot(
                r.gated[s], r.exp[:, block * ROW : (block + 1) * ROW]
            )
            norm_send(nh3, block, 2 + block)
        act_moves((s, 1, 1), (s, 2, 1))
        if s == 0:
            load_weight("exp", 1)
        slot = 1 - s

        def finish(j, s=s, nh3=nh3, slot=slot):
            gain, offset = gain_of(s, 2 * mid, j)
            normed = (nh3[view(j)] - row_of(r.mean, j)) * row_of(
                r.rstd.at[s], 2 * n_mid + j
            )
            nh3[view(j)] = normed
            before = v[:, tile(j)].astype(F32)[:rows] + normed * gain + offset
            out = cube(before * sigmoid(before)) * valid
            stage[slot, :, :, tile(j)] = out.astype(BF)
            if s == 0:
                v[:, tile(j)] = packed(out)

        for block in range(n_blocks):
            norm_receive(2 + block, s, block, 2 * n_mid)
            loop(GROUP, lambda j, block=block: finish(block * GROUP + j))
        put(slot, r.out, s, s)
        if s == 0:
            put_wait(slot, r.out, 0, 0)
            load_grad = pltpu.make_async_copy(r.out_grad.at[c], stage.at[1], r.load_sem.at[1])
            load_grad.start()

    def send_sem(chunk, s, k):
        return r.rs_send.at[s, chunks.index(chunk), k]

    def recv_sem(chunk, s, k):
        return r.rs_recv.at[s, chunks.index(chunk), k]

    def add_loop(target, others, pieces):
        def body(j):
            at = target.at[j]
            total = at[...]
            for item in others:
                total = total + item.at[j][...]
            at[...] = total

        loop(pieces, body)

    def along(to):
        px = to * (1 - c) + x * c
        py = y * (1 - c) + to * c
        return z * side * side + py * side + px

    def rs0(chunk, s):
        ref = chunk_refs[chunk]
        found = []
        for k in range(1, side):
            sems = (send_sem(chunk, s, k), recv_sem(chunk, s, k))
            source = ref.g.at[1 - c, lax.rem(gc + k, side)]
            found.append(remote(source, ref.far.at[s * grouped, k - 1], *sems, other))
        sems = (send_sem(chunk, s, 0), recv_sem(chunk, s, 0))
        return found, remote(ref.g.at[c, fc], ref.near.at[s * grouped], *sems, other)

    def rs1(chunk, s):
        ref = chunk_refs[chunk]
        found = []
        for k in range(1, side):
            at = side - 1 + k
            sems = (send_sem(chunk, s, at), recv_sem(chunk, s, at))
            device = (1 - c, along(lax.rem(fc + k, side)))
            found.append(remote(ref.far.at[s * grouped, k - 1], ref.r1.at[s * grouped, k - 1], *sems, device))
        return found

    def rs2(chunk, s):
        ref = chunk_refs[chunk]
        found = []
        for k in range(1, side):
            to = lax.rem(fc + k, side)
            at = 2 * (side - 1) + k
            sems = (send_sem(chunk, s, at), recv_sem(chunk, s, at))
            found.append(remote(ref.near.at[s * grouped, to], ref.r2.at[s * grouped, k - 1], *sems, (c, along(to))))
        return found

    def rs3(chunk, s):
        ref = chunk_refs[chunk]
        found = []
        for k in range(1, depth):
            to = lax.rem(z + k, depth)
            at = 3 * (side - 1) + k
            sems = (send_sem(chunk, s, at), recv_sem(chunk, s, at))
            source = ref.near.at[s * grouped, fc, lax.rem(to, slots)]
            device = (c, to * side * side + y * side + x)
            found.append((to, remote(source, ref.r3.at[s * grouped, k - 1], *sems, device)))
        return found

    def credit(chunk):
        return r.credit.at[chunks.index(chunk)]

    def rs0_start(chunk, s):
        if s == 0 and not grouped:
            pl.semaphore_wait(credit(chunk), 1)
        far, near = rs0(chunk, s)
        for copy in far:
            copy.start()
        near.start()

    def rs1_start(chunk, s):
        ref = chunk_refs[chunk]
        far, near = rs0(chunk, s)
        for k, copy in enumerate(far):
            copy.wait()
            to = lax.rem(fc + k + 1, side)
            for b in range(side):
                add_loop(ref.far.at[s * grouped, k, b], [ref.g.at[c, to, b]], slots)
        for copy in rs1(chunk, s):
            copy.start()
        near.wait()
        for b in range(side):
            add_loop(ref.near.at[s * grouped, b], [ref.g.at[1 - c, gc, b]], slots)

    def rs2_start(chunk, s):
        ref = chunk_refs[chunk]
        copies = rs1(chunk, s)
        for copy in copies:
            copy.wait_recv()
        for b in range(side):
            add_loop(ref.near.at[s * grouped, b], [ref.r1.at[s * grouped, k, b] for k in range(side - 1)], slots)
        for copy in copies:
            copy.wait_send()
        for copy in rs2(chunk, s):
            copy.start()

    def rs3_start(chunk, s):
        ref = chunk_refs[chunk]
        copies = rs2(chunk, s)
        for copy in copies:
            copy.wait_recv()
        add_loop(ref.near.at[s * grouped, fc], [ref.r2.at[s * grouped, k] for k in range(side - 1)], slots)
        for copy in copies:
            copy.wait_send()
        for to, copy in rs3(chunk, s):
            if slots == depth:
                copy.start()
            else:
                pl.when(to < slots)(copy.start)

    def block_rows(comp):
        size = parts[comp][1]
        return size if size % 96 and size < 128 else 96 if size % 96 == 0 else size // 2

    def owner_range(at, size):
        return lax.div(at * ROW, share), lax.div(jnp.minimum((at + size) * ROW, pp.total) - 1, share)

    def send_piece(comp, s, action):
        start, size = parts[comp]
        by_chip = grouped and comp == "spa"
        piece = c * depth + z if by_chip else i
        width = fin[comp].shape[1]
        part = lax.rem(i, side * side) if by_chip else 1 - c
        lanes = pl.ds(pl.multiple_of(part * width, width), width)
        which = COMPS.index(comp)
        step = block_rows(comp)
        count = size // step
        for b in range(count):
            at = start + size * piece + step * b
            first, last = owner_range(at, step)
            exists = jnp.logical_and(i < PIECES, at * ROW < pp.total)
            slot = lax.rem(piece * count + b, 16)
            source = fin[comp].at[pl.ds(b * step, step)]
            for k in range(pp.reach):
                to = first + k
                base = lax.div(to * share, ROW * 16) * 16
                row = pl.multiple_of(pp.margin + at - base, 16)
                there = r.land.at[pl.ds(row, step), lanes]
                needed = jnp.logical_and(exists, to <= last)
                here = jnp.logical_and(c == s, to == i)
                arrival = r.land_sem.at[which, slot, part]

                @pl.when(jnp.logical_and(needed, here))
                def _():
                    copy = pltpu.make_async_copy(source, there, arrival)
                    if action == "start":
                        copy.start()
                    else:
                        copy.wait()

                @pl.when(jnp.logical_and(needed, jnp.logical_not(here)))
                def _():
                    copy = remote(source, there, r.fin_sem.at[which, b, k], arrival, (s, to))
                    if action == "start":
                        copy.start()
                    else:
                        copy.wait_send()

    def arrivals(comp):
        start, size = parts[comp]
        by_chip = grouped and comp == "spa"
        width = fin[comp].shape[1]
        step = block_rows(comp)
        count = size // step
        which = COMPS.index(comp)
        low = i * share
        high = jnp.minimum(low + share, pp.total)
        before = jnp.maximum(lax.div(low, ROW) - start, 0)
        first = lax.div(before, step)
        blocks = (2 * depth if by_chip else PIECES) * count

        def arrive(k, _):
            block = first + k
            at = start + step * block
            piece = lax.div(block, count)
            near = jnp.logical_and(at * ROW < high, (at + step) * ROW > low)
            near = jnp.logical_and(near, block < blocks)
            for part in range(ROW // width):
                core = lax.div(piece, depth) if by_chip else 1 - part
                chip = lax.rem(piece, depth) * side * side + part if by_chip else piece
                own = jnp.logical_and(c == core, i == chip)

                @pl.when(jnp.logical_and(near, jnp.logical_not(own)))
                def _():
                    pltpu.make_async_copy(
                        fin[comp].at[pl.ds(0, step)],
                        r.land.at[pl.ds(0, step), pl.ds(0, width)],
                        r.land_sem.at[which, lax.rem(block, 16), part],
                    ).wait()

            return 0

        lax.fori_loop(0, min(share // (ROW * step) + 3, 16), arrive, 0)

    def finish_chunk(chunk, s):
        ref = chunk_refs[chunk]
        own = ref.near.at[s * grouped, fc]
        r3 = ref.r3
        copies = rs3(chunk, s)
        cins = mid // PIECES
        if s == 0 and chunk in OPENS:
            for comp in OPENS[chunk]:
                send_piece(comp, 1, "wait")

        def work():
            for _, copy in copies:
                copy.wait_recv()
            mine = own.at[lax.rem(z, slots)]

            def summed(first, count):
                total = mine[first : first + count, :].astype(F32)
                for k in range(depth - 1):
                    total = total + r3[s * grouped, k, first : first + count, :].astype(F32)
                return total

            def weave(mix, first, count, stride, value):
                for k in range(HALF // LANES):
                    mix[k, pl.ds(first, count, stride=stride), :] = value[
                        :, k * LANES : (k + 1) * LANES
                    ]

            def woven(mix, target, size):
                for k in range(HALF // LANES):
                    target[:, k * LANES : (k + 1) * LANES] = mix[k, 0:size, :].astype(BF)

            if chunk == "e":
                size = parts["exp"][1]
                quarters = size // cins
                for q in range(quarters):
                    weave(r.mix_e, q, cins, quarters, summed(q * cins, cins))
                woven(r.mix_e, r.fin_exp, size)
                r.fin_small[...] = summed(size, parts["small"][1]).astype(BF)
            elif chunk in TAPS:
                first, end = TAPS[chunk]
                for tap in range(first, end):
                    weave(r.mix, tap, cins, 9, summed((tap - first) * cins, cins))
                if end == 9:
                    woven(r.mix, r.fin_spa, parts["spa"][1])
            else:
                first, end = (k * parts["red"][1] // CUTS for k in ROWS[chunk])
                r.fin_red[first:end, :] = summed(0, end - first).astype(BF)

        if slots == depth:
            work()
        else:
            pl.when(z < slots)(work)
        for to, copy in copies:
            if slots == depth:
                copy.wait_send()
            else:
                pl.when(to < slots)(copy.wait_send)
        if s == 1 and not grouped:
            pl.semaphore_signal(credit(chunk), inc=1, device_id=other, device_id_type=MESH)
        for comp in CLOSES.get(chunk, ()):
            send_piece(comp, s, "start")

    def place(half, piece):
        px, py, pz = piece % side, (piece // side) % side, piece // (side * side)
        return (half, px, py, pz) if half == 0 else (half, py, px, pz)

    small_at = 2 * full

    def grads_e(s):
        cins = mid // PIECES
        g = chunk_refs["e"].g
        for q in range(ch // ROW):
            for half in range(2):
                lanes = slice(q * ROW + half * HALF, q * ROW + (half + 1) * HALF)
                value = dot_tn(r.gated[s], r.gz3[:, lanes]).astype(BF)
                for piece in range(PIECES):
                    where = place(half, piece)
                    g[where + (slice(q * cins, (q + 1) * cins),)] = value[
                        piece * cins : (piece + 1) * cins
                    ]

    def grads_small(s):
        g = chunk_refs["e"].g
        tmp = r.tmp1
        at = small_at
        per = ROW // LANES

        def spread(count):
            for q in range(per):
                free[at : at + count, q * LANES : (q + 1) * LANES] = tmp[
                    pl.ds(q, count, stride=per), :
                ]

        tmp[0:mid, :] = dot_tn(r.h2[s], r.gr[...])
        spread(mid // per)
        at += mid // per
        moved = dot_tn(r.field[s], r.patch_m[...])
        for tap in range(9):
            tmp[pl.ds(tap, red_w, stride=9), :] = moved[:, tap * LANES : (tap + 1) * LANES]
        spread(9 * red_w // per)
        at += 9 * red_w // per
        tmp[0:red_w, :] = lax.dot_general(
            r.cmean[s],
            r.ssum[...],
            (((0,), (0,)), ((), ())),
            precision=HIGH,
            preferred_element_type=F32,
        )
        spread(red_w // per)
        at += red_w // per
        free[at : at + red_w, :] = dot_tn(r.score[s], r.gl[...])
        at += red_w
        free[at : at + 8, :] = jnp.broadcast_to(r.gbias[...], (8, mid))
        start = parts["exp"][1]
        size = parts["small"][1]
        used = -(-pp.small_rows // size)
        for piece in range(PIECES):
            for half in range(2):
                where = place(half, piece) + (slice(start, start + size),)
                if piece < used:
                    g[where] = free[
                        small_at + piece * size : small_at + (piece + 1) * size,
                        half * HALF : (half + 1) * HALF,
                    ].astype(BF)
                else:
                    g[where] = jnp.zeros((size, HALF), BF)

    def grads_taps(chunk, s):
        cins = mid // PIECES
        g = chunk_refs[chunk].g
        first, end = TAPS[chunk]

        def body(tap):
            for half in range(2):
                lanes = pl.ds(pl.multiple_of((first + tap) * mid + half * HALF, HALF), HALF)
                value = dot_tn(r.a1g[s, 0], r.patch[:, lanes]).astype(BF)
                for piece in range(PIECES):
                    where = place(half, piece)
                    g[where + (pl.ds(pl.multiple_of(tap * cins, cins), cins),)] = value[
                        piece * cins : (piece + 1) * cins
                    ]

        loop(end - first, body)

    def grads_group(s):
        for k in range(4):
            if k:
                act_move(s, k, 0).wait_recv()
                act_move(s, k, 1).wait_recv()
                grad_move(s, k).wait_recv()
                grad = r.gzg[s, k - 1]
            else:
                grad = r.gz2q[lax.rem(i, 4)]
            to_grid(grad.astype(F32)[:rows], pl.ds(0, LANES))
            patches(r.patch.at[:, pl.ds(k * 9 * LANES, 9 * LANES)], LANES, True)
        def product(half):
            lanes = pl.ds(pl.multiple_of(half * HALF, HALF), HALF)
            total = None
            for k in range(4):
                part = dot_tn(
                    r.a1g[s, k, :, lanes], r.patch[:, k * 9 * LANES : (k + 1) * 9 * LANES]
                )
                total = part if total is None else total + part
            return total

        r.out_g[...] = product(1 - c).astype(BF)
        if s == 0:
            pl.semaphore_wait(r.credit.at[len(chunks)], 1)
        group_swap(s).start()
        r.sum_g[...] = product(c)

    def group_swap(s):
        return remote(r.out_g, r.in_g, r.g3_sem.at[s, 0, 0], r.g3_sem.at[s, 1, 0], other)

    def group_moves(s):
        found = []
        for k in range(1, depth):
            to = lax.rem(z + k, depth)
            device = (c, to * 4 + lax.rem(i, 4))
            found.append(
                remote(
                    r.pile_g.at[to],
                    r.r3_g.at[s, k - 1],
                    r.g3_sem.at[s, 0, k],
                    r.g3_sem.at[s, 1, k],
                    device,
                )
            )
        return found

    def group_start(s):
        cins = HALF // depth
        group_swap(s).wait()
        for to in range(depth):
            at = slice(to * cins, (to + 1) * cins)
            for tap in range(9):
                lanes = slice(tap * LANES, (tap + 1) * LANES)
                theirs = r.in_g[to * cins : (to + 1) * cins, lanes].astype(F32)
                value = r.sum_g[at, lanes] + theirs
                r.pile_g[to, tap * cins : (tap + 1) * cins, :] = value.astype(BF)
        if s == 1:
            pl.semaphore_signal(
                r.credit.at[len(chunks)], inc=1, device_id=other, device_id_type=MESH
            )
        for copy in group_moves(s):
            copy.start()

    def group_finish(s):
        cins = HALF // depth
        copies = group_moves(s)
        for copy in copies:
            copy.wait_recv()
        for tap in range(9):
            at = slice(tap * cins, (tap + 1) * cins)
            total = r.pile_g[z, at, :].astype(F32)
            for k in range(depth - 1):
                total = total + r.r3_g[s, k, at, :].astype(F32)
            r.mix[0, pl.ds(tap, cins, stride=9), :] = total
        if s == 0:
            send_piece("spa", 1, "wait")
        r.fin_spa[...] = r.mix[0].astype(BF)
        for copy in copies:
            copy.wait_send()
        send_piece("spa", s, "start")

    def grads_c(s):
        size = parts["red"][1]
        for half in range(2):
            value = dot_tn(v[...], r.gz1[:, half * HALF : (half + 1) * HALF]).astype(BF)
            for chunk, cut in ROWS.items():
                first, end = (k * size // CUTS for k in cut)
                for piece in range(PIECES):
                    chunk_refs[chunk].g[place(half, piece)] = value[
                        piece * size + first : piece * size + end
                    ]

    def back_receive(bank, s, block, row0, relayed=True):
        result = exchange_finish(bank, sum_combine, relayed)
        half_rows = 2 * n_mid + n_ch
        at = row0 + block * GROUP
        r.gnorm[s, at : at + GROUP, :] = result[GROUP : 2 * GROUP]
        r.gnorm[s, half_rows + at : half_rows + at + GROUP, :] = result[0:GROUP]
        r.bsum[block] = result / r.total[0:1, :]

    def norm_grad(grad, normed, s, offset, row0, j):
        gain, _ = gain_of(s, offset, j)
        scale = gain * row_of(r.rstd.at[s], row0 + j)
        means = r.bsum.at[lax.div(j, GROUP)]
        mean_grad = row_of(means, lax.rem(j, GROUP))
        mean_cross = row_of(means, GROUP + lax.rem(j, GROUP))
        return scale * (cube(grad) - valid * (mean_grad + cube(normed) * mean_cross))

    def slope(s, grad_at, normed_ref, offset, bank):
        def body(j):
            gain, shift = gain_of(s, offset, j)
            normed = normed_ref[view(j)]
            grad = free[view(j, grad_at)] * silu_slope(normed * gain + shift)
            free[view(j, grad_at)] = grad
            msg[bank, 0, pl.ds(j, 1), :] = fold(cube(grad))
            msg[bank, 0, pl.ds(GROUP + j, 1), :] = fold(cube(grad * normed))

        loop(GROUP, body)

    gs = r.gs
    reload = pltpu.make_async_copy(r.frames.at[c], stage.at[1], r.load_sem.at[0])

    def bank_three(s, block):
        return 2 + n_blocks * s + block

    def back_three(s, block):
        if s == 1 and block == 0:
            load_grad.wait()
        nh3 = r.nh3.at[s]
        bank = bank_three(s, block)

        def body(j):
            at = block * GROUP + j
            gain, shift = gain_of(s, 2 * mid, at)
            normed = nh3[view(at)]
            before = v[:, tile(at)].astype(F32)[:rows] + normed * gain + shift
            grad = cube(silu_slope(before)) * valid * stage[s, :, :, tile(at)].astype(F32)
            gs[view(at)] = grad.reshape(rows, LANES)
            msg[bank, 0, pl.ds(j, 1), :] = fold(grad)
            msg[bank, 0, pl.ds(GROUP + j, 1), :] = fold(grad * cube(normed))

        loop(GROUP, body)

    def send_sums(bank, relayed):
        if relayed:
            relay_start(bank)
            relay_pass(bank)
        else:
            exchange_start(bank)

    def grad_three(s, block, relayed):
        nh3 = r.nh3.at[s]
        back_receive(bank_three(s, block), s, block, 2 * n_mid, relayed)

        def body(j):
            at = block * GROUP + j
            r.gz3[:, tile(at)] = packed(
                norm_grad(gs[view(at)], nh3[view(at)], s, 2 * mid, 2 * n_mid, at)
            )

        loop(GROUP, body)

    def back_expander(s):
        if s == 0:
            wait_weight("exp")
        free[0:full, :] = dot_nt(r.gz3[...], r.exp[...])
        if s == 1:
            load_weight("exp", 0)

    def back_gate(s):
        def body(j):
            grad = free[view(j)]
            sigma = r.sigma[s, :, tile(j)].astype(F32)[:rows]
            h2 = r.h2[s, :, tile(j)].astype(F32)[:rows]
            free[view(j, full)] = grad * (0.5 + sigma)
            value = packed(grad * h2 * sigma * (1.0 - sigma))
            r.gl[:, tile(j)] = value
            r.gbias[0:1, tile(j)] = fold(cube(value.astype(F32)[:rows]))

        loop(n_mid, body)

    def back_motion(s):
        if s == 0:
            for name in SMALL:
                wait_weight(name)
        r.gq[...] = dot_nt(r.gl[...], r.gat[...]).astype(BF)
        rounded = r.gq[...].astype(F32)[:rows]
        to_grid(rounded, pl.ds(0, LANES))
        patches(r.patch_m, red_w, True)
        score_sums = jnp.sum(cube(rounded), axis=0)
        r.ssum[...] = score_sums
        grad_field = None
        for tap in range(9):
            part = dot_nt(
                r.patch_m[:, tap * red_w : (tap + 1) * red_w],
                r.mot[tap * red_w : (tap + 1) * red_w, :],
            )
            grad_field = part if grad_field is None else grad_field + part
        from_mean = lax.dot_general(
            score_sums,
            r.con[...].astype(F32),
            (((1,), (1,)), ((), ())),
            precision=HIGH,
            preferred_element_type=F32,
        ) * (1.0 / PIX)
        weighted = paired * (cube(grad_field[:rows]) + from_mean)
        r.gr[...] = packed(pltpu.roll(weighted, 1, 1) - weighted)
        free[full : 2 * full, :] += dot_nt(r.gr[...], r.squ[...])
        if s == 1:
            for name in SMALL:
                load_weight(name, 0)

    def back_spread(s):
        nh2 = r.nh2.at[s]

        def body(j):
            value = norm_grad(free[view(j, full)], nh2[view(j)], s, mid, n_mid, j)
            to_grid(value.reshape(rows, LANES), tile(j))
            if grouped:
                r.gz2q[j] = packed(value)

        if grouped and s == 0:
            for k in range(1, 4):
                grad_move(1, k).wait_send()
        loop(n_mid, body)
        patches(r.patch, mid, True)

    def back_conv(s):
        if s == 0:
            wait_weight("spa")
        acc = None
        for tap in range(9):
            part = dot_nt(
                r.patch[:, tap * mid : (tap + 1) * mid], r.spa[tap * mid : (tap + 1) * mid, :]
            )
            acc = part if acc is None else acc + part
        free[0:full, :] = acc
        if s == 1:
            load_weight("spa", 0)

    def grad_one(s):
        nh1 = r.nh1.at[s]

        def body(j):
            r.gz1[:, tile(j)] = packed(norm_grad(free[view(j)], nh1[view(j)], s, 0, 0, j))

        loop(n_mid, body)

    def back_input(s):
        if s == 1:
            put_wait(0, r.out, 1, 1)
            reload.start()
        else:
            wait_weight("red")
        for block in range(n_blocks):
            value = gs[block * full : block * full + rows, :] + dot_nt(
                r.gz1[...], r.red[block * ROW : (block + 1) * ROW, :]
            )[:rows]
            stage[1 - s, :, :, block * ROW : (block + 1) * ROW] = cube(value).astype(BF)
        put(1 - s, r.ing, 2 + s, s)
        if s == 1:
            load_weight("red", 0)

    def back_reload(s):
        reload.wait()
        stage_to(1, v)

    def perform(token):
        op, s = token[:-1], int(token[-1])
        kind, rest = op[0], op[1:]
        if kind == "s":
            back_three(s, int(rest))
        elif kind == "x":
            send_sums(bank_three(s, int(rest)), kind + token[-1] in RELAYED)
        elif kind == "w":
            grad_three(s, int(rest), "x" + token[-1] in RELAYED)
        elif kind == "y":
            send_sums(int(rest) - 1, token in RELAYED)
        elif op == "z2":
            back_receive(1, s, 0, n_mid, "y" + token[1:] in RELAYED)
        elif op == "z1":
            back_receive(0, s, 0, 0, "y" + token[1:] in RELAYED)
        elif op == "g":
            if grouped:
                for k in range(1, 4):
                    grad_move(s, k).start()
        elif kind == "m":
            act_moves((s, 3, int(rest)))
        elif rest == "b" and grouped:
            if kind == "G":
                grads_group(s)
            elif kind == "3":
                group_start(s)
            else:
                group_finish(s)
        elif rest == "b":
            for chunk in TAPS:
                if kind == "G":
                    grads_taps(chunk, s)
                    rs0_start(chunk, s)
                    rs1_start(chunk, s)
                    rs2_start(chunk, s)
                elif kind == "3":
                    rs3_start(chunk, s)
                else:
                    finish_chunk(chunk, s)
        elif kind == "G":
            if rest == "e":
                grads_e(s)
            elif rest == "s":
                grads_small(s)
            else:
                grads_c(s)
        elif kind == "0":
            rs0_start(rest, s)
        elif kind == "1":
            rs1_start(rest, s)
        elif kind == "2":
            rs2_start(rest, s)
        elif kind == "3":
            rs3_start(rest, s)
        elif kind == "4":
            finish_chunk(rest, s)
        elif op == "l2":
            slope(s, full, r.nh2.at[s], mid, 1)
        elif op == "l1":
            slope(s, 0, r.nh1.at[s], 0, 0)
        else:
            table[op](s)

    table = dict(
        a=back_expander,
        b=back_gate,
        q=back_motion,
        p=back_spread,
        v=back_conv,
        o=grad_one,
        i=back_input,
        r=back_reload,
    )
    if grouped:
        for token in ORDER:
            perform(token)
    else:
        for token in ORDER:
            if token[-1] == "1":
                perform(token)
        everybody(r.between.at[0])
        pl.semaphore_wait(r.between.at[0], 2 * n - 1)
        for token in ORDER:
            if token[-1] == "0":
                perform(token)

    gn_send = remote(
        r.gnorm.at[1 - c], r.gnorm_in, r.gn_sem.at[0], r.gn_sem.at[1], other
    )
    gn_send.start()
    gn_send.wait()
    r.gnorm_out[...] = r.gnorm[c] + r.gnorm_in[...]

    if grouped:
        for k in range(1, 4):
            for s in range(2):
                act_move(s, k, 0).wait_send()
                act_move(s, k, 1).wait_send()
            grad_move(0, k).wait_send()
    for copy in param_sends:
        copy.wait_send()
    for name in WEIGHTS:
        kept_send(name).wait_send()

    @pl.when(c == 0)
    def _():
        for name in WEIGHTS[1:]:
            first_send(name).wait_send()

    put_wait(0, r.ing, 3, 1)
    put_wait(1, r.ing, 2, 0)
    for base, target in ((0, r.out), (2, r.ing)):
        for s in range(2):

            @pl.when(c == s)
            def _():
                remote(
                    stage.at[0],
                    target.at[1 - c],
                    r.o_sem.at[base + s, 1],
                    r.o_sem.at[base + s, 2],
                    other,
                ).wait_recv()

    for comp in COMPS:
        send_piece(comp, 0, "wait")
    for comp in COMPS:
        arrivals(comp)


def run(n, sizes, frames, out_grad, seg_counts, weights, bias, norm):
    ch, mid, red_w, segs, share = sizes
    pp = plan(n, ch, mid, red_w, segs, share)
    side, depth, slots, levels, parts = pp.side, pp.depth, pp.slots, pp.levels, pp.parts
    rows = PIX * segs
    full = up(rows, 16)
    norm_rows = 2 * (2 * mid + ch) // LANES
    group = max(size for size, _ in levels)
    any_spec = pl.BlockSpec(memory_space=pl.ANY)
    vmem_spec = pl.BlockSpec(memory_space=pltpu.VMEM)

    ins = dict(
        frames=frames,
        out_grad=out_grad,
        in_red=weights.red,
        in_spa=weights.spa,
        in_exp=weights.exp,
        in_squ=weights.squ,
        in_mot=weights.mot,
        in_con=weights.con,
        in_gat=weights.gat,
        counts=seg_counts,
        in_bias=bias,
        in_norm=norm,
    )
    in_specs = [any_spec] * 9 + [pl.BlockSpec(memory_space=pltpu.SMEM), any_spec, any_spec]

    def like(item):
        return jax.ShapeDtypeStruct(item.shape, item.dtype)

    outs = dict(
        out=like(frames),
        ing=like(frames),
        land=jax.ShapeDtypeStruct((pp.land, ROW), BF),
        sib_red=like(weights.red),
        sib_spa=like(weights.spa),
        sib_exp=like(weights.exp),
        sib_squ=like(weights.squ),
        sib_mot=like(weights.mot),
        sib_con=like(weights.con),
        sib_gat=like(weights.gat),
        gnorm_out=jax.ShapeDtypeStruct((norm_rows, LANES), F32),
    )
    out_specs = [any_spec] * 10 + [vmem_spec]

    def low(*dims):
        return pltpu.VMEM(dims, BF)

    def wide(*dims):
        return pltpu.VMEM(dims, F32)

    def sems(*dims):
        return pltpu.SemaphoreType.DMA(dims)

    def piled(size):
        return (
            low(2, side, side, slots, size, HALF),
            low(1 + pp.grouped, max(side - 1, 1), side, slots, size, HALF),
            low(1 + pp.grouped, side, slots, size, HALF),
            low(1 + pp.grouped, max(side - 1, 1), side, slots, size, HALF),
            low(1 + pp.grouped, max(side - 1, 1), slots, size, HALF),
            low(1 + pp.grouped, max(depth - 1, 1), size, HALF),
        )

    cins = mid // PIECES
    sizes_of = dict(e=parts["exp"][1] + parts["small"][1])
    for chunk, (first, end) in TAPS.items():
        sizes_of[chunk] = (end - first) * cins
    for chunk, (first, end) in ROWS.items():
        sizes_of[chunk] = (end - first) * parts["red"][1] // CUTS
    chunks = chunk_names(n)
    piles = [item for chunk in chunks for item in piled(sizes_of[chunk])]
    spa_width = LANES if pp.grouped else HALF
    spa_size = parts["spa"][1]
    hops = 3 * (side - 1) + depth
    banks = 2 + 2 * (ch // ROW)
    scratch = dict(
        red=low(*weights.red.shape),
        spa=low(*weights.spa.shape),
        exp=low(*weights.exp.shape),
        squ=low(*weights.squ.shape),
        mot=low(*weights.mot.shape),
        con=low(*weights.con.shape),
        gat=low(*weights.gat.shape),
        bias=wide(2, *bias.shape),
        norm=wide(2, *norm.shape),
        stage=low(2, *frames.shape[1:]),
        v=low(full, ch),
        nh1=wide(2, full, mid),
        nh2=wide(2, full, mid),
        nh3=wide(2, full * ch // ROW, ROW),
        gs=wide(full * ch // ROW, ROW),
        sigma=low(2, full, mid),
        a1g=low(2, 4 if pp.grouped else 1, full, mid),
        h2=low(2, full, mid),
        gated=low(2, full, mid),
        field=low(2, full, red_w),
        score=low(2, full, red_w),
        cmean=wide(2, segs, red_w),
        ssum=wide(segs, red_w),
        gbias=wide(1, mid),
        gz3=low(full, ch),
        gz1=low(full, mid),
        gl=low(full, mid),
        gq=low(full, red_w),
        gr=low(full, red_w),
        patch=low(full, 9 * mid),
        patch_m=low(full, 9 * red_w),
        grid=wide(GRID * GRID * segs, mid),
        tmp1=wide(9 * red_w, LANES),
        mix=wide(spa_width // LANES, spa_size, LANES),
        mix_e=wide(HALF // LANES, parts["exp"][1], LANES),
        msg=wide(banks, len(levels), 2 * GROUP, LANES),
        inbox=wide(banks, len(levels), group, 2 * GROUP, LANES),
        cnt=wide(len(levels), group, 8, LANES),
        relay=wide(banks, 2 * GROUP, LANES),
        total=wide(8, LANES),
        mean=wide(ch // LANES, LANES),
        bsum=wide(ch // ROW, 2 * GROUP, LANES),
        rstd=wide(2, norm_rows // 2, LANES),
        gnorm=wide(2, norm_rows, LANES),
        gnorm_in=wide(norm_rows, LANES),
        fin_red=low(parts["red"][1], HALF),
        fin_spa=low(spa_size, spa_width),
        fin_exp=low(parts["exp"][1], HALF),
        fin_small=low(parts["small"][1], HALF),
        load_sem=sems(2),
        w_sem=sems(len(WEIGHTS)),
        vs_sem=sems(len(WEIGHTS)),
        ws_sem=sems(len(WEIGHTS)),
        wr_sem=sems(len(WEIGHTS)),
        p_sem=sems(2),
        ps_sem=sems(2),
        pr_sem=sems(2),
        ms_sem=sems(banks, len(levels), group),
        mr_sem=sems(banks, len(levels), group),
        cs_sem=sems(len(levels), group),
        hs_sem=sems(banks),
        hr_sem=sems(banks),
        fs_sem=sems(banks, group),
        cr_sem=sems(len(levels), group),
        o_sem=sems(4, 3),
        rs_send=sems(2, len(chunks), hops),
        rs_recv=sems(2, len(chunks), hops),
        fin_sem=sems(4, 6, pp.reach),
        land_sem=sems(4, 16, ROW // LANES),
        gn_sem=sems(2),
        b_sem=sems(4),
        between=pltpu.SemaphoreType.REGULAR((1,)),
        credit=pltpu.SemaphoreType.REGULAR((len(chunks) + 1,)),
    )
    if pp.grouped:
        scratch |= dict(
            gzg=low(2, 3, full, LANES),
            gz2q=low(mid // LANES, full, LANES),
            sum_g=wide(HALF, 9 * LANES),
            out_g=low(HALF, 9 * LANES),
            in_g=low(HALF, 9 * LANES),
            pile_g=low(depth, spa_size, LANES),
            r3_g=low(2, max(depth - 1, 1), spa_size, LANES),
            as_sem=sems(2, 4, 2),
            ar_sem=sems(2, 4, 2),
            gs_sem=sems(2, 4),
            gr_sem=sems(2, 4),
            g3_sem=sems(2, 2, depth),
        )
    names = list(ins) + list(outs) + list(scratch)
    results = pl.pallas_call(
        functools.partial(kernel, n, sizes, names),
        out_shape=list(outs.values()),
        in_specs=in_specs,
        out_specs=out_specs,
        scratch_shapes=list(scratch.values()) + piles,
        cost_estimate=pl.CostEstimate(
            flops=22 * 10**9, bytes_accessed=10**8, transcendentals=10**7
        ),
        compiler_params=pltpu.CompilerParams(
            collective_id=0, has_side_effects=True, vmem_limit_bytes=64 * 2**20 - 2**17
        ),
    )(*ins.values())
    return results[0], results[1], results[2], results[-1]


def on_device(n, share, frames, out_grad, seg_counts, *params):
    reducer, spatial, expander, squeezer, motion, context, gating, bias, norm = params
    _, segs, pixels, ch = frames.shape
    mid, red_w = reducer.shape[-1], squeezer.shape[-1]
    sizes = (ch, mid, red_w, segs, share)
    weights = SimpleNamespace(
        red=reducer[0],
        spa=spatial[0].transpose(1, 0, 2).reshape(9 * mid, mid),
        exp=expander[0],
        squ=squeezer[0],
        mot=motion[0].transpose(1, 0, 2).reshape(9 * red_w, red_w),
        con=context[0],
        gat=gating[0],
    )
    out, ing, land, gnorm = run(
        n,
        sizes,
        frames.transpose(0, 2, 1, 3),
        out_grad.transpose(0, 2, 1, 3),
        seg_counts,
        weights,
        bias,
        norm[0],
    )
    margin = plan(n, ch, mid, red_w, segs, share).margin
    window = land[margin : land.shape[0] - margin].astype(F32).reshape(-1, LANES)
    start = lax.rem(lax.axis_index("dp") * share, ROW * 16)
    flat = lax.dynamic_slice(window.reshape(1, -1), (0, start), (1, share))
    return (
        out.transpose(0, 2, 1, 3)[None],
        ing.transpose(0, 2, 1, 3)[None],
        flat,
        gnorm.reshape(norm.shape),
    )


def solution(mesh):
    n = mesh.shape["dp"]

    def whole(*args):
        entries = sum(item.size // item.shape[0] for item in args[3:11])
        share = up(entries, n) // n
        body = jax.shard_map(
            functools.partial(on_device, n, share),
            mesh=mesh,
            in_specs=(
                P("dp", None, None, None),
                P("dp", None, None, None),
                P("dp"),
                P("pipe", None, None),
                P("pipe", None, None, None),
                P("pipe", None, None),
                P("pipe", None, None),
                P("pipe", None, None, None),
                P("pipe", None, None),
                P("pipe", None, None),
                P("pipe", None),
                P("pipe", None, None),
            ),
            out_specs=(
                P("pipe", "dp", None, None, None),
                P("pipe", "dp", None, None, None),
                P("pipe", "dp"),
                P("pipe", None, None),
            ),
            check_vma=False,
        )
        return body(*args)

    return whole
```

```python
import functools
from types import SimpleNamespace

import jax
import jax.numpy as jnp
from jax import lax
from jax.experimental import pallas as pl
from jax.experimental.pallas import tpu as pltpu
from jax.sharding import PartitionSpec as P

SIDE = 7
PIX = 49
MICRO = 2
PIECES = 16
EPSILON = 1e-05
HIGH = lax.Precision.HIGHEST
BF = jnp.bfloat16
F32 = jnp.float32
MESH = pl.DeviceIdType.MESH
LANES = 128
GROUP = 4
HALF = 256
ROW = 512
GRID = SIDE + 2
WEIGHTS = ("red", "spa", "exp", "squ", "mot", "con", "gat")
SMALL = ("squ", "mot", "con", "gat")
COMPS = ("red", "spa", "exp", "small")
CHUNKS = ("e", "c", "d")
TAPS = dict(m=(0, 5), t=(5, 9))
ROWS = dict(c=(0, 1), d=(1, 2))
CUTS = 2
OPENS = dict(e=("exp", "small"), c=("red",), m=("spa",))
CLOSES = dict(e=("exp", "small"), d=("red",), t=("spa",))
RELAYED = ()
ORDER = (
    "s01", "x01", "s11", "x11", "s21", "x21", "s31", "x31", "m01", "w01", "w11", "w21", "w31",
    "a1", "b1", "q1", "l21", "y21", "m11", "Gs1", "Ge1", "z21", "p1", "v1", "l11", "y11",
    "g1", "0e1", "1e1", "z11", "o1", "i1", "Gc1", "r1", "Gb1", "s00", "x00", "s10", "0c1",
    "x10", "s20", "x20", "s30", "x30", "3b1", "2e1", "w00", "w10", "w20", "w30", "0d1", "a0",
    "1c1", "b0", "q0", "l20", "y20", "3e1", "1d1", "Ge0", "4b1", "Gs0", "2c1", "z20", "p0",
    "g0", "v0", "4e1", "l10", "0e0", "y10", "3c1", "2d1", "1e0", "Gb0", "3d1", "3b0", "z10",
    "o0", "Gc0", "4c1", "4d1", "0c0", "0d0", "2e0", "1d0", "3e0", "1c0", "2d0", "2c0", "3d0",
    "3c0", "i0", "4e0", "4c0", "4d0", "4b0",
)


def sigmoid(values):
    return 0.5 * jnp.tanh(0.5 * values) + 0.5


def silu_slope(values):
    sigma = sigmoid(values)
    return sigma * (1.0 + values * (1.0 - sigma))


def dot(a, b):
    return jnp.dot(a, b, preferred_element_type=F32)


def dot_nt(a, b):
    return lax.dot_general(a, b, (((1,), (1,)), ((), ())), preferred_element_type=F32)


def dot_tn(a, b):
    return lax.dot_general(a, b, (((0,), (0,)), ((), ())), preferred_element_type=F32)


def up(value, step):
    return -(-value // step) * step


def plan(n, ch, mid, red, segs, share):
    side = 4 if n % 64 == 0 else 2 if n % 4 == 0 else 1
    depth = n // (side * side)
    slots = PIECES // (side * side)
    levels = [(n, 1)] if n <= 16 else [(side * side, 1), (depth, side * side)]
    rows = dict(red=ch * mid // ROW, spa=9 * mid * mid // ROW, exp=mid * ch // ROW)
    small = mid * red + 9 * red * red + red * red + red * mid + mid
    small_rows = up(small, ROW) // ROW
    grouped = side == 2
    spa_size = rows["spa"] // (2 * depth if grouped else PIECES)
    parts = dict(
        red=(0, rows["red"] // PIECES),
        spa=(rows["red"], spa_size),
        exp=(rows["red"] + rows["spa"], rows["exp"] // PIECES),
        small=(rows["red"] + rows["spa"] + rows["exp"], up(up(small_rows, PIECES) // PIECES, 16)),
    )
    total = (parts["small"][0] + small_rows) * ROW
    margin = max(size for _, size in parts.values())
    reach = 1
    for comp, (start, size) in parts.items():
        for piece in range(rows[comp] // size if comp in rows else PIECES):
            first = (start + size * piece) * ROW
            if first < total:
                last = min((start + size * (piece + 1)) * ROW, total) - 1
                reach = max(reach, last // share - first // share + 1)
    land = margin + up(share // ROW + 22, 16) + margin
    return SimpleNamespace(
        side=side,
        depth=depth,
        slots=slots,
        levels=levels,
        parts=parts,
        total=total,
        margin=margin,
        reach=reach,
        grouped=grouped,
        land=land,
        small_rows=small_rows,
    )


def chunk_names(n):
    grouped = n % 64 and n % 4 == 0
    return CHUNKS if grouped else CHUNKS + tuple(TAPS)


def kernel(n, sizes, names, *refs):
    r = SimpleNamespace(**dict(zip(names, refs)))
    rest = refs[len(names) :]
    chunks = chunk_names(n)
    piles = {chunk: rest[6 * k : 6 * k + 6] for k, chunk in enumerate(chunks)}
    own_w = dict(
        red=r.in_red, spa=r.in_spa, exp=r.in_exp, squ=r.in_squ, mot=r.in_mot, con=r.in_con, gat=r.in_gat
    )
    sib_w = dict(
        red=r.sib_red, spa=r.sib_spa, exp=r.sib_exp, squ=r.sib_squ, mot=r.sib_mot, con=r.sib_con, gat=r.sib_gat
    )
    held_w = dict(red=r.red, spa=r.spa, exp=r.exp, squ=r.squ, mot=r.mot, con=r.con, gat=r.gat)
    chunk_refs = {
        chunk: SimpleNamespace(g=part[0], far=part[1], near=part[2], r1=part[3], r2=part[4], r3=part[5])
        for chunk, part in piles.items()
    }
    fin = dict(red=r.fin_red, spa=r.fin_spa, exp=r.fin_exp, small=r.fin_small)
    ch, mid, red_w, segs, share = sizes
    pp = plan(n, ch, mid, red_w, segs, share)
    side, depth, slots, levels, parts = pp.side, pp.depth, pp.slots, pp.levels, pp.parts
    grouped = pp.grouped
    rows = PIX * segs
    full = up(rows, 16)
    pad = full - rows
    c = lax.axis_index("pipe")
    i = lax.axis_index("dp")
    x = lax.rem(i, side)
    y = lax.rem(lax.div(i, side), side)
    z = lax.div(i, side * side)
    fc = x * (1 - c) + y * c
    gc = y * (1 - c) + x * c
    other = (1 - c, i)

    def remote(src, dst, send, recv, device):
        return pltpu.make_async_remote_copy(
            src_ref=src,
            dst_ref=dst,
            send_sem=send,
            recv_sem=recv,
            device_id=device,
            device_id_type=MESH,
        )

    def everybody(semaphore):
        def greet(k, _):
            peer = lax.rem(i + k, n)
            for core in (c, 1 - c):
                pl.semaphore_signal(
                    semaphore, inc=1, device_id=(core, peer), device_id_type=MESH
                )
            return 0

        pl.semaphore_signal(semaphore, inc=1, device_id=other, device_id_type=MESH)
        lax.fori_loop(1, n, greet, 0)

    barrier = pltpu.get_barrier_semaphore()
    everybody(barrier)

    count_own = r.counts[c]
    segment = lax.broadcasted_iota(jnp.int32, (segs, LANES), 0)

    def valid_for(count):
        return jnp.where(segment < count, 1.0, 0.0).astype(F32)

    valid = valid_for(count_own)
    paired = jnp.where(segment + 1 < count_own, 1.0, 0.0).astype(F32)
    pixels_own = PIX * count_own.astype(F32)

    stage = r.stage
    v = r.v
    free = r.nh3.at[1]

    def tile(j):
        return pl.ds(pl.multiple_of(j * LANES, LANES), LANES)

    def view(j, base=0):
        return (
            pl.ds(pl.multiple_of(base + lax.div(j, 4) * full, 16), rows),
            tile(lax.rem(j, 4)),
        )

    def loop(count, body):
        def step(j, _):
            body(j)
            return 0

        lax.fori_loop(0, count, step, 0)

    def packed(values):
        flat = values.reshape(rows, values.shape[-1])
        return jnp.concatenate([flat, jnp.zeros((pad, flat.shape[-1]), F32)], axis=0).astype(BF)

    def cube(values):
        return values.reshape(PIX, segs, values.shape[-1])

    def fold(values):
        return jnp.sum(jnp.sum(values, axis=0), axis=0, keepdims=True)

    def stage_to(slot, target):
        def body(j):
            target[:, tile(j)] = packed(stage[slot, :, :, tile(j)].astype(F32))

        loop(ch // LANES, body)

    def moments(values, mask=None, pixels=None):
        mask = valid if mask is None else mask
        pixels = pixels_own if pixels is None else pixels
        origin = values[0, 0:1, :]
        gaps = values - origin
        first = jnp.sum(mask * jnp.sum(gaps, axis=0), axis=0, keepdims=True)
        second = jnp.sum(mask * jnp.sum(gaps * gaps, axis=0), axis=0, keepdims=True)
        return first + pixels * origin, second - first * (first / pixels)

    load_frames = pltpu.make_async_copy(r.frames.at[c], stage.at[0], r.load_sem.at[0])
    load_frames.start()
    load_other = pltpu.make_async_copy(r.frames.at[1], stage.at[1], r.load_sem.at[1])
    pl.when(c == 0)(load_other.start)

    def weight_index(name):
        return WEIGHTS.index(name)

    def held_copy(source, name):
        return pltpu.make_async_copy(source, held_w[name], r.w_sem.at[weight_index(name)])

    def wait_weight(name):
        held_copy(own_w[name], name).wait()

    def first_send(name):
        k = weight_index(name)
        return remote(own_w[name], held_w[name], r.vs_sem.at[k], r.w_sem.at[k], other)

    def first_sends(*chosen):
        @pl.when(c == 0)
        def _():
            for name in chosen:
                first_send(name).start()

    def kept_send(name):
        k = weight_index(name)
        return remote(own_w[name], sib_w[name], r.ws_sem.at[k], r.wr_sem.at[k], other)

    def kept_sends(core):
        @pl.when(c == core)
        def _():
            for name in WEIGHTS:
                kept_send(name).start()

    def load_weight(name, s):
        @pl.when(c == s)
        def _():
            held_copy(own_w[name], name).start()

        @pl.when(c != s)
        def _():
            kept_send(name).wait_recv()
            held_copy(sib_w[name], name).start()

    @pl.when(c == 0)
    def _():
        for name in WEIGHTS:
            held_copy(own_w[name], name).start()

    own_params = [
        pltpu.make_async_copy(r.in_norm, r.norm.at[c], r.p_sem.at[0]),
        pltpu.make_async_copy(r.in_bias, r.bias.at[c], r.p_sem.at[1]),
    ]
    for copy in own_params:
        copy.start()

    r.grid[...] = jnp.zeros(r.grid.shape, F32)
    load_frames.wait()
    stage_to(0, v)
    msg, inbox = r.msg, r.inbox

    @pl.when(c == 0)
    def _():
        load_other.wait()
        stage_to(1, r.gz3)
        wait_weight("red")
        r.nh1[0] = dot(v[...], r.red[...])
        r.gs[0:full, :] = dot(r.gz3[...], r.red[...])
        count_other = r.counts[1]
        mask_other = valid_for(count_other)
        pixels_other = PIX * count_other.astype(F32)

        def body(j):
            for ref, target, with_other in (
                (r.nh1.at[0], msg.at[0, 0], ()),
                (r.gs, r.relay.at[0], (mask_other, pixels_other)),
            ):
                total, spread = moments(cube(ref[view(j)]), *with_other)
                target[pl.ds(j, 1), :] = total
                target[pl.ds(GROUP + j, 1), :] = spread

        loop(GROUP, body)

    pl.semaphore_wait(barrier, 2 * n - 1)

    param_sends = [
        remote(r.in_norm, r.norm.at[c], r.ps_sem.at[0], r.pr_sem.at[0], other),
        remote(r.in_bias, r.bias.at[c], r.ps_sem.at[1], r.pr_sem.at[1], other),
    ]
    for copy in param_sends:
        copy.start()

    def peer_of(level, k):
        size, stride = levels[level]
        here = lax.rem(lax.div(i, stride), size)
        return (c, i + (lax.rem(here + k, size) - here) * stride)

    def copies_of(bank, level):
        size, _ = levels[level]
        return [
            remote(
                msg.at[bank, level],
                inbox.at[bank, level, k],
                r.ms_sem.at[bank, level, k],
                r.mr_sem.at[bank, level, k],
                peer_of(level, k),
            )
            for k in range(1, size)
        ]

    def exchange_start(bank):
        for copy in copies_of(bank, 0):
            copy.start()

    def routed(core):
        size = levels[0][0]
        return [k for k in range(1, size) if (k % side == 0) == (core == 0)]

    def hand_over(bank):
        return remote(
            msg.at[bank, 0], r.relay.at[bank], r.hs_sem.at[bank], r.hr_sem.at[bank], other
        )

    def passed_on(bank, k):
        core, peer = peer_of(0, k)
        return remote(
            r.relay.at[bank],
            inbox.at[bank, 0, k],
            r.fs_sem.at[bank, k],
            r.mr_sem.at[bank, 0, k],
            (1 - core, peer),
        )

    def relay_start(bank):
        hand_over(bank).start()
        copies = copies_of(bank, 0)
        for core in range(2):

            @pl.when(c == core)
            def _():
                for k in routed(core):
                    copies[k - 1].start()

    def relay_pass(bank):
        hand_over(bank).wait_recv()
        for core in range(2):

            @pl.when(c == core)
            def _():
                for k in routed(core):
                    passed_on(bank, k).start()

    def exchange_finish(bank, combine, relayed=False, first=False):
        for level in range(len(levels)):
            copies = copies_of(bank, level)
            if level:
                for copy in copies:
                    copy.start()
            for copy in copies:
                copy.wait_recv()
            result = combine(bank, level)
            if level == 0 and relayed:
                hand_over(bank).wait_send()
                for core in range(2):

                    @pl.when(c == core)
                    def _():
                        for k in routed(core):
                            copies[k - 1].wait_send()
                            passed_on(bank, k).wait_send()
            elif level == 0 and first:

                @pl.when(c == 0)
                def _():
                    for k, copy in enumerate(copies):
                        copy.wait_send()
                        passed_on(bank, k + 1).wait_send()
                    for copy in first_moves:
                        copy.wait_send()
            else:
                for copy in copies:
                    copy.wait_send()
            if level + 1 < len(levels):
                msg[bank, level + 1] = result
        return result

    first_moves = [
        remote(r.relay.at[0], msg.at[0, 0], r.b_sem.at[0], r.b_sem.at[1], other),
        remote(r.gs.at[pl.ds(0, full)], r.nh1.at[0], r.b_sem.at[2], r.b_sem.at[3], other),
    ]

    @pl.when(c == 0)
    def _():
        exchange_start(0)
        for k in range(1, levels[0][0]):
            passed_on(0, k).start()
        for copy in first_moves:
            copy.start()

    cnt = r.cnt

    def count_copies(level):
        size, _ = levels[level]
        return [
            remote(
                cnt.at[level, 0],
                cnt.at[level, k],
                r.cs_sem.at[level, k],
                r.cr_sem.at[level, k],
                peer_of(level, k),
            )
            for k in range(1, size)
        ]

    cnt[0, 0] = jnp.full((8, LANES), pixels_own, F32)
    for copy in count_copies(0):
        copy.start()
    first_sends("spa", *SMALL)
    kept_sends(1)

    def count_finish():
        for level in range(len(levels)):
            copies = count_copies(level)
            if level:
                for copy in copies:
                    copy.start()
            total = cnt[level, 0]
            for k, copy in enumerate(copies):
                copy.wait()
                total = total + cnt[level, k + 1]
            if level + 1 < len(levels):
                cnt[level + 1, 0] = total
        r.total[...] = total

    def sum_combine(bank, level):
        total = msg[bank, level]
        for k in range(1, levels[level][0]):
            total = total + inbox[bank, level, k]
        return total

    def moment_combine(bank, level):
        size, _ = levels[level]
        nt = GROUP
        items = [msg[bank, level]] + [inbox[bank, level, k] for k in range(1, size)]
        counts = [cnt[level, k, 0:1, :] for k in range(size)]
        total = items[0][0:nt]
        count = counts[0]
        for k in range(1, size):
            total = total + items[k][0:nt]
            count = count + counts[k]
        mean = total / count
        spread = jnp.zeros_like(total)
        for k in range(size):
            gap = items[k][0:nt] / counts[k] - mean
            spread = spread + items[k][nt : 2 * nt] + counts[k] * gap * gap
        return jnp.concatenate([total, spread], axis=0)

    def norm_send(ref, block, bank):
        def body(j):
            total, spread = moments(cube(ref[view(block * GROUP + j)]))
            msg[bank, 0, pl.ds(j, 1), :] = total
            msg[bank, 0, pl.ds(GROUP + j, 1), :] = spread

        loop(GROUP, body)
        exchange_start(bank)

    def norm_receive(bank, s, block, row0, first=False):
        result = exchange_finish(bank, moment_combine, first=first)
        everyone = r.total[0:1, :]
        at = block * GROUP
        r.mean[at : at + GROUP, :] = result[0:GROUP] / everyone
        r.rstd[s, row0 + at : row0 + at + GROUP, :] = lax.rsqrt(
            result[GROUP : 2 * GROUP] / everyone + EPSILON
        )

    def gain_of(s, offset, j):
        lanes = pl.ds(pl.multiple_of(offset + j * LANES, LANES), LANES)
        return (r.norm[s, 0:1, lanes], r.norm[s, 1:2, lanes])

    def row_of(ref, j):
        return ref[pl.ds(j, 1), :]

    grid = r.grid

    def to_grid(values, lanes):
        for h in range(SIDE):
            at = ((h + 1) * GRID + 1) * segs
            grid[at : at + SIDE * segs, lanes] = values[h * SIDE * segs : (h + 1) * SIDE * segs]

    def patches(target, width, flip):
        def body(j):
            lanes = tile(j)
            for tap in range(9):
                down, right = tap // 3, tap % 3
                if flip:
                    down, right = 2 - down, 2 - right
                pieces = []
                for h in range(SIDE):
                    at = ((h + down) * GRID + right) * segs
                    pieces.append(grid[at : at + SIDE * segs, lanes])
                target[:, pl.ds(pl.multiple_of(tap * width + j * LANES, LANES), LANES)] = packed(
                    jnp.concatenate(pieces, axis=0)
                )

        loop(width // LANES, body)

    def put(slot, target, kind, s):
        @pl.when(c == s)
        def _():
            pltpu.make_async_copy(stage.at[slot], target.at[c], r.o_sem.at[kind, 0]).start()

        @pl.when(c != s)
        def _():
            remote(
                stage.at[slot],
                target.at[c],
                r.o_sem.at[kind, 1],
                r.o_sem.at[kind, 2],
                other,
            ).start()

    def put_wait(slot, target, kind, s):
        @pl.when(c == s)
        def _():
            pltpu.make_async_copy(stage.at[slot], target.at[c], r.o_sem.at[kind, 0]).wait()

        @pl.when(c != s)
        def _():
            remote(
                stage.at[slot],
                target.at[c],
                r.o_sem.at[kind, 1],
                r.o_sem.at[kind, 2],
                other,
            ).wait_send()

    n_mid = mid // LANES
    n_ch = ch // LANES
    n_blocks = ch // ROW

    def across(k):
        to_y = y + k // 2 - 2 * y * (k // 2)
        to_x = x + k % 2 - 2 * x * (k % 2)
        return to_y * 2 + to_x, (c, z * 4 + to_y * 2 + to_x)

    def act_move(s, k, half):
        lanes = pl.ds(half * HALF, HALF)
        sems = (r.as_sem.at[s, k, half], r.ar_sem.at[s, k, half])
        return remote(r.a1g.at[s, 0, :, lanes], r.a1g.at[s, k, :, lanes], *sems, across(k)[1])

    def grad_move(s, k):
        to_q, device = across(k)
        sems = (r.gs_sem.at[s, k], r.gr_sem.at[s, k])
        return remote(r.gz2q.at[to_q], r.gzg.at[s, k - 1], *sems, device)

    def act_moves(*chosen):
        if grouped:
            for move in chosen:
                act_move(*move).start()

    for copy in own_params:
        copy.wait()
    load_grad = pltpu.make_async_copy(r.out_grad.at[c], stage.at[1], r.load_sem.at[1])
    for s in range(2):
        nh1, nh2, nh3 = r.nh1.at[s], r.nh2.at[s], r.nh3.at[s]
        if s == 0:
            load_weight("red", 1)
            for copy in param_sends:
                copy.wait_recv()

            @pl.when(c == 1)
            def _():
                for copy in first_moves:
                    copy.wait_recv()

            count_finish()
        else:
            wait_weight("red")
            nh1[...] = dot(v[...], r.red[...])
            kept_sends(0)
            norm_send(nh1, 0, 0)
            act_moves((0, 3, 0))
            put_wait(1, r.out, 0, 0)
            load_grad.start()
        norm_receive(0, s, 0, 0, s == 0)

        def act_one(j, s=s, nh1=nh1):
            gain, offset = gain_of(s, 0, j)
            normed = (nh1[view(j)] - row_of(r.mean, j)) * row_of(r.rstd.at[s], j)
            nh1[view(j)] = normed
            before = normed * gain + offset
            act = before * sigmoid(before)
            r.a1g[s, 0, :, tile(j)] = packed(act)
            to_grid(act, tile(j))

        loop(n_mid, act_one)
        patches(r.patch, mid, False)
        wait_weight("spa")
        nh2[...] = dot(r.patch[...], r.spa[...])
        if s == 0:
            first_sends("exp")
            load_weight("spa", 1)
        norm_send(nh2, 0, 1)
        if s == 0:
            act_moves((0, 1, 0), (0, 2, 0))
        else:
            act_moves((0, 3, 1), (1, 1, 0), (1, 2, 0))
        norm_receive(1, s, 0, n_mid)

        def act_two(j, s=s, nh2=nh2):
            gain, offset = gain_of(s, mid, j)
            normed = (nh2[view(j)] - row_of(r.mean, j)) * row_of(r.rstd.at[s], n_mid + j)
            nh2[view(j)] = normed
            before = normed * gain + offset
            r.h2[s, :, tile(j)] = packed(before * sigmoid(before))

        loop(n_mid, act_two)
        for name in SMALL:
            wait_weight(name)
        squeezed = cube(dot(r.h2[s], r.squ[...])[:rows])
        later = pltpu.roll(squeezed, segs - 1, 1)
        field = (paired * (later - squeezed)).reshape(rows, red_w)
        r.field[s] = packed(field)
        rounded = r.field[s].astype(F32)[:rows]
        to_grid(rounded, pl.ds(0, LANES))
        patches(r.patch_m, red_w, False)
        context_mean = jnp.sum(cube(rounded), axis=0) * (1.0 / PIX)
        r.cmean[s] = context_mean
        from_mean = jnp.dot(
            context_mean, r.con[...].astype(F32), precision=HIGH, preferred_element_type=F32
        )
        mixed = cube(dot(r.patch_m[...], r.mot[...])[:rows]) + from_mean
        r.score[s] = packed(mixed)
        free[0:full, :] = dot(r.score[s], r.gat[...])

        def gate(j, s=s):
            bias = r.bias[s, 0:1, tile(j)]
            sigma = sigmoid(free[view(j)] + bias)
            r.sigma[s, :, tile(j)] = packed(sigma)
            h2 = r.h2[s, :, tile(j)].astype(F32)[:rows]
            r.gated[s, :, tile(j)] = packed(h2 * (0.5 + sigma))

        loop(n_mid, gate)
        if s == 0:
            for name in SMALL:
                load_weight(name, 1)
        wait_weight("exp")
        for block in range(n_blocks):
            nh3[block * full : (block + 1) * full, :] = dot(
                r.gated[s], r.exp[:, block * ROW : (block + 1) * ROW]
            )
            norm_send(nh3, block, 2 + block)
        act_moves((s, 1, 1), (s, 2, 1))
        if s == 0:
            load_weight("exp", 1)
        slot = 1 - s

        def finish(j, s=s, nh3=nh3, slot=slot):
            gain, offset = gain_of(s, 2 * mid, j)
            normed = (nh3[view(j)] - row_of(r.mean, j)) * row_of(
                r.rstd.at[s], 2 * n_mid + j
            )
            nh3[view(j)] = normed
            before = v[:, tile(j)].astype(F32)[:rows] + normed * gain + offset
            out = cube(before * sigmoid(before)) * valid
            stage[slot, :, :, tile(j)] = out.astype(BF)
            if s == 0:
                v[:, tile(j)] = packed(out)

        for block in range(n_blocks):
            norm_receive(2 + block, s, block, 2 * n_mid)
            loop(GROUP, lambda j, block=block: finish(block * GROUP + j))
        put(slot, r.out, s, s)

    def send_sem(chunk, s, k):
        return r.rs_send.at[s, chunks.index(chunk), k]

    def recv_sem(chunk, s, k):
        return r.rs_recv.at[s, chunks.index(chunk), k]

    def add_loop(target, others, pieces):
        def body(j):
            at = target.at[j]
            total = at[...]
            for item in others:
                total = total + item.at[j][...]
            at[...] = total

        loop(pieces, body)

    def along(to):
        px = to * (1 - c) + x * c
        py = y * (1 - c) + to * c
        return z * side * side + py * side + px

    def rs0(chunk, s):
        ref = chunk_refs[chunk]
        found = []
        for k in range(1, side):
            sems = (send_sem(chunk, s, k), recv_sem(chunk, s, k))
            source = ref.g.at[1 - c, lax.rem(gc + k, side)]
            found.append(remote(source, ref.far.at[s * grouped, k - 1], *sems, other))
        sems = (send_sem(chunk, s, 0), recv_sem(chunk, s, 0))
        return found, remote(ref.g.at[c, fc], ref.near.at[s * grouped], *sems, other)

    def rs1(chunk, s):
        ref = chunk_refs[chunk]
        found = []
        for k in range(1, side):
            at = side - 1 + k
            sems = (send_sem(chunk, s, at), recv_sem(chunk, s, at))
            device = (1 - c, along(lax.rem(fc + k, side)))
            found.append(remote(ref.far.at[s * grouped, k - 1], ref.r1.at[s * grouped, k - 1], *sems, device))
        return found

    def rs2(chunk, s):
        ref = chunk_refs[chunk]
        found = []
        for k in range(1, side):
            to = lax.rem(fc + k, side)
            at = 2 * (side - 1) + k
            sems = (send_sem(chunk, s, at), recv_sem(chunk, s, at))
            found.append(remote(ref.near.at[s * grouped, to], ref.r2.at[s * grouped, k - 1], *sems, (c, along(to))))
        return found

    def rs3(chunk, s):
        ref = chunk_refs[chunk]
        found = []
        for k in range(1, depth):
            to = lax.rem(z + k, depth)
            at = 3 * (side - 1) + k
            sems = (send_sem(chunk, s, at), recv_sem(chunk, s, at))
            source = ref.near.at[s * grouped, fc, lax.rem(to, slots)]
            device = (c, to * side * side + y * side + x)
            found.append((to, remote(source, ref.r3.at[s * grouped, k - 1], *sems, device)))
        return found

    def credit(chunk):
        return r.credit.at[chunks.index(chunk)]

    def rs0_start(chunk, s):
        if s == 0 and not grouped:
            pl.semaphore_wait(credit(chunk), 1)
        far, near = rs0(chunk, s)
        for copy in far:
            copy.start()
        near.start()

    def rs1_start(chunk, s):
        ref = chunk_refs[chunk]
        far, near = rs0(chunk, s)
        for k, copy in enumerate(far):
            copy.wait()
            to = lax.rem(fc + k + 1, side)
            for b in range(side):
                add_loop(ref.far.at[s * grouped, k, b], [ref.g.at[c, to, b]], slots)
        for copy in rs1(chunk, s):
            copy.start()
        near.wait()
        for b in range(side):
            add_loop(ref.near.at[s * grouped, b], [ref.g.at[1 - c, gc, b]], slots)

    def rs2_start(chunk, s):
        ref = chunk_refs[chunk]
        copies = rs1(chunk, s)
        for copy in copies:
            copy.wait_recv()
        for b in range(side):
            add_loop(ref.near.at[s * grouped, b], [ref.r1.at[s * grouped, k, b] for k in range(side - 1)], slots)
        for copy in copies:
            copy.wait_send()
        for copy in rs2(chunk, s):
            copy.start()

    def rs3_start(chunk, s):
        ref = chunk_refs[chunk]
        copies = rs2(chunk, s)
        for copy in copies:
            copy.wait_recv()
        add_loop(ref.near.at[s * grouped, fc], [ref.r2.at[s * grouped, k] for k in range(side - 1)], slots)
        for copy in copies:
            copy.wait_send()
        for to, copy in rs3(chunk, s):
            if slots == depth:
                copy.start()
            else:
                pl.when(to < slots)(copy.start)

    def block_rows(comp):
        size = parts[comp][1]
        return size if size % 96 and size < 128 else 96 if size % 96 == 0 else size // 2

    def owner_range(at, size):
        return lax.div(at * ROW, share), lax.div(jnp.minimum((at + size) * ROW, pp.total) - 1, share)

    def send_piece(comp, s, action):
        start, size = parts[comp]
        by_chip = grouped and comp == "spa"
        piece = c * depth + z if by_chip else i
        width = fin[comp].shape[1]
        part = lax.rem(i, side * side) if by_chip else 1 - c
        lanes = pl.ds(pl.multiple_of(part * width, width), width)
        which = COMPS.index(comp)
        step = block_rows(comp)
        count = size // step
        for b in range(count):
            at = start + size * piece + step * b
            first, last = owner_range(at, step)
            exists = jnp.logical_and(i < PIECES, at * ROW < pp.total)
            slot = lax.rem(piece * count + b, 16)
            source = fin[comp].at[pl.ds(b * step, step)]
            for k in range(pp.reach):
                to = first + k
                base = lax.div(to * share, ROW * 16) * 16
                row = pl.multiple_of(pp.margin + at - base, 16)
                there = r.land.at[pl.ds(row, step), lanes]
                needed = jnp.logical_and(exists, to <= last)
                here = jnp.logical_and(c == s, to == i)
                arrival = r.land_sem.at[which, slot, part]

                @pl.when(jnp.logical_and(needed, here))
                def _():
                    copy = pltpu.make_async_copy(source, there, arrival)
                    if action == "start":
                        copy.start()
                    else:
                        copy.wait()

                @pl.when(jnp.logical_and(needed, jnp.logical_not(here)))
                def _():
                    copy = remote(source, there, r.fin_sem.at[which, b, k], arrival, (s, to))
                    if action == "start":
                        copy.start()
                    else:
                        copy.wait_send()

    def arrivals(comp):
        start, size = parts[comp]
        by_chip = grouped and comp == "spa"
        width = fin[comp].shape[1]
        step = block_rows(comp)
        count = size // step
        which = COMPS.index(comp)
        low = i * share
        high = jnp.minimum(low + share, pp.total)
        before = jnp.maximum(lax.div(low, ROW) - start, 0)
        first = lax.div(before, step)
        blocks = (2 * depth if by_chip else PIECES) * count

        def arrive(k, _):
            block = first + k
            at = start + step * block
            piece = lax.div(block, count)
            near = jnp.logical_and(at * ROW < high, (at + step) * ROW > low)
            near = jnp.logical_and(near, block < blocks)
            for part in range(ROW // width):
                core = lax.div(piece, depth) if by_chip else 1 - part
                chip = lax.rem(piece, depth) * side * side + part if by_chip else piece
                own = jnp.logical_and(c == core, i == chip)

                @pl.when(jnp.logical_and(near, jnp.logical_not(own)))
                def _():
                    pltpu.make_async_copy(
                        fin[comp].at[pl.ds(0, step)],
                        r.land.at[pl.ds(0, step), pl.ds(0, width)],
                        r.land_sem.at[which, lax.rem(block, 16), part],
                    ).wait()

            return 0

        lax.fori_loop(0, min(share // (ROW * step) + 3, 16), arrive, 0)

    def finish_chunk(chunk, s):
        ref = chunk_refs[chunk]
        own = ref.near.at[s * grouped, fc]
        r3 = ref.r3
        copies = rs3(chunk, s)
        cins = mid // PIECES
        if s == 0 and chunk in OPENS:
            for comp in OPENS[chunk]:
                send_piece(comp, 1, "wait")

        def work():
            for _, copy in copies:
                copy.wait_recv()
            mine = own.at[lax.rem(z, slots)]

            def summed(first, count):
                total = mine[first : first + count, :].astype(F32)
                for k in range(depth - 1):
                    total = total + r3[s * grouped, k, first : first + count, :].astype(F32)
                return total

            def weave(mix, first, count, stride, value):
                for k in range(HALF // LANES):
                    mix[k, pl.ds(first, count, stride=stride), :] = value[
                        :, k * LANES : (k + 1) * LANES
                    ]

            def woven(mix, target, size):
                for k in range(HALF // LANES):
                    target[:, k * LANES : (k + 1) * LANES] = mix[k, 0:size, :].astype(BF)

            if chunk == "e":
                size = parts["exp"][1]
                quarters = size // cins
                for q in range(quarters):
                    weave(r.mix_e, q, cins, quarters, summed(q * cins, cins))
                woven(r.mix_e, r.fin_exp, size)
                r.fin_small[...] = summed(size, parts["small"][1]).astype(BF)
            elif chunk in TAPS:
                first, end = TAPS[chunk]
                for tap in range(first, end):
                    weave(r.mix, tap, cins, 9, summed((tap - first) * cins, cins))
                if end == 9:
                    woven(r.mix, r.fin_spa, parts["spa"][1])
            else:
                first, end = (k * parts["red"][1] // CUTS for k in ROWS[chunk])
                r.fin_red[first:end, :] = summed(0, end - first).astype(BF)

        if slots == depth:
            work()
        else:
            pl.when(z < slots)(work)
        for to, copy in copies:
            if slots == depth:
                copy.wait_send()
            else:
                pl.when(to < slots)(copy.wait_send)
        if s == 1 and not grouped:
            pl.semaphore_signal(credit(chunk), inc=1, device_id=other, device_id_type=MESH)
        for comp in CLOSES.get(chunk, ()):
            send_piece(comp, s, "start")

    def place(half, piece):
        px, py, pz = piece % side, (piece // side) % side, piece // (side * side)
        return (half, px, py, pz) if half == 0 else (half, py, px, pz)

    small_at = 2 * full

    def grads_e(s):
        cins = mid // PIECES
        g = chunk_refs["e"].g
        for q in range(ch // ROW):
            for half in range(2):
                lanes = slice(q * ROW + half * HALF, q * ROW + (half + 1) * HALF)
                value = dot_tn(r.gated[s], r.gz3[:, lanes]).astype(BF)
                for piece in range(PIECES):
                    where = place(half, piece)
                    g[where + (slice(q * cins, (q + 1) * cins),)] = value[
                        piece * cins : (piece + 1) * cins
                    ]

    def grads_small(s):
        g = chunk_refs["e"].g
        tmp = r.tmp1
        at = small_at
        per = ROW // LANES

        def spread(count):
            for q in range(per):
                free[at : at + count, q * LANES : (q + 1) * LANES] = tmp[
                    pl.ds(q, count, stride=per), :
                ]

        tmp[0:mid, :] = dot_tn(r.h2[s], r.gr[...])
        spread(mid // per)
        at += mid // per
        moved = dot_tn(r.field[s], r.patch_m[...])
        for tap in range(9):
            tmp[pl.ds(tap, red_w, stride=9), :] = moved[:, tap * LANES : (tap + 1) * LANES]
        spread(9 * red_w // per)
        at += 9 * red_w // per
        tmp[0:red_w, :] = lax.dot_general(
            r.cmean[s],
            r.ssum[...],
            (((0,), (0,)), ((), ())),
            precision=HIGH,
            preferred_element_type=F32,
        )
        spread(red_w // per)
        at += red_w // per
        free[at : at + red_w, :] = dot_tn(r.score[s], r.gl[...])
        at += red_w
        free[at : at + 8, :] = jnp.broadcast_to(r.gbias[...], (8, mid))
        start = parts["exp"][1]
        size = parts["small"][1]
        used = -(-pp.small_rows // size)
        for piece in range(PIECES):
            for half in range(2):
                where = place(half, piece) + (slice(start, start + size),)
                if piece < used:
                    g[where] = free[
                        small_at + piece * size : small_at + (piece + 1) * size,
                        half * HALF : (half + 1) * HALF,
                    ].astype(BF)
                else:
                    g[where] = jnp.zeros((size, HALF), BF)

    def grads_taps(chunk, s):
        cins = mid // PIECES
        g = chunk_refs[chunk].g
        first, end = TAPS[chunk]

        def body(tap):
            for half in range(2):
                lanes = pl.ds(pl.multiple_of((first + tap) * mid + half * HALF, HALF), HALF)
                value = dot_tn(r.a1g[s, 0], r.patch[:, lanes]).astype(BF)
                for piece in range(PIECES):
                    where = place(half, piece)
                    g[where + (pl.ds(pl.multiple_of(tap * cins, cins), cins),)] = value[
                        piece * cins : (piece + 1) * cins
                    ]

        loop(end - first, body)

    def grads_group(s):
        for k in range(4):
            if k:
                act_move(s, k, 0).wait_recv()
                act_move(s, k, 1).wait_recv()
                grad_move(s, k).wait_recv()
                grad = r.gzg[s, k - 1]
            else:
                grad = r.gz2q[lax.rem(i, 4)]
            to_grid(grad.astype(F32)[:rows], pl.ds(0, LANES))
            patches(r.patch.at[:, pl.ds(k * 9 * LANES, 9 * LANES)], LANES, True)
        def product(half):
            lanes = pl.ds(pl.multiple_of(half * HALF, HALF), HALF)
            total = None
            for k in range(4):
                part = dot_tn(
                    r.a1g[s, k, :, lanes], r.patch[:, k * 9 * LANES : (k + 1) * 9 * LANES]
                )
                total = part if total is None else total + part
            return total

        r.out_g[...] = product(1 - c).astype(BF)
        if s == 0:
            pl.semaphore_wait(r.credit.at[len(chunks)], 1)
        group_swap(s).start()
        r.sum_g[...] = product(c)

    def group_swap(s):
        return remote(r.out_g, r.in_g, r.g3_sem.at[s, 0, 0], r.g3_sem.at[s, 1, 0], other)

    def group_moves(s):
        found = []
        for k in range(1, depth):
            to = lax.rem(z + k, depth)
            device = (c, to * 4 + lax.rem(i, 4))
            found.append(
                remote(
                    r.pile_g.at[to],
                    r.r3_g.at[s, k - 1],
                    r.g3_sem.at[s, 0, k],
                    r.g3_sem.at[s, 1, k],
                    device,
                )
            )
        return found

    def group_start(s):
        cins = HALF // depth
        group_swap(s).wait()
        for to in range(depth):
            at = slice(to * cins, (to + 1) * cins)
            for tap in range(9):
                lanes = slice(tap * LANES, (tap + 1) * LANES)
                theirs = r.in_g[to * cins : (to + 1) * cins, lanes].astype(F32)
                value = r.sum_g[at, lanes] + theirs
                r.pile_g[to, tap * cins : (tap + 1) * cins, :] = value.astype(BF)
        if s == 1:
            pl.semaphore_signal(
                r.credit.at[len(chunks)], inc=1, device_id=other, device_id_type=MESH
            )
        for copy in group_moves(s):
            copy.start()

    def group_finish(s):
        cins = HALF // depth
        copies = group_moves(s)
        for copy in copies:
            copy.wait_recv()
        for tap in range(9):
            at = slice(tap * cins, (tap + 1) * cins)
            total = r.pile_g[z, at, :].astype(F32)
            for k in range(depth - 1):
                total = total + r.r3_g[s, k, at, :].astype(F32)
            r.mix[0, pl.ds(tap, cins, stride=9), :] = total
        if s == 0:
            send_piece("spa", 1, "wait")
        r.fin_spa[...] = r.mix[0].astype(BF)
        for copy in copies:
            copy.wait_send()
        send_piece("spa", s, "start")

    def grads_c(s):
        size = parts["red"][1]
        for half in range(2):
            value = dot_tn(v[...], r.gz1[:, half * HALF : (half + 1) * HALF]).astype(BF)
            for chunk, cut in ROWS.items():
                first, end = (k * size // CUTS for k in cut)
                for piece in range(PIECES):
                    chunk_refs[chunk].g[place(half, piece)] = value[
                        piece * size + first : piece * size + end
                    ]

    def back_receive(bank, s, block, row0, relayed=True):
        result = exchange_finish(bank, sum_combine, relayed)
        half_rows = 2 * n_mid + n_ch
        at = row0 + block * GROUP
        r.gnorm[s, at : at + GROUP, :] = result[GROUP : 2 * GROUP]
        r.gnorm[s, half_rows + at : half_rows + at + GROUP, :] = result[0:GROUP]
        r.bsum[block] = result / r.total[0:1, :]

    def norm_grad(grad, normed, s, offset, row0, j):
        gain, _ = gain_of(s, offset, j)
        scale = gain * row_of(r.rstd.at[s], row0 + j)
        means = r.bsum.at[lax.div(j, GROUP)]
        mean_grad = row_of(means, lax.rem(j, GROUP))
        mean_cross = row_of(means, GROUP + lax.rem(j, GROUP))
        return scale * (cube(grad) - valid * (mean_grad + cube(normed) * mean_cross))

    def slope(s, grad_at, normed_ref, offset, bank):
        def body(j):
            gain, shift = gain_of(s, offset, j)
            normed = normed_ref[view(j)]
            grad = free[view(j, grad_at)] * silu_slope(normed * gain + shift)
            free[view(j, grad_at)] = grad
            msg[bank, 0, pl.ds(j, 1), :] = fold(cube(grad))
            msg[bank, 0, pl.ds(GROUP + j, 1), :] = fold(cube(grad * normed))

        loop(GROUP, body)

    gs = r.gs
    reload = pltpu.make_async_copy(r.frames.at[c], stage.at[1], r.load_sem.at[0])

    def bank_three(s, block):
        return 2 + n_blocks * s + block

    def back_three(s, block):
        if s == 1 and block == 0:
            load_grad.wait()
        nh3 = r.nh3.at[s]
        bank = bank_three(s, block)

        def body(j):
            at = block * GROUP + j
            gain, shift = gain_of(s, 2 * mid, at)
            normed = nh3[view(at)]
            before = v[:, tile(at)].astype(F32)[:rows] + normed * gain + shift
            grad = cube(silu_slope(before)) * valid * stage[s, :, :, tile(at)].astype(F32)
            gs[view(at)] = grad.reshape(rows, LANES)
            msg[bank, 0, pl.ds(j, 1), :] = fold(grad)
            msg[bank, 0, pl.ds(GROUP + j, 1), :] = fold(grad * cube(normed))

        loop(GROUP, body)

    def send_sums(bank, relayed):
        if relayed:
            relay_start(bank)
            relay_pass(bank)
        else:
            exchange_start(bank)

    def grad_three(s, block, relayed):
        nh3 = r.nh3.at[s]
        back_receive(bank_three(s, block), s, block, 2 * n_mid, relayed)

        def body(j):
            at = block * GROUP + j
            r.gz3[:, tile(at)] = packed(
                norm_grad(gs[view(at)], nh3[view(at)], s, 2 * mid, 2 * n_mid, at)
            )

        loop(GROUP, body)

    def back_expander(s):
        if s == 0:
            wait_weight("exp")
        free[0:full, :] = dot_nt(r.gz3[...], r.exp[...])
        if s == 1:
            load_weight("exp", 0)

    def back_gate(s):
        def body(j):
            grad = free[view(j)]
            sigma = r.sigma[s, :, tile(j)].astype(F32)[:rows]
            h2 = r.h2[s, :, tile(j)].astype(F32)[:rows]
            free[view(j, full)] = grad * (0.5 + sigma)
            value = packed(grad * h2 * sigma * (1.0 - sigma))
            r.gl[:, tile(j)] = value
            r.gbias[0:1, tile(j)] = fold(cube(value.astype(F32)[:rows]))

        loop(n_mid, body)

    def back_motion(s):
        if s == 0:
            for name in SMALL:
                wait_weight(name)
        r.gq[...] = dot_nt(r.gl[...], r.gat[...]).astype(BF)
        rounded = r.gq[...].astype(F32)[:rows]
        to_grid(rounded, pl.ds(0, LANES))
        patches(r.patch_m, red_w, True)
        score_sums = jnp.sum(cube(rounded), axis=0)
        r.ssum[...] = score_sums
        grad_field = None
        for tap in range(9):
            part = dot_nt(
                r.patch_m[:, tap * red_w : (tap + 1) * red_w],
                r.mot[tap * red_w : (tap + 1) * red_w, :],
            )
            grad_field = part if grad_field is None else grad_field + part
        from_mean = lax.dot_general(
            score_sums,
            r.con[...].astype(F32),
            (((1,), (1,)), ((), ())),
            precision=HIGH,
            preferred_element_type=F32,
        ) * (1.0 / PIX)
        weighted = paired * (cube(grad_field[:rows]) + from_mean)
        r.gr[...] = packed(pltpu.roll(weighted, 1, 1) - weighted)
        free[full : 2 * full, :] += dot_nt(r.gr[...], r.squ[...])
        if s == 1:
            for name in SMALL:
                load_weight(name, 0)

    def back_spread(s):
        nh2 = r.nh2.at[s]

        def body(j):
            value = norm_grad(free[view(j, full)], nh2[view(j)], s, mid, n_mid, j)
            to_grid(value.reshape(rows, LANES), tile(j))
            if grouped:
                r.gz2q[j] = packed(value)

        if grouped and s == 0:
            for k in range(1, 4):
                grad_move(1, k).wait_send()
        loop(n_mid, body)
        patches(r.patch, mid, True)

    def back_conv(s):
        if s == 0:
            wait_weight("spa")
        acc = None
        for tap in range(9):
            part = dot_nt(
                r.patch[:, tap * mid : (tap + 1) * mid], r.spa[tap * mid : (tap + 1) * mid, :]
            )
            acc = part if acc is None else acc + part
        free[0:full, :] = acc
        if s == 1:
            load_weight("spa", 0)

    def grad_one(s):
        nh1 = r.nh1.at[s]

        def body(j):
            r.gz1[:, tile(j)] = packed(norm_grad(free[view(j)], nh1[view(j)], s, 0, 0, j))

        loop(n_mid, body)

    def back_input(s):
        if s == 1:
            put_wait(0, r.out, 1, 1)
            reload.start()
        else:
            wait_weight("red")
        for block in range(n_blocks):
            value = gs[block * full : block * full + rows, :] + dot_nt(
                r.gz1[...], r.red[block * ROW : (block + 1) * ROW, :]
            )[:rows]
            stage[1 - s, :, :, block * ROW : (block + 1) * ROW] = cube(value).astype(BF)
        put(1 - s, r.ing, 2 + s, s)
        if s == 1:
            load_weight("red", 0)

    def back_reload(s):
        reload.wait()
        stage_to(1, v)

    def perform(token):
        op, s = token[:-1], int(token[-1])
        kind, rest = op[0], op[1:]
        if kind == "s":
            back_three(s, int(rest))
        elif kind == "x":
            send_sums(bank_three(s, int(rest)), kind + token[-1] in RELAYED)
        elif kind == "w":
            grad_three(s, int(rest), "x" + token[-1] in RELAYED)
        elif kind == "y":
            send_sums(int(rest) - 1, token in RELAYED)
        elif op == "z2":
            back_receive(1, s, 0, n_mid, "y" + token[1:] in RELAYED)
        elif op == "z1":
            back_receive(0, s, 0, 0, "y" + token[1:] in RELAYED)
        elif op == "g":
            if grouped:
                for k in range(1, 4):
                    grad_move(s, k).start()
        elif kind == "m":
            act_moves((s, 3, int(rest)))
        elif rest == "b" and grouped:
            if kind == "G":
                grads_group(s)
            elif kind == "3":
                group_start(s)
            else:
                group_finish(s)
        elif rest == "b":
            for chunk in TAPS:
                if kind == "G":
                    grads_taps(chunk, s)
                    rs0_start(chunk, s)
                    rs1_start(chunk, s)
                    rs2_start(chunk, s)
                elif kind == "3":
                    rs3_start(chunk, s)
                else:
                    finish_chunk(chunk, s)
        elif kind == "G":
            if rest == "e":
                grads_e(s)
            elif rest == "s":
                grads_small(s)
            else:
                grads_c(s)
        elif kind == "0":
            rs0_start(rest, s)
        elif kind == "1":
            rs1_start(rest, s)
        elif kind == "2":
            rs2_start(rest, s)
        elif kind == "3":
            rs3_start(rest, s)
        elif kind == "4":
            finish_chunk(rest, s)
        elif op == "l2":
            slope(s, full, r.nh2.at[s], mid, 1)
        elif op == "l1":
            slope(s, 0, r.nh1.at[s], 0, 0)
        else:
            table[op](s)

    table = dict(
        a=back_expander,
        b=back_gate,
        q=back_motion,
        p=back_spread,
        v=back_conv,
        o=grad_one,
        i=back_input,
        r=back_reload,
    )
    if grouped:
        for token in ORDER:
            perform(token)
    else:
        for token in ORDER:
            if token[-1] == "1":
                perform(token)
        everybody(r.between.at[0])
        pl.semaphore_wait(r.between.at[0], 2 * n - 1)
        for token in ORDER:
            if token[-1] == "0":
                perform(token)

    gn_send = remote(
        r.gnorm.at[1 - c], r.gnorm_in, r.gn_sem.at[0], r.gn_sem.at[1], other
    )
    gn_send.start()
    gn_send.wait()
    r.gnorm_out[...] = r.gnorm[c] + r.gnorm_in[...]

    if grouped:
        for k in range(1, 4):
            for s in range(2):
                act_move(s, k, 0).wait_send()
                act_move(s, k, 1).wait_send()
            grad_move(0, k).wait_send()
    for copy in param_sends:
        copy.wait_send()
    for name in WEIGHTS:
        kept_send(name).wait_send()

    @pl.when(c == 0)
    def _():
        for name in WEIGHTS[1:]:
            first_send(name).wait_send()

    put_wait(0, r.ing, 3, 1)
    put_wait(1, r.ing, 2, 0)
    for base, target in ((0, r.out), (2, r.ing)):
        for s in range(2):

            @pl.when(c == s)
            def _():
                remote(
                    stage.at[0],
                    target.at[1 - c],
                    r.o_sem.at[base + s, 1],
                    r.o_sem.at[base + s, 2],
                    other,
                ).wait_recv()

    for comp in COMPS:
        send_piece(comp, 0, "wait")
    for comp in COMPS:
        arrivals(comp)


def run(n, sizes, frames, out_grad, seg_counts, weights, bias, norm):
    ch, mid, red_w, segs, share = sizes
    pp = plan(n, ch, mid, red_w, segs, share)
    side, depth, slots, levels, parts = pp.side, pp.depth, pp.slots, pp.levels, pp.parts
    rows = PIX * segs
    full = up(rows, 16)
    norm_rows = 2 * (2 * mid + ch) // LANES
    group = max(size for size, _ in levels)
    any_spec = pl.BlockSpec(memory_space=pl.ANY)
    vmem_spec = pl.BlockSpec(memory_space=pltpu.VMEM)

    ins = dict(
        frames=frames,
        out_grad=out_grad,
        in_red=weights.red,
        in_spa=weights.spa,
        in_exp=weights.exp,
        in_squ=weights.squ,
        in_mot=weights.mot,
        in_con=weights.con,
        in_gat=weights.gat,
        counts=seg_counts,
        in_bias=bias,
        in_norm=norm,
    )
    in_specs = [any_spec] * 9 + [pl.BlockSpec(memory_space=pltpu.SMEM), any_spec, any_spec]

    def like(item):
        return jax.ShapeDtypeStruct(item.shape, item.dtype)

    outs = dict(
        out=like(frames),
        ing=like(frames),
        land=jax.ShapeDtypeStruct((pp.land, ROW), BF),
        sib_red=like(weights.red),
        sib_spa=like(weights.spa),
        sib_exp=like(weights.exp),
        sib_squ=like(weights.squ),
        sib_mot=like(weights.mot),
        sib_con=like(weights.con),
        sib_gat=like(weights.gat),
        gnorm_out=jax.ShapeDtypeStruct((norm_rows, LANES), F32),
    )
    out_specs = [any_spec] * 10 + [vmem_spec]

    def low(*dims):
        return pltpu.VMEM(dims, BF)

    def wide(*dims):
        return pltpu.VMEM(dims, F32)

    def sems(*dims):
        return pltpu.SemaphoreType.DMA(dims)

    def piled(size):
        return (
            low(2, side, side, slots, size, HALF),
            low(1 + pp.grouped, max(side - 1, 1), side, slots, size, HALF),
            low(1 + pp.grouped, side, slots, size, HALF),
            low(1 + pp.grouped, max(side - 1, 1), side, slots, size, HALF),
            low(1 + pp.grouped, max(side - 1, 1), slots, size, HALF),
            low(1 + pp.grouped, max(depth - 1, 1), size, HALF),
        )

    cins = mid // PIECES
    sizes_of = dict(e=parts["exp"][1] + parts["small"][1])
    for chunk, (first, end) in TAPS.items():
        sizes_of[chunk] = (end - first) * cins
    for chunk, (first, end) in ROWS.items():
        sizes_of[chunk] = (end - first) * parts["red"][1] // CUTS
    chunks = chunk_names(n)
    piles = [item for chunk in chunks for item in piled(sizes_of[chunk])]
    spa_width = LANES if pp.grouped else HALF
    spa_size = parts["spa"][1]
    hops = 3 * (side - 1) + depth
    banks = 2 + 2 * (ch // ROW)
    scratch = dict(
        red=low(*weights.red.shape),
        spa=low(*weights.spa.shape),
        exp=low(*weights.exp.shape),
        squ=low(*weights.squ.shape),
        mot=low(*weights.mot.shape),
        con=low(*weights.con.shape),
        gat=low(*weights.gat.shape),
        bias=wide(2, *bias.shape),
        norm=wide(2, *norm.shape),
        stage=low(2, *frames.shape[1:]),
        v=low(full, ch),
        nh1=wide(2, full, mid),
        nh2=wide(2, full, mid),
        nh3=wide(2, full * ch // ROW, ROW),
        gs=wide(full * ch // ROW, ROW),
        sigma=low(2, full, mid),
        a1g=low(2, 4 if pp.grouped else 1, full, mid),
        h2=low(2, full, mid),
        gated=low(2, full, mid),
        field=low(2, full, red_w),
        score=low(2, full, red_w),
        cmean=wide(2, segs, red_w),
        ssum=wide(segs, red_w),
        gbias=wide(1, mid),
        gz3=low(full, ch),
        gz1=low(full, mid),
        gl=low(full, mid),
        gq=low(full, red_w),
        gr=low(full, red_w),
        patch=low(full, 9 * mid),
        patch_m=low(full, 9 * red_w),
        grid=wide(GRID * GRID * segs, mid),
        tmp1=wide(9 * red_w, LANES),
        mix=wide(spa_width // LANES, spa_size, LANES),
        mix_e=wide(HALF // LANES, parts["exp"][1], LANES),
        msg=wide(banks, len(levels), 2 * GROUP, LANES),
        inbox=wide(banks, len(levels), group, 2 * GROUP, LANES),
        cnt=wide(len(levels), group, 8, LANES),
        relay=wide(banks, 2 * GROUP, LANES),
        total=wide(8, LANES),
        mean=wide(ch // LANES, LANES),
        bsum=wide(ch // ROW, 2 * GROUP, LANES),
        rstd=wide(2, norm_rows // 2, LANES),
        gnorm=wide(2, norm_rows, LANES),
        gnorm_in=wide(norm_rows, LANES),
        fin_red=low(parts["red"][1], HALF),
        fin_spa=low(spa_size, spa_width),
        fin_exp=low(parts["exp"][1], HALF),
        fin_small=low(parts["small"][1], HALF),
        load_sem=sems(2),
        w_sem=sems(len(WEIGHTS)),
        vs_sem=sems(len(WEIGHTS)),
        ws_sem=sems(len(WEIGHTS)),
        wr_sem=sems(len(WEIGHTS)),
        p_sem=sems(2),
        ps_sem=sems(2),
        pr_sem=sems(2),
        ms_sem=sems(banks, len(levels), group),
        mr_sem=sems(banks, len(levels), group),
        cs_sem=sems(len(levels), group),
        hs_sem=sems(banks),
        hr_sem=sems(banks),
        fs_sem=sems(banks, group),
        cr_sem=sems(len(levels), group),
        o_sem=sems(4, 3),
        rs_send=sems(2, len(chunks), hops),
        rs_recv=sems(2, len(chunks), hops),
        fin_sem=sems(4, 6, pp.reach),
        land_sem=sems(4, 16, ROW // LANES),
        gn_sem=sems(2),
        b_sem=sems(4),
        between=pltpu.SemaphoreType.REGULAR((1,)),
        credit=pltpu.SemaphoreType.REGULAR((len(chunks) + 1,)),
    )
    if pp.grouped:
        scratch |= dict(
            gzg=low(2, 3, full, LANES),
            gz2q=low(mid // LANES, full, LANES),
            sum_g=wide(HALF, 9 * LANES),
            out_g=low(HALF, 9 * LANES),
            in_g=low(HALF, 9 * LANES),
            pile_g=low(depth, spa_size, LANES),
            r3_g=low(2, max(depth - 1, 1), spa_size, LANES),
            as_sem=sems(2, 4, 2),
            ar_sem=sems(2, 4, 2),
            gs_sem=sems(2, 4),
            gr_sem=sems(2, 4),
            g3_sem=sems(2, 2, depth),
        )
    names = list(ins) + list(outs) + list(scratch)
    results = pl.pallas_call(
        functools.partial(kernel, n, sizes, names),
        out_shape=list(outs.values()),
        in_specs=in_specs,
        out_specs=out_specs,
        scratch_shapes=list(scratch.values()) + piles,
        cost_estimate=pl.CostEstimate(
            flops=22 * 10**9, bytes_accessed=10**8, transcendentals=10**7
        ),
        compiler_params=pltpu.CompilerParams(
            collective_id=0, has_side_effects=True, vmem_limit_bytes=64 * 2**20 - 2**17
        ),
    )(*ins.values())
    return results[0], results[1], results[2], results[-1]


def on_device(n, share, frames, out_grad, seg_counts, *params):
    reducer, spatial, expander, squeezer, motion, context, gating, bias, norm = params
    _, segs, pixels, ch = frames.shape
    mid, red_w = reducer.shape[-1], squeezer.shape[-1]
    sizes = (ch, mid, red_w, segs, share)
    weights = SimpleNamespace(
        red=reducer[0],
        spa=spatial[0].transpose(1, 0, 2).reshape(9 * mid, mid),
        exp=expander[0],
        squ=squeezer[0],
        mot=motion[0].transpose(1, 0, 2).reshape(9 * red_w, red_w),
        con=context[0],
        gat=gating[0],
    )
    out, ing, land, gnorm = run(
        n,
        sizes,
        frames.transpose(0, 2, 1, 3),
        out_grad.transpose(0, 2, 1, 3),
        seg_counts,
        weights,
        bias,
        norm[0],
    )
    margin = plan(n, ch, mid, red_w, segs, share).margin
    window = land[margin : land.shape[0] - margin].astype(F32).reshape(-1, LANES)
    start = lax.rem(lax.axis_index("dp") * share, ROW * 16)
    flat = lax.dynamic_slice(window.reshape(1, -1), (0, start), (1, share))
    return (
        out.transpose(0, 2, 1, 3)[None],
        ing.transpose(0, 2, 1, 3)[None],
        flat,
        gnorm.reshape(norm.shape),
    )


def solution(mesh):
    n = mesh.shape["dp"]

    def whole(*args):
        entries = sum(item.size // item.shape[0] for item in args[3:11])
        share = up(entries, n) // n
        body = jax.shard_map(
            functools.partial(on_device, n, share),
            mesh=mesh,
            in_specs=(
                P("dp", None, None, None),
                P("dp", None, None, None),
                P("dp"),
                P("pipe", None, None),
                P("pipe", None, None, None),
                P("pipe", None, None),
                P("pipe", None, None),
                P("pipe", None, None, None),
                P("pipe", None, None),
                P("pipe", None, None),
                P("pipe", None),
                P("pipe", None, None),
            ),
            out_specs=(
                P("pipe", "dp", None, None, None),
                P("pipe", "dp", None, None, None),
                P("pipe", "dp"),
                P("pipe", None, None),
            ),
            check_vma=False,
        )
        return body(*args)

    return whole
```
